256 devices in a mesh: dap: 64 (over x, z, core), blk: 4 (over y).
Axes of the slice: x: 4, y: 4, z: 8, core: 2. Of those that a mesh axis runs over, the one named last changes fastest.
Arguments:
- coevolution_profile_tensor: bfloat16 [512, 512, 256], P('blk', 'dap'), may hold values from -60 to 60
- residue_couple_embedding: bfloat16 [512, 512, 128], P('dap'), may hold values from -0.47851562 to 0.47851562
- leftward_aggregate_vector: bfloat16 [256, 32], replicated, may hold values from -0.375 to 0.375
- starboard_pooled_factor: bfloat16 [256, 32], replicated, may hold values from -0.375 to 0.375
- average_final_matrix: bfloat16 [1024, 128], replicated, may hold values from -0.1875 to 0.1875
- first_edge_sigmoid: bfloat16 [128, 128], replicated, may hold values from -0.5 to 0.5
- first_edge_matrix: bfloat16 [128, 128], replicated, may hold values from -0.5 to 0.5
- second_edge_sigmoid: bfloat16 [128, 128], replicated, may hold values from -0.5 to 0.5
- latter_pairing_grid: bfloat16 [128, 128], replicated, may hold values from -0.5 to 0.5
- edge_final_sigmoid: bfloat16 [128, 128], replicated, may hold values from -0.5 to 0.5
- edge_final_matrix: bfloat16 [128, 128], replicated, may hold values from -0.5 to 0.5
Outputs:
- pair_out: bfloat16 [512, 512, 128], P('dap', 'blk')
The draws below stay inside these ranges and needn't reach their ends.
All inputs are finite; a program needn't handle non-finite values.
Results may differ from the reference program's by a relative error of at most 0.03.
Values may be sent and summed in bfloat16 or wider, within the bound.
A program may use at most 128 MiB of HBM per device.

```python
import math
import jax
import jax.numpy as jnp
from jax import lax

CM = 256
CZ = 128
CH = 32
CT = 128
RES_DEV = 8
SEQ_DEV = 128
N = 512
S = 512
N_DAP = 64


def draw_coevolution_profile_tensor(key, part):
    key = jax.random.fold_in(key, 11)
    keys = jax.random.split(key, 2)
    spread = jnp.exp(jax.random.uniform(keys[1], (CM,), jnp.float32, 0.0, math.log(12.0)))
    noise = jax.random.normal(keys[0], (S, N, CM), jnp.float32)
    values = noise * spread[None, None, :]
    return jnp.clip(values, -60.0, 60.0).astype(jnp.bfloat16)


def levels(stream_key, shape, cuts, low, top_value):
    factor_of, own = 1.0, jax.random.fold_in(stream_key, 6)
    for axis_at, parts in cuts:
        heights = jnp.exp(jax.random.uniform(jax.random.fold_in(own, axis_at), (parts,), jnp.float32, low / len(cuts), top_value / len(cuts)))
        factor_of = factor_of * jnp.repeat(heights, shape[axis_at] // parts).reshape([-1 if axis == axis_at else 1 for axis in range(len(shape))])
    return factor_of


def bell_draw(own_key, dims, scale, most, cuts=(), held_as=jnp.bfloat16):
    result = scale * jax.random.normal(own_key, dims, jnp.float32)
    if cuts:
        result = result * levels(own_key, dims, cuts, -0.22, 0.18)
    return jnp.clip(result, -most, most).astype(held_as)


def setup_inputs(seed: int = 0) -> dict:
    splits = jax.random.split(jax.random.key(seed), 12)
    return {
        "coevolution_profile_tensor": draw_coevolution_profile_tensor(jax.random.fold_in(splits[11], 71), 0),
        "residue_couple_embedding": bell_draw(splits[1], (N, N, CZ), 0.08, 0.47851562, ((0, 64),)),
        "leftward_aggregate_vector": bell_draw(splits[2], (CM, CH), CM ** -0.5, 0.375),
        "starboard_pooled_factor": bell_draw(splits[3], (CM, CH), CM ** -0.5, 0.375),
        "average_final_matrix": bell_draw(splits[4], (CH * CH, CZ), (CH * CH) ** -0.5, 0.1875),
        "first_edge_sigmoid": bell_draw(splits[5], (CZ, CT), CZ ** -0.5, 0.5),
        "first_edge_matrix": bell_draw(splits[6], (CZ, CT), CZ ** -0.5, 0.5),
        "second_edge_sigmoid": bell_draw(splits[7], (CZ, CT), CZ ** -0.5, 0.5),
        "latter_pairing_grid": bell_draw(splits[8], (CZ, CT), CZ ** -0.5, 0.5),
        "edge_final_sigmoid": bell_draw(splits[9], (CZ, CZ), CZ ** -0.5, 0.5),
        "edge_final_matrix": bell_draw(splits[10], (CT, CZ), CT ** -0.5, 0.5),
    }


def zscore_channelwise(values):
    mean = lax.optimization_barrier(jnp.mean(values, axis=-1, keepdims=True))
    centered = values - mean
    var = lax.optimization_barrier(jnp.mean(centered * centered, axis=-1, keepdims=True))
    return centered * lax.rsqrt(var + 1e-05)

def linear_map_onto(values, weight):
    return jnp.einsum('abd,dc->abc', values.astype(jnp.float32), weight.astype(jnp.float32))

def reference(coevolution_profile_tensor, residue_couple_embedding, leftward_aggregate_vector, starboard_pooled_factor, average_final_matrix, first_edge_sigmoid, first_edge_matrix, second_edge_sigmoid, latter_pairing_grid, edge_final_sigmoid, edge_final_matrix):
    weighted_covariation_array = zscore_channelwise(coevolution_profile_tensor.astype(jnp.float32)).astype(jnp.bfloat16)
    port_operand = linear_map_onto(weighted_covariation_array, leftward_aggregate_vector).astype(jnp.bfloat16)
    rightward_multiplicand = linear_map_onto(weighted_covariation_array, starboard_pooled_factor).astype(jnp.bfloat16)
    groups = S // SEQ_DEV
    left_groups = port_operand.reshape(groups, SEQ_DEV, N, CH)
    right_groups = rightward_multiplicand.reshape(groups, SEQ_DEV, N, CH).astype(jnp.float32)
    outer_weight = average_final_matrix.astype(jnp.float32)

    def tile_of_lines(index):
        start = (index * RES_DEV).astype(jnp.int32)
        piece = lax.dynamic_slice_in_dim(left_groups, start, RES_DEV, 2)

        def add_group(outer, pieces):
            left_part, right_part = pieces
            product = jnp.einsum('sic,sje->ijce', left_part.astype(jnp.float32), right_part)
            return (outer + product.reshape(RES_DEV, N, CH * CH), None)
        initial = jnp.zeros((RES_DEV, N, CH * CH), jnp.float32)
        outer, _ = lax.scan(add_group, initial, (piece, right_groups))
        return jnp.einsum('ijf,fd->ijd', outer, outer_weight, precision=lax.Precision.HIGHEST)
    total = lax.map(tile_of_lines, jnp.arange(N_DAP, dtype=jnp.int32)).reshape(N, N, CZ)
    updated = (residue_couple_embedding.astype(jnp.float32) + total / S).astype(jnp.bfloat16)
    pair_norm = zscore_channelwise(updated.astype(jnp.float32)).astype(jnp.bfloat16)
    lhs = (jax.nn.sigmoid(linear_map_onto(pair_norm, first_edge_sigmoid)) * linear_map_onto(pair_norm, first_edge_matrix)).astype(jnp.bfloat16)
    rhs = (jax.nn.sigmoid(linear_map_onto(pair_norm, second_edge_sigmoid)) * linear_map_onto(pair_norm, latter_pairing_grid)).astype(jnp.bfloat16)
    rhs_wide = rhs.astype(jnp.float32)

    def triangle_block(index):
        start = (index * RES_DEV).astype(jnp.int32)
        piece = lax.dynamic_slice_in_dim(lhs, start, RES_DEV, 0).astype(jnp.float32)
        return jnp.einsum('ikc,jkc->ijc', piece, rhs_wide)
    mixed = lax.map(triangle_block, jnp.arange(N_DAP, dtype=jnp.int32)).reshape(N, N, CT)
    mixed_norm = zscore_channelwise(mixed).astype(jnp.bfloat16)
    projected = linear_map_onto(mixed_norm, edge_final_matrix)
    gate = jax.nn.sigmoid(linear_map_onto(pair_norm, edge_final_sigmoid))
    return (updated.astype(jnp.float32) + gate * projected).astype(jnp.bfloat16)
```

```python
import functools

import jax
import jax.numpy as jnp
from jax import lax
from jax.experimental import pallas as pl
from jax.experimental.pallas import tpu as pltpu
from jax.sharding import PartitionSpec as P

NZ = 8
NC = 2
ROWS = 8
EPS = 1e-5
MESH = pl.DeviceIdType.MESH
F32 = jnp.float32
BF16 = jnp.bfloat16


def nt(a, b):
    return lax.dot_general(a, b, (((1,), (1,)), ((), ())), preferred_element_type=F32)


def zscore(v, axis):
    centered = v - jnp.mean(v, axis=axis, keepdims=True)
    var = jnp.mean(centered * centered, axis=axis, keepdims=True)
    return centered * lax.rsqrt(var + EPS)


def device(x, y, z, c):
    return (x * NZ + z) * NC + c, y


def kernel(
    nx, ny, seqs,
    msa_ref, pair_ref, wl_ref, wr_ref, wo_ref, ag_ref, ap_ref, bg_ref, bp_ref, fg_ref, fp_ref,
    out_ref,
    xf, lscr, lsend, lbuf, rsend, rbuf, abuf, bd, tsend, tbuf, vbuf, pairv, upd, pn, wt4,
    lrscr, lrsend, lrbuf, lrsib, msend, mbuf, nscr, gates,
    pair_sem, lsem, rsem, csem, tsend_sem, trecv_sem, asem, ssem, msem,
):
    d = lax.axis_index("dap")
    y = lax.axis_index("blk")
    x, z, c = d // (NZ * NC), (d // NC) % NZ, d % NC
    sd = msa_ref.shape[0] // ROWS
    ch = wl_ref.shape[1]
    cz = wo_ref.shape[1]
    jr = ROWS // ny
    slab = 4
    njo = NZ * jr // slab
    width = NZ * NC * ROWS
    nxz = nx * NZ
    peers = nx * ny * NZ
    sibling = device(x, y, z, 1 - c)

    def peer(k):
        r = lax.rem(k, ny * NZ)
        x2 = lax.rem(x + lax.div(k, ny * NZ), nx)
        z2 = lax.rem(z + lax.div(r, ny), NZ)
        y2 = lax.rem(y + lax.rem(r, ny), ny)
        return x2, y2, z2

    def greet(k, carry):
        x2, y2, z2 = peer(k)
        pl.semaphore_signal(barrier, inc=1, device_id=device(x2, y2, z2, c), device_id_type=MESH)
        return carry

    barrier = pltpu.get_barrier_semaphore()
    pl.semaphore_signal(barrier, inc=1, device_id=sibling, device_id_type=MESH)
    lax.fori_loop(1, peers, greet, 0)

    pair_copy = pltpu.make_async_copy(
        pair_ref.at[:, pl.ds(pl.multiple_of(y * width, width), width), :], pairv, pair_sem
    )
    pair_copy.start()

    lanes = xf.shape[1]
    blocks = msa_ref.shape[1] // lanes
    for h in range(blocks):
        xf[h * sd * ROWS : (h + 1) * sd * ROWS] = msa_ref[:, h * lanes : (h + 1) * lanes].astype(F32)
    wlr = jnp.concatenate([wl_ref[...].astype(F32).T, wr_ref[...].astype(F32).T], axis=0).astype(BF16)
    for i in range(ROWS):
        v = jnp.concatenate(
            [xf[pl.ds(h * sd * ROWS + i, sd, stride=ROWS), :] for h in range(blocks)], axis=1
        )
        v = zscore(v, 1).astype(BF16)
        proj = nt(wlr, v)
        lscr[pl.ds(i, ch, stride=ROWS), :] = proj[:ch]
        rsend[i // jr, (i % jr) * ch : (i % jr + 1) * ch, :] = proj[ch:].astype(BF16)
    left = lscr[...].astype(BF16)
    lsend[...] = left
    lbuf[y * nx + x] = left
    rbuf[c, y * NZ + z] = rsend[y]

    pl.semaphore_wait(barrier, peers)

    def send_right(k, carry):
        z2 = lax.rem(z + lax.div(k, ny), NZ)
        y2 = lax.rem(y + lax.rem(k, ny), ny)
        pltpu.make_async_remote_copy(
            rsend.at[y2], rbuf.at[c, y * NZ + z], rsem.at[0], rsem.at[1],
            device_id=device(x, y2, z2, c), device_id_type=MESH,
        ).start()
        return carry

    def send_left(k, carry):
        x2 = lax.rem(x + lax.div(k, ny), nx)
        y2 = lax.rem(y + lax.rem(k, ny), ny)
        pltpu.make_async_remote_copy(
            lsend, lbuf.at[y * nx + x], lsem.at[0], lsem.at[1],
            device_id=device(x2, y2, z, c), device_id_type=MESH,
        ).start()
        return carry

    lax.fori_loop(1, ny * NZ, send_right, 0)
    lax.fori_loop(1, nx * ny, send_left, 0)

    bd[...] = jnp.zeros_like(bd)
    for q in range(ch):
        w = wo_ref[q * ch : (q + 1) * ch, :]
        for t in range(slab):
            bd[(q * slab + t) * ch : (q * slab + t + 1) * ch, t * cz : (t + 1) * cz] = w
    for t, ref in enumerate((ag_ref, ap_ref, bg_ref, bp_ref)):
        wt4[t * cz : (t + 1) * cz, :] = ref[...].astype(F32).T.astype(BF16)

    def many(ref, count, sem):
        part = ref.at[pl.ds(0, count)]
        pltpu.make_async_copy(part, part, sem).wait()

    many(rbuf.at[0], ny * NZ - 1, rsem.at[1])
    cross = pltpu.make_async_remote_copy(
        rbuf.at[c], rbuf.at[c], csem.at[0], csem.at[1], device_id=sibling, device_id_type=MESH
    )
    cross.start()
    many(lbuf, nx * ny - 1, lsem.at[1])

    def outer(half):
        right = rbuf[half]
        right = jnp.concatenate(
            [right[s * NZ : (s + 1) * NZ].reshape(NZ * jr * ch, sd) for s in range(ny)], axis=1
        )

        def one(g, carry):
            rows = jnp.concatenate([lbuf[s * nx + g] for s in range(ny)], axis=1)
            prod = nt(rows, right)
            for q in range(ch):
                part = prod[q * ROWS : (q + 1) * ROWS]
                abuf[half * nx + g, :, q * slab * ch : (q + 1) * slab * ch] = jnp.concatenate(
                    [part[:, t * slab * ch : (t + 1) * slab * ch] for t in range(njo)], axis=0
                ).astype(BF16)
            return carry

        lax.fori_loop(0, nx, one, 0)

    outer(c)
    cross.wait_recv()
    outer(1 - c)
    mixer = abuf[...].reshape(NC * nx * njo * ROWS, slab * ch * ch)
    total = jnp.dot(mixer, bd[...], preferred_element_type=F32)
    step = njo * ROWS
    for h in range(NC):
        for g in range(nx):
            part = total[(h * nx + g) * step : (h * nx + g + 1) * step]
            for t in range(slab):
                tsend[g, h, t] = part[:, t * cz : (t + 1) * cz].astype(BF16)

    for g in range(nx):
        here = jnp.logical_and(x == g, y == x)

        @pl.when(here)
        def _():
            tbuf[y] = tsend[g]

        @pl.when(jnp.logical_not(here))
        def _():
            pltpu.make_async_remote_copy(
                tsend.at[g], tbuf.at[y], tsend_sem.at[g], trecv_sem.at[y],
                device_id=device(g, x, z, c), device_id_type=MESH,
            ).start()

    pair_copy.wait()
    for s in range(ny):

        @pl.when(jnp.logical_not(jnp.logical_and(x == y, y == s)))
        def _():
            pltpu.make_async_copy(tbuf.at[s], tbuf.at[s], trecv_sem.at[s]).wait()

        for h in range(NC):
            for t in range(slab):
                part = tbuf[s, h, t].astype(F32)
                for o in range(njo):
                    flat = o * slab + t
                    j = ((flat // jr) * NC + h) * ROWS + s * jr + flat % jr
                    vbuf[j * ROWS : (j + 1) * ROWS, :] = part[o * ROWS : (o + 1) * ROWS]

    for i in range(ROWS):
        v = pairv[i].astype(F32) + vbuf[pl.ds(i, width, stride=ROWS), :] * (1.0 / seqs)
        u = v.astype(BF16)
        upd[i] = u
        norm = zscore(u.astype(F32), 1).astype(BF16)
        pn[i] = norm
        four = nt(wt4[...], norm)
        lrscr[pl.ds(i, cz, stride=2 * ROWS), :] = jax.nn.sigmoid(four[:cz]) * four[cz : 2 * cz]
        lrscr[pl.ds(ROWS + i, cz, stride=2 * ROWS), :] = (
            jax.nn.sigmoid(four[2 * cz : 3 * cz]) * four[3 * cz :]
        )
    lrsend[...] = lrscr[...].reshape(cz, 2 * ROWS, width).astype(BF16)

    own = y * nxz + x * NZ + z

    def send_channel(k, carry):
        x2, y2, z2 = peer(k)
        pltpu.make_async_remote_copy(
            lrsend.at[y2 * nxz + x2 * NZ + z2], lrbuf.at[own], asem.at[0], asem.at[1],
            device_id=device(x2, y2, z2, c), device_id_type=MESH,
        ).start()
        return carry

    lax.fori_loop(1, peers, send_channel, 0)
    lrbuf[own] = lrsend[own]
    gates[...] = jax.nn.sigmoid(
        jnp.dot(pn[...].reshape(ROWS * width, cz), fg_ref[...], preferred_element_type=F32)
    )
    many(lrbuf, peers - 1, asem.at[1])
    swap = pltpu.make_async_remote_copy(
        lrbuf, lrsib, ssem.at[0], ssem.at[1], device_id=sibling, device_id_type=MESH
    )
    swap.start()

    def wide(ref):
        return jnp.concatenate(
            [ref[s * nxz : (s + 1) * nxz].astype(F32) for s in range(ny)], axis=2
        )

    mine = wide(lrbuf)
    lhs = mine[:, :ROWS].reshape(nxz * ROWS, ny * width).astype(BF16)
    mine = mine[:, ROWS:]
    swap.wait_recv()
    other = wide(lrsib)[:, ROWS:]
    first = c == 0
    rhs = jnp.concatenate([jnp.where(first, mine, other), jnp.where(first, other, mine)], axis=1)
    rhs = rhs.reshape(nxz * NC * ROWS, ny * width).astype(BF16)
    mixed = nt(lhs, rhs)
    for s in range(ny):
        msend[s * nxz : (s + 1) * nxz] = mixed[:, s * width : (s + 1) * width].reshape(
            nxz, ROWS, width
        )

    def send_back(k, carry):
        x2, y2, z2 = peer(k)
        pltpu.make_async_remote_copy(
            msend.at[y2 * nxz + x2 * NZ + z2], mbuf.at[own], msem.at[0], msem.at[1],
            device_id=device(x2, y2, z2, c), device_id_type=MESH,
        ).start()
        return carry

    lax.fori_loop(1, peers, send_back, 0)
    mbuf[own] = msend[own]
    many(mbuf, peers - 1, msem.at[1])

    nscr[...] = zscore(mbuf[...], 0).reshape(cz * ROWS, width)
    for i in range(ROWS):
        norm = nscr[pl.ds(i, cz, stride=ROWS), :].T.astype(BF16)
        proj = jnp.dot(norm, fp_ref[...], preferred_element_type=F32)
        out_ref[i] = (upd[i].astype(F32) + gates[i * width : (i + 1) * width] * proj).astype(BF16)

    many(rbuf.at[0], ny * NZ - 1, rsem.at[0])
    many(lbuf, nx * ny - 1, lsem.at[0])
    cross.wait_send()
    for g in range(nx):

        @pl.when(jnp.logical_not(jnp.logical_and(x == g, y == x)))
        def _():
            pltpu.make_async_copy(tsend.at[g], tsend.at[g], tsend_sem.at[g]).wait()

    many(lrbuf, peers - 1, asem.at[0])
    swap.wait_send()
    many(mbuf, peers - 1, msem.at[0])


def shards(msa, pair, wl, wr, wo, *weights):
    ny = lax.axis_size("blk")
    nx = lax.axis_size("dap") // (NZ * NC)
    sd, _, cm = msa.shape
    ch, cz = wl.shape[1], wo.shape[1]
    jr = ROWS // ny
    width = NZ * NC * ROWS
    step = NZ * jr // 4 * ROWS
    peers = nx * ny * NZ
    vmem = pltpu.VMEM
    scratch = [
        vmem((cm // 128 * sd * ROWS, 128), F32),
        vmem((ch * ROWS, sd), F32),
        vmem((ch * ROWS, sd), BF16),
        vmem((ny * nx, ch * ROWS, sd), BF16),
        vmem((ny, jr * ch, sd), BF16),
        vmem((NC, ny * NZ, jr * ch, sd), BF16),
        vmem((NC * nx, step, 4 * ch * ch), BF16),
        vmem((4 * ch * ch, 4 * cz), BF16),
        vmem((nx, NC, 4, step, cz), BF16),
        vmem((ny, NC, 4, step, cz), BF16),
        vmem((width * ROWS, cz), F32),
        vmem((ROWS, width, cz), BF16),
        vmem((ROWS, width, cz), BF16),
        vmem((ROWS, width, cz), BF16),
        vmem((4 * cz, cz), BF16),
        vmem((cz * 2 * ROWS, width), F32),
        vmem((cz, 2 * ROWS, width), BF16),
        vmem((peers, 2 * ROWS, width), BF16),
        vmem((peers, 2 * ROWS, width), BF16),
        vmem((peers, ROWS, width), F32),
        vmem((peers, ROWS, width), F32),
        vmem((cz * ROWS, width), F32),
        vmem((ROWS * width, cz), F32),
        pltpu.SemaphoreType.DMA,
        pltpu.SemaphoreType.DMA((2,)),
        pltpu.SemaphoreType.DMA((2,)),
        pltpu.SemaphoreType.DMA((2,)),
        pltpu.SemaphoreType.DMA((nx,)),
        pltpu.SemaphoreType.DMA((ny,)),
        pltpu.SemaphoreType.DMA((2,)),
        pltpu.SemaphoreType.DMA((2,)),
        pltpu.SemaphoreType.DMA((2,)),
    ]
    whole = pl.BlockSpec(memory_space=pltpu.VMEM)
    return pl.pallas_call(
        functools.partial(kernel, nx, ny, ny * sd),
        out_shape=jax.ShapeDtypeStruct((ROWS, width, cz), BF16),
        in_specs=[whole, pl.BlockSpec(memory_space=pl.ANY)] + [whole] * 9,
        out_specs=whole,
        scratch_shapes=scratch,
        compiler_params=pltpu.CompilerParams(
            collective_id=0, has_side_effects=True, vmem_limit_bytes=48 * 2**20
        ),
    )(msa.reshape(sd * ROWS, cm), pair, wl, wr, wo, *weights)


def solution(mesh):
    placed = (P("blk", "dap", None), P("dap", None, None)) + (P(),) * 9
    return jax.shard_map(
        shards, mesh=mesh, in_specs=placed, out_specs=P("dap", "blk", None), check_vma=False
    )
```

```python
import functools

import jax
import jax.numpy as jnp
from jax import lax
from jax.experimental import pallas as pl
from jax.experimental.pallas import tpu as pltpu
from jax.sharding import PartitionSpec as P

NZ = 8
NC = 2
ROWS = 8
EPS = 1e-5
MESH = pl.DeviceIdType.MESH
F32 = jnp.float32
BF16 = jnp.bfloat16


def nt(a, b):
    return lax.dot_general(a, b, (((1,), (1,)), ((), ())), preferred_element_type=F32)


def zscore(v, axis):
    centered = v - jnp.mean(v, axis=axis, keepdims=True)
    var = jnp.mean(centered * centered, axis=axis, keepdims=True)
    return centered * lax.rsqrt(var + EPS)


def device(x, y, z, c):
    return (x * NZ + z) * NC + c, y


def kernel(
    nx, ny, seqs,
    msa_ref, pair_ref, wl_ref, wr_ref, wo_ref, ag_ref, ap_ref, bg_ref, bp_ref, fg_ref, fp_ref,
    out_ref,
    xf, lscr, lsend, lbuf, rsend, rbuf, abuf, bd, tsend, tbuf, vbuf, pairv, upd, pn, wt4,
    lrscr, lrsend, lrbuf, lrsib, msend, mbuf, nscr, gates,
    msa_v, wl_v, wr_v, wo_v, ag_v, ap_v, bg_v, bp_v, fg_v, fp_v,
    load_sem, pair_sem, lsem, rsem, csem, tsend_sem, trecv_sem, asem, ssem, msem,
):
    local = (msa_v, wl_v, wr_v, wo_v, ag_v, ap_v, bg_v, bp_v, fg_v, fp_v)
    d = lax.axis_index("dap")
    y = lax.axis_index("blk")
    x, z, c = d // (NZ * NC), (d // NC) % NZ, d % NC
    sd = msa_ref.shape[0] // ROWS
    ch = wl_ref.shape[0]
    cz = wo_ref.shape[1]
    jr = ROWS // ny
    slab = 4
    njo = NZ * jr // slab
    width = NZ * NC * ROWS
    nxz = nx * NZ
    peers = nx * ny * NZ
    sibling = device(x, y, z, 1 - c)

    def peer(k):
        r = lax.rem(k, ny * NZ)
        x2 = lax.rem(x + lax.div(k, ny * NZ), nx)
        z2 = lax.rem(z + lax.div(r, ny), NZ)
        y2 = lax.rem(y + lax.rem(r, ny), ny)
        return x2, y2, z2

    barrier = pltpu.get_barrier_semaphore()

    def greet(x2, y2, z2, c2):
        pl.semaphore_signal(barrier, inc=1, device_id=device(x2, y2, z2, c2), device_id_type=MESH)

    def greet_yz(k, carry):
        greet(x, lax.rem(y + lax.rem(k, ny), ny), lax.rem(z + lax.div(k, ny), NZ), c)
        return carry

    def greet_xy(k, carry):
        greet(lax.rem(x + lax.div(k, ny), nx), lax.rem(y + lax.rem(k, ny), ny), z, c)
        return carry

    greet(x, y, z, 1 - c)
    lax.fori_loop(1, ny * NZ, greet_yz, 0)
    lax.fori_loop(ny, nx * ny, greet_xy, 0)

    sources = (msa_ref, wl_ref, wr_ref, wo_ref, ag_ref, ap_ref, bg_ref, bp_ref, fg_ref, fp_ref)
    loads = [
        pltpu.make_async_copy(source, target, load_sem.at[t])
        for t, (source, target) in enumerate(zip(sources, local))
    ]
    for load in loads:
        load.start()
    msa_ref, wl_ref, wr_ref, wo_ref, ag_ref, ap_ref, bg_ref, bp_ref, fg_ref, fp_ref = local
    pair_copy = pltpu.make_async_copy(
        pair_ref.at[:, pl.ds(pl.multiple_of(y * width, width), width), :], pairv, pair_sem
    )
    pair_copy.start()
    for load in loads[:3]:
        load.wait()

    lanes = xf.shape[1]
    blocks = msa_ref.shape[1] // lanes
    for h in range(blocks):
        xf[h * sd * ROWS : (h + 1) * sd * ROWS] = msa_ref[:, h * lanes : (h + 1) * lanes].astype(F32)
    wlr = jnp.concatenate([wl_ref[...], wr_ref[...]], axis=0)
    for i in range(ROWS):
        v = jnp.concatenate(
            [xf[pl.ds(h * sd * ROWS + i, sd, stride=ROWS), :] for h in range(blocks)], axis=1
        )
        v = zscore(v, 1).astype(BF16)
        proj = nt(wlr, v)
        lscr[pl.ds(i, ch, stride=ROWS), :] = proj[:ch]
        rsend[i // jr, (i % jr) * ch : (i % jr + 1) * ch, :] = proj[ch:].astype(BF16)
    left = lscr[...].astype(BF16)
    lsend[...] = left
    lbuf[y * nx + x] = left
    rbuf[c, y * NZ + z] = rsend[y]

    pl.semaphore_wait(barrier, ny * NZ + (nx - 1) * ny)

    def send_right(k, carry):
        z2 = lax.rem(z + lax.div(k, ny), NZ)
        y2 = lax.rem(y + lax.rem(k, ny), ny)
        pltpu.make_async_remote_copy(
            rsend.at[y2], rbuf.at[c, y * NZ + z], rsem.at[0], rsem.at[1],
            device_id=device(x, y2, z2, c), device_id_type=MESH,
        ).start()
        return carry

    def send_left(k, carry):
        x2 = lax.rem(x + lax.div(k, ny), nx)
        y2 = lax.rem(y + lax.rem(k, ny), ny)
        pltpu.make_async_remote_copy(
            lsend, lbuf.at[y * nx + x], lsem.at[0], lsem.at[1],
            device_id=device(x2, y2, z, c), device_id_type=MESH,
        ).start()
        return carry

    lax.fori_loop(1, ny * NZ, send_right, 0)
    lax.fori_loop(1, nx * ny, send_left, 0)

    for load in loads[3:]:
        load.wait()
    bd[...] = jnp.zeros_like(bd)
    for q in range(ch):
        w = wo_ref[q * ch : (q + 1) * ch, :]
        for t in range(slab):
            bd[(q * slab + t) * ch : (q * slab + t + 1) * ch, t * cz : (t + 1) * cz] = w
    for t, ref in enumerate((ag_ref, ap_ref, bg_ref, bp_ref)):
        wt4[t * cz : (t + 1) * cz, :] = ref[...].astype(F32).T.astype(BF16)

    def many(ref, count, sem):
        part = ref.at[pl.ds(0, count)]
        pltpu.make_async_copy(part, part, sem).wait()

    many(rbuf.at[0], ny * NZ - 1, rsem.at[1])
    cross = pltpu.make_async_remote_copy(
        rbuf.at[c], rbuf.at[c], csem.at[0], csem.at[1], device_id=sibling, device_id_type=MESH
    )
    cross.start()
    many(lbuf, nx * ny - 1, lsem.at[1])

    def outer(half):
        right = rbuf[half]
        right = jnp.concatenate(
            [right[s * NZ : (s + 1) * NZ].reshape(NZ * jr * ch, sd) for s in range(ny)], axis=1
        )

        def one(g, carry):
            rows = jnp.concatenate([lbuf[s * nx + g] for s in range(ny)], axis=1)
            prod = nt(rows, right)
            for q in range(ch):
                part = prod[q * ROWS : (q + 1) * ROWS]
                abuf[half * nx + g, :, q * slab * ch : (q + 1) * slab * ch] = jnp.concatenate(
                    [part[:, t * slab * ch : (t + 1) * slab * ch] for t in range(njo)], axis=0
                ).astype(BF16)
            return carry

        lax.fori_loop(0, nx, one, 0)

    outer(c)
    cross.wait_recv()
    outer(1 - c)
    mixer = abuf[...].reshape(NC * nx * njo * ROWS, slab * ch * ch)
    total = jnp.dot(mixer, bd[...], preferred_element_type=F32)
    step = njo * ROWS
    for h in range(NC):
        for g in range(nx):
            part = total[(h * nx + g) * step : (h * nx + g + 1) * step]
            for t in range(slab):
                tsend[g, h, t] = part[:, t * cz : (t + 1) * cz].astype(BF16)

    for g in range(nx):
        here = jnp.logical_and(x == g, y == x)

        @pl.when(here)
        def _():
            tbuf[y] = tsend[g]

        @pl.when(jnp.logical_not(here))
        def _():
            pltpu.make_async_remote_copy(
                tsend.at[g], tbuf.at[y], tsend_sem.at[g], trecv_sem.at[y],
                device_id=device(g, x, z, c), device_id_type=MESH,
            ).start()

    pair_copy.wait()
    for s in range(ny):

        @pl.when(jnp.logical_not(jnp.logical_and(x == y, y == s)))
        def _():
            pltpu.make_async_copy(tbuf.at[s], tbuf.at[s], trecv_sem.at[s]).wait()

        for h in range(NC):
            for t in range(slab):
                part = tbuf[s, h, t].astype(F32)
                for o in range(njo):
                    flat = o * slab + t
                    j = ((flat // jr) * NC + h) * ROWS + s * jr + flat % jr
                    vbuf[j * ROWS : (j + 1) * ROWS, :] = part[o * ROWS : (o + 1) * ROWS]

    for i in range(ROWS):
        v = pairv[i].astype(F32) + vbuf[pl.ds(i, width, stride=ROWS), :] * (1.0 / seqs)
        u = v.astype(BF16)
        upd[i] = u
        norm = zscore(u.astype(F32), 1).astype(BF16)
        pn[i] = norm
        four = nt(wt4[...], norm)
        lrscr[pl.ds(i, cz, stride=2 * ROWS), :] = jax.nn.sigmoid(four[:cz]) * four[cz : 2 * cz]
        lrscr[pl.ds(ROWS + i, cz, stride=2 * ROWS), :] = (
            jax.nn.sigmoid(four[2 * cz : 3 * cz]) * four[3 * cz :]
        )
    lrsend[...] = lrscr[...].reshape(cz, 2 * ROWS, width).astype(BF16)

    own = y * nxz + x * NZ + z

    def send_channel(k, carry):
        x2, y2, z2 = peer(k)
        pltpu.make_async_remote_copy(
            lrsend.at[y2 * nxz + x2 * NZ + z2], lrbuf.at[own], asem.at[0], asem.at[1],
            device_id=device(x2, y2, z2, c), device_id_type=MESH,
        ).start()
        return carry

    lax.fori_loop(1, peers, send_channel, 0)
    lrbuf[own] = lrsend[own]
    gates[...] = jax.nn.sigmoid(
        jnp.dot(pn[...].reshape(ROWS * width, cz), fg_ref[...], preferred_element_type=F32)
    )
    many(lrbuf, peers - 1, asem.at[1])
    swap = pltpu.make_async_remote_copy(
        lrbuf, lrsib, ssem.at[0], ssem.at[1], device_id=sibling, device_id_type=MESH
    )
    swap.start()

    def wide(ref):
        return jnp.concatenate(
            [ref[s * nxz : (s + 1) * nxz].astype(F32) for s in range(ny)], axis=2
        )

    mine = wide(lrbuf)
    lhs = mine[:, :ROWS].reshape(nxz * ROWS, ny * width).astype(BF16)
    mine = mine[:, ROWS:]
    swap.wait_recv()
    other = wide(lrsib)[:, ROWS:]
    first = c == 0
    rhs = jnp.concatenate([jnp.where(first, mine, other), jnp.where(first, other, mine)], axis=1)
    rhs = rhs.reshape(nxz * NC * ROWS, ny * width).astype(BF16)
    mixed = nt(lhs, rhs)
    for s in range(ny):
        msend[s * nxz : (s + 1) * nxz] = mixed[:, s * width : (s + 1) * width].reshape(
            nxz, ROWS, width
        )

    def send_back(k, carry):
        x2, y2, z2 = peer(k)
        pltpu.make_async_remote_copy(
            msend.at[y2 * nxz + x2 * NZ + z2], mbuf.at[own], msem.at[0], msem.at[1],
            device_id=device(x2, y2, z2, c), device_id_type=MESH,
        ).start()
        return carry

    lax.fori_loop(1, peers, send_back, 0)
    mbuf[own] = msend[own]
    many(mbuf, peers - 1, msem.at[1])

    nscr[...] = zscore(mbuf[...], 0).reshape(cz * ROWS, width)
    for i in range(ROWS):
        norm = nscr[pl.ds(i, cz, stride=ROWS), :].T.astype(BF16)
        proj = jnp.dot(norm, fp_ref[...], preferred_element_type=F32)
        out_ref[i] = (upd[i].astype(F32) + gates[i * width : (i + 1) * width] * proj).astype(BF16)

    many(rbuf.at[0], ny * NZ - 1, rsem.at[0])
    many(lbuf, nx * ny - 1, lsem.at[0])
    cross.wait_send()
    for g in range(nx):

        @pl.when(jnp.logical_not(jnp.logical_and(x == g, y == x)))
        def _():
            pltpu.make_async_copy(tsend.at[g], tsend.at[g], tsend_sem.at[g]).wait()

    many(lrbuf, peers - 1, asem.at[0])
    swap.wait_send()
    many(mbuf, peers - 1, msem.at[0])


def shards(msa, pair, wl, wr, wo, *weights):
    ny = lax.axis_size("blk")
    nx = lax.axis_size("dap") // (NZ * NC)
    sd, _, cm = msa.shape
    ch, cz = wl.shape[1], wo.shape[1]
    jr = ROWS // ny
    width = NZ * NC * ROWS
    step = NZ * jr // 4 * ROWS
    peers = nx * ny * NZ
    vmem = pltpu.VMEM
    scratch = [
        vmem((cm // 128 * sd * ROWS, 128), F32),
        vmem((ch * ROWS, sd), F32),
        vmem((ch * ROWS, sd), BF16),
        vmem((ny * nx, ch * ROWS, sd), BF16),
        vmem((ny, jr * ch, sd), BF16),
        vmem((NC, ny * NZ, jr * ch, sd), BF16),
        vmem((NC * nx, step, 4 * ch * ch), BF16),
        vmem((4 * ch * ch, 4 * cz), BF16),
        vmem((nx, NC, 4, step, cz), BF16),
        vmem((ny, NC, 4, step, cz), BF16),
        vmem((width * ROWS, cz), F32),
        vmem((ROWS, width, cz), BF16),
        vmem((ROWS, width, cz), BF16),
        vmem((ROWS, width, cz), BF16),
        vmem((4 * cz, cz), BF16),
        vmem((cz * 2 * ROWS, width), F32),
        vmem((cz, 2 * ROWS, width), BF16),
        vmem((peers, 2 * ROWS, width), BF16),
        vmem((peers, 2 * ROWS, width), BF16),
        vmem((peers, ROWS, width), F32),
        vmem((peers, ROWS, width), F32),
        vmem((cz * ROWS, width), F32),
        vmem((ROWS * width, cz), F32),
        vmem((sd * ROWS, cm), BF16),
        vmem((ch, cm), BF16),
        vmem((ch, cm), BF16),
        vmem((ch * ch, cz), BF16),
    ] + [vmem((cz, cz), BF16)] * 6 + [
        pltpu.SemaphoreType.DMA((10,)),
        pltpu.SemaphoreType.DMA,
        pltpu.SemaphoreType.DMA((2,)),
        pltpu.SemaphoreType.DMA((2,)),
        pltpu.SemaphoreType.DMA((2,)),
        pltpu.SemaphoreType.DMA((nx,)),
        pltpu.SemaphoreType.DMA((ny,)),
        pltpu.SemaphoreType.DMA((2,)),
        pltpu.SemaphoreType.DMA((2,)),
        pltpu.SemaphoreType.DMA((2,)),
    ]
    return pl.pallas_call(
        functools.partial(kernel, nx, ny, ny * sd),
        out_shape=jax.ShapeDtypeStruct((ROWS, width, cz), BF16),
        in_specs=[pl.BlockSpec(memory_space=pltpu.HBM)] * 11,
        out_specs=pl.BlockSpec(memory_space=pltpu.VMEM),
        scratch_shapes=scratch,
        compiler_params=pltpu.CompilerParams(
            collective_id=0, has_side_effects=True, vmem_limit_bytes=60 * 2**20
        ),
    )(msa.reshape(sd * ROWS, cm), pair, wl.T, wr.T, wo, *weights)


def solution(mesh):
    placed = (P("blk", "dap", None), P("dap", None, None)) + (P(),) * 9
    return jax.shard_map(
        shards, mesh=mesh, in_specs=placed, out_specs=P("dap", "blk", None), check_vma=False
    )
```

```python
import functools

import jax
import jax.numpy as jnp
from jax import lax
from jax.experimental import pallas as pl
from jax.experimental.pallas import tpu as pltpu
from jax.sharding import PartitionSpec as P

NZ = 8
NC = 2
ROWS = 8
EPS = 1e-5
MESH = pl.DeviceIdType.MESH
F32 = jnp.float32
BF16 = jnp.bfloat16


def nt(a, b):
    return lax.dot_general(a, b, (((1,), (1,)), ((), ())), preferred_element_type=F32)


def zscore(v, axis):
    centered = v - jnp.mean(v, axis=axis, keepdims=True)
    var = jnp.mean(centered * centered, axis=axis, keepdims=True)
    return centered * lax.rsqrt(var + EPS)


def device(x, y, z, c):
    return (x * NZ + z) * NC + c, y


def kernel(
    nx, ny, seqs,
    msa_ref, pair_ref, wl_ref, wr_ref, wo_ref, ag_ref, ap_ref, bg_ref, bp_ref, fg_ref, fp_ref,
    out_ref,
    xf, lscr, lbuf, rsend, rbuf, abuf, bd, pairv, pairf, pstage, psend, pbuf, usend, ubuf, vbuf, upd,
    wt4, lrscr, lrsend, lrbuf, lrsib, lwide, rwide, msend, mbuf, nscr, gates,
    msa_v, wl_v, wr_v, wo_v, ag_v, ap_v, bg_v, bp_v, fg_v, fp_v,
    load_sem, pair_sem, lsem, rsem, csem, psem, usend_sem, urecv_sem, asem, ssem, msem, fsem,
):
    local = (msa_v, wl_v, wr_v, wo_v, ag_v, ap_v, bg_v, bp_v, fg_v, fp_v)
    d = lax.axis_index("dap")
    y = lax.axis_index("blk")
    x, z, c = d // (NZ * NC), (d // NC) % NZ, d % NC
    sd = msa_ref.shape[0] // ROWS
    ch = wl_ref.shape[0]
    cz = wo_ref.shape[1]
    jr = ROWS // ny
    slab = 4
    njo = NZ * jr // slab
    thirds = NC * NZ * jr
    width = NZ * NC * ROWS
    nyx = ny * nx
    zh = NZ // 2
    peers = nyx * NZ
    sibling = device(x, y, z, 1 - c)
    first = c == 0

    def place(x1, y1, z1):
        return (y1 * nx + x1) * NZ + lax.rem(z1, 2) * zh + lax.div(z1, 2)

    def remote(source, target, send, recv, to):
        return pltpu.make_async_remote_copy(
            source, target, send, recv, device_id=to, device_id_type=MESH
        )

    def arrived(part, sem):
        pltpu.make_async_copy(part, part, sem).wait()

    barrier = pltpu.get_barrier_semaphore()

    def greet(x2, y2, z2, c2):
        pl.semaphore_signal(barrier, inc=1, device_id=device(x2, y2, z2, c2), device_id_type=MESH)

    def greet_yz(k, carry):
        greet(x, lax.rem(y + lax.rem(k, ny), ny), lax.rem(z + lax.div(k, ny), NZ), c)
        return carry

    greet(x, y, z, 1 - c)
    for k in range(1, nx):
        greet(lax.rem(x + k, nx), y, z, c)
    lax.fori_loop(1, ny * NZ, greet_yz, 0)

    sources = (msa_ref, wl_ref, wr_ref, wo_ref, ag_ref, ap_ref, bg_ref, bp_ref, fg_ref, fp_ref)
    loads = [
        pltpu.make_async_copy(source, target, load_sem.at[t])
        for t, (source, target) in enumerate(zip(sources, local))
    ]
    for load in loads:
        load.start()
    pair_copy = pltpu.make_async_copy(pair_ref, pairv, pair_sem)
    pair_copy.start()
    for load in loads[:3]:
        load.wait()

    lanes = xf.shape[1]
    blocks = msa_v.shape[1] // lanes
    for h in range(blocks):
        xf[h * sd * ROWS : (h + 1) * sd * ROWS] = msa_v[:, h * lanes : (h + 1) * lanes].astype(F32)
    wlr = jnp.concatenate([wl_v[...], wr_v[...]], axis=0)
    for i in range(ROWS):
        v = jnp.concatenate(
            [xf[pl.ds(h * sd * ROWS + i, sd, stride=ROWS), :] for h in range(blocks)], axis=1
        )
        v = zscore(v, 1).astype(BF16)
        proj = nt(wlr, v)
        lscr[pl.ds(i, ch, stride=ROWS), :] = proj[:ch]
        rsend[i // jr, (i % jr) * ch : (i % jr + 1) * ch, :] = proj[ch:].astype(BF16)
    lbuf[y, x] = lscr[...].astype(BF16)
    rbuf[c, y * NZ + z] = rsend[y]

    pl.semaphore_wait(barrier, ny * NZ + nx - 1)

    half = ch * ROWS // 2
    low, high = pl.ds(0, half), pl.ds(half, half)
    xfirst = lbuf.at[y, x, low]
    yfirst = lbuf.at[y, x, high]
    for k in range(1, nx):
        remote(xfirst, xfirst, lsem.at[0], lsem.at[1], device(lax.rem(x + k, nx), y, z, c)).start()
    for k in range(1, ny):
        remote(yfirst, yfirst, lsem.at[2], lsem.at[3], device(x, lax.rem(y + k, ny), z, c)).start()

    def send_right(k, carry):
        z2 = lax.rem(z + lax.div(k, ny), NZ)
        y2 = lax.rem(y + lax.rem(k, ny), ny)
        remote(
            rsend.at[y2], rbuf.at[c, y * NZ + z], rsem.at[0], rsem.at[1], device(x, y2, z2, c)
        ).start()
        return carry

    lax.fori_loop(1, ny * NZ, send_right, 0)

    arrived(lbuf.at[0, pl.ds(0, nx - 1), low], lsem.at[1])
    ythen = lbuf.at[y, :, low]
    for k in range(1, ny):
        remote(ythen, ythen, lsem.at[4], lsem.at[5], device(x, lax.rem(y + k, ny), z, c)).start()
    arrived(lbuf.at[pl.ds(0, ny - 1), 0, high], lsem.at[3])
    xthen = lbuf.at[:, x, high]
    for k in range(1, nx):
        remote(xthen, xthen, lsem.at[6], lsem.at[7], device(lax.rem(x + k, nx), y, z, c)).start()

    pair_copy.wait()
    columns = pairv.shape[1]
    pairf[...] = pairv[...].astype(F32).reshape(ROWS * columns, cz)
    for i in range(ROWS):
        for h in range(NC):
            for r in range(jr):
                v = pairf[pl.ds(i * columns + h * ROWS + y * jr + r, nx * NZ, stride=NC * ROWS), :]
                for g in range(nx):
                    start = (g * thirds + h * NZ * jr + r) * ROWS + i
                    pstage[pl.ds(start, NZ, stride=jr * ROWS), :] = v[g * NZ : (g + 1) * NZ]
    psend[...] = pstage[...].astype(BF16).reshape(nx, thirds * ROWS, cz)
    pbuf[x] = psend[x]
    for k in range(1, nx):
        x2 = lax.rem(x + k, nx)
        remote(psend.at[x2], pbuf.at[x], psem.at[0], psem.at[1], device(x2, y, z, c)).start()

    for load in loads[3:]:
        load.wait()
    bd[...] = jnp.zeros_like(bd)
    for q in range(ch):
        w = wo_v[q * ch : (q + 1) * ch, :]
        for t in range(slab):
            bd[(q * slab + t) * ch : (q * slab + t + 1) * ch, t * cz : (t + 1) * cz] = w
    for t, ref in enumerate((ag_v, ap_v, bg_v, bp_v)):
        wt4[t * cz : (t + 1) * cz, :] = ref[...].astype(F32).T.astype(BF16)

    arrived(rbuf.at[0, pl.ds(0, ny * NZ - 1)], rsem.at[1])
    cross = remote(rbuf.at[c], rbuf.at[c], csem.at[0], csem.at[1], sibling)
    cross.start()
    arrived(lbuf.at[pl.ds(0, ny - 1), :, low], lsem.at[5])
    arrived(lbuf.at[:, pl.ds(0, nx - 1), high], lsem.at[7])

    def outer(side):
        right = rbuf[side]
        right = jnp.concatenate(
            [right[s * NZ : (s + 1) * NZ].reshape(NZ * jr * ch, sd) for s in range(ny)], axis=1
        )

        def one(g, carry):
            rows = jnp.concatenate([lbuf[s, g] for s in range(ny)], axis=1)
            prod = nt(rows, right)
            for q in range(ch):
                part = prod[q * ROWS : (q + 1) * ROWS]
                abuf[side * nx + g, :, q * slab * ch : (q + 1) * slab * ch] = jnp.concatenate(
                    [part[:, t * slab * ch : (t + 1) * slab * ch] for t in range(njo)], axis=0
                ).astype(BF16)
            return carry

        lax.fori_loop(0, nx, one, 0)

    outer(c)
    cross.wait_recv()
    outer(1 - c)
    step = njo * ROWS
    mixer = abuf[...].reshape(NC * nx * step, slab * ch * ch)
    total = jnp.dot(mixer, bd[...], preferred_element_type=F32)

    arrived(pbuf.at[pl.ds(0, nx - 1)], psem.at[1])
    for g in range(nx):
        tiles = []
        for kk in range(thirds):
            h, flat = divmod(kk, NZ * jr)
            o, t = divmod(flat, slab)
            start = (h * nx + g) * step + o * ROWS
            tiles.append(total[start : start + ROWS, t * cz : (t + 1) * cz])
        u = pbuf[g].astype(F32) + jnp.concatenate(tiles, axis=0) * (1.0 / seqs)
        u = u.astype(BF16)
        usend[g] = u
        vbuf[g * thirds * ROWS : (g + 1) * thirds * ROWS] = u.astype(F32)

    for i in range(ROWS):
        norm = zscore(vbuf[pl.ds(i, width, stride=ROWS), :], 1).astype(BF16)
        four = nt(wt4[...], norm)
        lrscr[pl.ds(i, cz, stride=2 * ROWS), :] = jax.nn.sigmoid(four[:cz]) * four[cz : 2 * cz]
        lrscr[pl.ds(ROWS + i, cz, stride=2 * ROWS), :] = (
            jax.nn.sigmoid(four[2 * cz : 3 * cz]) * four[3 * cz :]
        )
    lrsend[...] = lrscr[...].reshape(cz, 2 * ROWS, width).astype(BF16)

    own = place(x, y, z)

    def send_channel(k, carry):
        r = lax.rem(k, ny * NZ)
        x2 = lax.rem(x + lax.div(k, ny * NZ), nx)
        z2 = lax.rem(z + lax.div(r, ny), NZ)
        y2 = lax.rem(y + lax.rem(r, ny), ny)
        remote(
            lrsend.at[place(x2, y2, z2)], lrbuf.at[own], asem.at[0], asem.at[1],
            device(x2, y2, z2, c),
        ).start()
        return carry

    lax.fori_loop(1, peers, send_channel, 0)
    lrbuf[own] = lrsend[own]

    for g in range(nx):
        here = jnp.logical_and(x == g, y == x)

        @pl.when(here)
        def _():
            ubuf[y] = usend[g]

        @pl.when(jnp.logical_not(here))
        def _():
            remote(
                usend.at[g], ubuf.at[y], usend_sem.at[g], urecv_sem.at[y], device(g, x, z, c)
            ).start()

    for s in range(ny):

        @pl.when(jnp.logical_not(jnp.logical_and(x == y, y == s)))
        def _():
            arrived(ubuf.at[s], urecv_sem.at[s])

        part = ubuf[s].astype(F32)
        for kk in range(thirds):
            h, flat = divmod(kk, NZ * jr)
            j = ((flat // jr) * NC + h) * ROWS + s * jr + flat % jr
            vbuf[j * ROWS : (j + 1) * ROWS, :] = part[kk * ROWS : (kk + 1) * ROWS]
    for i in range(ROWS):
        u = vbuf[pl.ds(i, width, stride=ROWS), :]
        upd[i] = u
        norm = zscore(u, 1).astype(BF16)
        gates[i] = jax.nn.sigmoid(jnp.dot(norm, fg_v[...], preferred_element_type=F32))

    arrived(lrbuf.at[pl.ds(0, peers - 1)], asem.at[1])
    swaps = []
    for s in range(ny):
        part = pl.ds(s * nx * NZ, nx * NZ)
        swaps.append(remote(lrbuf.at[part], lrsib.at[part], ssem.at[0, s], ssem.at[1, s], sibling))
        swaps[-1].start()
    group = lax.broadcasted_iota(jnp.int32, (zh * NC * ROWS, width), 1) // thirds
    for s in range(nyx):
        if s % nx == 0:
            swaps[s // nx].wait_recv()
        mine = lrbuf[s * NZ : (s + 1) * NZ].astype(F32)
        other = lrsib[s * NZ : (s + 1) * NZ].astype(F32)
        m0, m1 = jnp.where(first, mine, other), jnp.where(first, other, mine)
        span = slice(s * width, (s + 1) * width)
        rows = []
        for z2 in range(NZ):
            at = z2 % 2 * zh + z2 // 2
            rows += [m0[at, ROWS:], m1[at, ROWS:]]
        right = jnp.concatenate(rows, axis=0)
        for m in range(nx):
            rolled = pltpu.roll(right, m * thirds, 1) if m else right
            rwide[m * width : (m + 1) * width, span] = rolled.astype(BF16)
        rows = []
        for m in (m0, m1):
            rows.append(jnp.where(first, m[:zh, :ROWS], m[zh:, :ROWS]))
        left = jnp.concatenate(rows, axis=1).reshape(zh * NC * ROWS, width)
        for g in range(nx):
            lwide[g * zh * NC * ROWS : (g + 1) * zh * NC * ROWS, span] = jnp.where(
                group == g, left, 0.0
            ).astype(BF16)
    mixed = nt(lwide[...], rwide[...])
    for g in range(nx):
        for m in range(nx):
            g2 = (g - m) % nx
            part = mixed[g * zh * NC * ROWS : (g + 1) * zh * NC * ROWS, m * width : (m + 1) * width]
            msend[(g2 * nx + g) * zh : (g2 * nx + g + 1) * zh] = part.reshape(
                zh, NC * ROWS, width
            ).astype(BF16)

    side = lax.rem(z, 2)
    home = (y * nx + x) * zh + lax.div(z, 2)

    def send_back(k, carry):
        x2 = lax.rem(x + lax.div(k, ny * zh), nx)
        y2 = lax.rem(y + lax.rem(lax.div(k, zh), ny), ny)
        zh2 = lax.rem(lax.div(z, 2) + lax.rem(k, zh), zh)
        remote(
            msend.at[(y2 * nx + x2) * zh + zh2], mbuf.at[side, home], msem.at[0], msem.at[1],
            device(x2, y2, 2 * zh2 + c, side),
        ).start()
        return carry

    stays = side == c
    lax.fori_loop(1, nyx * zh, send_back, 0)

    @pl.when(stays)
    def _():
        mbuf[side, home] = msend[home]
        arrived(mbuf.at[c, pl.ds(0, nyx * zh - 1)], msem.at[1])

    @pl.when(jnp.logical_not(stays))
    def _():
        send_back(0, 0)
        arrived(mbuf.at[c], msem.at[1])

    final = remote(mbuf.at[c], mbuf.at[c], fsem.at[0], fsem.at[1], sibling)
    final.start()
    final.wait_recv()

    full = mbuf[...].astype(F32)
    full = jnp.where(first, full[:, :, :ROWS], full[:, :, ROWS:])
    norm = zscore(full.reshape(cz, ROWS, width), 0)
    for p in range(2):
        for s in range(nyx):
            start = s * NZ + p * zh
            part = norm[(p * nyx + s) * zh : (p * nyx + s + 1) * zh]
            nscr[start * ROWS : (start + zh) * ROWS] = part.reshape(zh * ROWS, width)
    for i in range(ROWS):
        norm = nscr[pl.ds(i, cz, stride=ROWS), :].T.astype(BF16)
        proj = jnp.dot(norm, fp_v[...], preferred_element_type=F32)
        out_ref[i] = (upd[i] + gates[i] * proj).astype(BF16)

    arrived(lbuf.at[0, pl.ds(0, nx - 1), low], lsem.at[0])
    arrived(lbuf.at[pl.ds(0, ny - 1), 0, high], lsem.at[2])
    arrived(lbuf.at[pl.ds(0, ny - 1), :, low], lsem.at[4])
    arrived(lbuf.at[:, pl.ds(0, nx - 1), high], lsem.at[6])
    arrived(rbuf.at[0, pl.ds(0, ny * NZ - 1)], rsem.at[0])
    arrived(psend.at[pl.ds(0, nx - 1)], psem.at[0])
    cross.wait_send()
    for g in range(nx):

        @pl.when(jnp.logical_not(jnp.logical_and(x == g, y == x)))
        def _():
            arrived(usend.at[g], usend_sem.at[g])

    arrived(lrbuf.at[pl.ds(0, peers - 1)], asem.at[0])
    for swap in swaps:
        swap.wait_send()

    @pl.when(stays)
    def _():
        arrived(msend.at[pl.ds(0, nyx * zh - 1)], msem.at[0])

    @pl.when(jnp.logical_not(stays))
    def _():
        arrived(msend, msem.at[0])

    final.wait_send()


def shards(msa, pair, wl, wr, wo, *weights):
    ny = lax.axis_size("blk")
    nx = lax.axis_size("dap") // (NZ * NC)
    sd, _, cm = msa.shape
    ch, cz = wl.shape[1], wo.shape[1]
    columns = pair.shape[1]
    jr = ROWS // ny
    width = NZ * NC * ROWS
    thirds = NC * NZ * jr
    step = NZ * jr // 4 * ROWS
    peers = nx * ny * NZ
    vmem = pltpu.VMEM
    dma = pltpu.SemaphoreType.DMA
    scratch = [
        vmem((cm // 128 * sd * ROWS, 128), F32),
        vmem((ch * ROWS, sd), F32),
        vmem((ny, nx, ch * ROWS, sd), BF16),
        vmem((ny, jr * ch, sd), BF16),
        vmem((NC, ny * NZ, jr * ch, sd), BF16),
        vmem((NC * nx, step, 4 * ch * ch), BF16),
        vmem((4 * ch * ch, 4 * cz), BF16),
        vmem((ROWS, columns, cz), BF16),
        vmem((ROWS * columns, cz), F32),
        vmem((nx * thirds * ROWS, cz), F32),
        vmem((nx, thirds * ROWS, cz), BF16),
        vmem((nx, thirds * ROWS, cz), BF16),
        vmem((nx, thirds * ROWS, cz), BF16),
        vmem((ny, thirds * ROWS, cz), BF16),
        vmem((width * ROWS, cz), F32),
        vmem((ROWS, width, cz), F32),
        vmem((4 * cz, cz), BF16),
        vmem((cz * 2 * ROWS, width), F32),
        vmem((cz, 2 * ROWS, width), BF16),
        vmem((peers, 2 * ROWS, width), BF16),
        vmem((peers, 2 * ROWS, width), BF16),
        vmem((nx * NZ * ROWS, ny * nx * width), BF16),
        vmem((nx * width, ny * nx * width), BF16),
        vmem((peers // 2, 2 * ROWS, width), BF16),
        vmem((2, peers // 2, 2 * ROWS, width), BF16),
        vmem((cz * ROWS, width), F32),
        vmem((ROWS, width, cz), F32),
        vmem((sd * ROWS, cm), BF16),
        vmem((ch, cm), BF16),
        vmem((ch, cm), BF16),
        vmem((ch * ch, cz), BF16),
    ] + [vmem((cz, cz), BF16)] * 6 + [
        dma((10,)),
        dma,
        dma((8,)),
        dma((2,)),
        dma((2,)),
        dma((2,)),
        dma((nx,)),
        dma((ny,)),
        dma((2,)),
        dma((2, ny)),
        dma((2,)),
        dma((2,)),
    ]
    return pl.pallas_call(
        functools.partial(kernel, nx, ny, ny * sd),
        out_shape=jax.ShapeDtypeStruct((ROWS, width, cz), BF16),
        in_specs=[pl.BlockSpec(memory_space=pltpu.HBM)] * 11,
        out_specs=pl.BlockSpec(memory_space=pltpu.VMEM),
        scratch_shapes=scratch,
        compiler_params=pltpu.CompilerParams(
            collective_id=0, has_side_effects=True, vmem_limit_bytes=60 * 2**20
        ),
    )(msa.reshape(sd * ROWS, cm), pair, wl.T, wr.T, wo, *weights)


def solution(mesh):
    placed = (P("blk", "dap", None), P("dap", None, None)) + (P(),) * 9
    return jax.shard_map(
        shards, mesh=mesh, in_specs=placed, out_specs=P("dap", "blk", None), check_vma=False
    )
```

```python
import functools

import jax
import jax.numpy as jnp
from jax import lax
from jax.experimental import pallas as pl
from jax.experimental.pallas import tpu as pltpu
from jax.sharding import PartitionSpec as P

NZ = 8
NC = 2
ROWS = 8
EPS = 1e-5
MESH = pl.DeviceIdType.MESH
F32 = jnp.float32
BF16 = jnp.bfloat16


def nt(a, b):
    return lax.dot_general(a, b, (((1,), (1,)), ((), ())), preferred_element_type=F32)


def zscore(v, axis):
    centered = v - jnp.mean(v, axis=axis, keepdims=True)
    var = jnp.mean(centered * centered, axis=axis, keepdims=True)
    return centered * lax.rsqrt(var + EPS)


def device(x, y, z, c):
    return (x * NZ + z) * NC + c, y


def kernel(
    nx, ny, seqs,
    msa_ref, pair_ref, wl_ref, wr_ref, wo_ref, ag_ref, ap_ref, bg_ref, bp_ref, fg_ref, fp_ref,
    out_ref,
    xf, lscr, lbuf, rsend, rbuf, abuf, bd, pairv, pairf, pstage, psend, pbuf, usend, ubuf, vbuf, upd,
    wt4, lrscr, lrsend, lrbuf, lrsib, lwide, rwide, mixed, msend, mbuf, nscr, gates,
    msa_v, wl_v, wr_v, wo_v, ag_v, ap_v, bg_v, bp_v, fg_v, fp_v,
    load_sem, pair_sem, lsem, rsem, csem, psem, usend_sem, urecv_sem, asem, ssem, msem, fsem,
):
    local = (msa_v, wl_v, wr_v, wo_v, ag_v, ap_v, bg_v, bp_v, fg_v, fp_v)
    d = lax.axis_index("dap")
    y = lax.axis_index("blk")
    x, z, c = d // (NZ * NC), (d // NC) % NZ, d % NC
    sd = msa_ref.shape[0] // ROWS
    ch = wl_ref.shape[0]
    cz = wo_ref.shape[1]
    jr = ROWS // ny
    slab = 4
    njo = NZ * jr // slab
    thirds = NC * NZ * jr
    width = NZ * NC * ROWS
    nyx = ny * nx
    zh = NZ // 2
    sibling = device(x, y, z, 1 - c)
    first = c == 0

    def place(x1, y1, z1):
        return (x1 * ny + y1) * NZ + lax.rem(z1, 2) * zh + lax.div(z1, 2)

    def remote(source, target, send, recv, to):
        return pltpu.make_async_remote_copy(
            source, target, send, recv, device_id=to, device_id_type=MESH
        )

    def away(k, n):
        return lax.rem(n // 2 + jnp.where(lax.rem(k, 2) == 1, lax.div(k + 1, 2), n - lax.div(k, 2)), n)

    def arrived(part, sem):
        pltpu.make_async_copy(part, part, sem).wait()

    barrier = pltpu.get_barrier_semaphore()

    def greet(x2, y2, z2, c2):
        pl.semaphore_signal(barrier, inc=1, device_id=device(x2, y2, z2, c2), device_id_type=MESH)

    def greet_yz(k, carry):
        greet(x, lax.rem(y + lax.rem(k, ny), ny), lax.rem(z + lax.div(k, ny), NZ), c)
        return carry

    greet(x, y, z, 1 - c)
    for k in range(1, nx):
        greet(lax.rem(x + k, nx), y, z, c)
    lax.fori_loop(1, ny * NZ, greet_yz, 0)

    sources = (msa_ref, wl_ref, wr_ref, wo_ref, ag_ref, ap_ref, bg_ref, bp_ref, fg_ref, fp_ref)
    loads = [
        pltpu.make_async_copy(source, target, load_sem.at[t])
        for t, (source, target) in enumerate(zip(sources, local))
    ]
    for load in loads:
        load.start()
    pair_copy = pltpu.make_async_copy(pair_ref, pairv, pair_sem)
    pair_copy.start()
    for load in loads[:3]:
        load.wait()

    lanes = xf.shape[1]
    blocks = msa_v.shape[1] // lanes
    for h in range(blocks):
        xf[h * sd * ROWS : (h + 1) * sd * ROWS] = msa_v[:, h * lanes : (h + 1) * lanes].astype(F32)
    wlr = jnp.concatenate([wl_v[...], wr_v[...]], axis=0)
    for i in range(ROWS):
        v = jnp.concatenate(
            [xf[pl.ds(h * sd * ROWS + i, sd, stride=ROWS), :] for h in range(blocks)], axis=1
        )
        v = zscore(v, 1).astype(BF16)
        proj = nt(wlr, v)
        lscr[pl.ds(i, ch, stride=ROWS), :] = proj[:ch]
        rsend[i // jr, (i % jr) * ch : (i % jr + 1) * ch, :] = proj[ch:].astype(BF16)
    lbuf[y, x] = lscr[...].astype(BF16)
    rbuf[c, y * NZ + z] = rsend[y]

    pl.semaphore_wait(barrier, ny * NZ + nx - 1)

    half = ch * ROWS // 2
    low, high = pl.ds(0, half), pl.ds(half, half)
    xfirst = lbuf.at[y, x, low]
    yfirst = lbuf.at[y, x, high]
    for k in range(1, nx):
        remote(xfirst, xfirst, lsem.at[0], lsem.at[1], device(lax.rem(x + k, nx), y, z, c)).start()
    for k in range(1, ny):
        remote(yfirst, yfirst, lsem.at[2], lsem.at[3], device(x, lax.rem(y + k, ny), z, c)).start()

    def send_right(k, carry):
        z2 = lax.rem(z + lax.div(k, ny), NZ)
        y2 = lax.rem(y + lax.rem(k, ny), ny)
        remote(
            rsend.at[y2], rbuf.at[c, y * NZ + z], rsem.at[0], rsem.at[1], device(x, y2, z2, c)
        ).start()
        return carry

    lax.fori_loop(1, ny * NZ, send_right, 0)

    arrived(lbuf.at[0, pl.ds(0, nx - 1), low], lsem.at[1])
    ythen = lbuf.at[y, :, low]
    for k in range(1, ny):
        remote(ythen, ythen, lsem.at[4], lsem.at[5], device(x, lax.rem(y + k, ny), z, c)).start()
    arrived(lbuf.at[pl.ds(0, ny - 1), 0, high], lsem.at[3])
    xthen = lbuf.at[:, x, high]
    for k in range(1, nx):
        remote(xthen, xthen, lsem.at[6], lsem.at[7], device(lax.rem(x + k, nx), y, z, c)).start()

    pair_copy.wait()
    columns = pairv.shape[1]
    pairf[...] = pairv[...].astype(F32).reshape(ROWS * columns, cz)
    for i in range(ROWS):
        for h in range(NC):
            for r in range(jr):
                v = pairf[pl.ds(i * columns + h * ROWS + y * jr + r, nx * NZ, stride=NC * ROWS), :]
                for g in range(nx):
                    start = (g * thirds + h * NZ * jr + r) * ROWS + i
                    pstage[pl.ds(start, NZ, stride=jr * ROWS), :] = v[g * NZ : (g + 1) * NZ]
    psend[...] = pstage[...].astype(BF16).reshape(nx, thirds * ROWS, cz)
    pbuf[x] = psend[x]
    for k in range(1, nx):
        x2 = lax.rem(x + k, nx)
        remote(psend.at[x2], pbuf.at[x], psem.at[0], psem.at[1], device(x2, y, z, c)).start()

    for load in loads[3:]:
        load.wait()
    bd[...] = jnp.zeros_like(bd)
    for q in range(ch):
        w = wo_v[q * ch : (q + 1) * ch, :]
        for t in range(slab):
            bd[(q * slab + t) * ch : (q * slab + t + 1) * ch, t * cz : (t + 1) * cz] = w
    for t, ref in enumerate((ag_v, ap_v, bg_v, bp_v)):
        wt4[t * cz : (t + 1) * cz, :] = ref[...].astype(F32).T.astype(BF16)

    arrived(rbuf.at[0, pl.ds(0, ny * NZ - 1)], rsem.at[1])
    cross = remote(rbuf.at[c], rbuf.at[c], csem.at[0], csem.at[1], sibling)
    cross.start()
    arrived(lbuf.at[pl.ds(0, ny - 1), :, low], lsem.at[5])
    arrived(lbuf.at[:, pl.ds(0, nx - 1), high], lsem.at[7])

    def outer(side):
        right = rbuf[side]
        right = jnp.concatenate(
            [right[s * NZ : (s + 1) * NZ].reshape(NZ * jr * ch, sd) for s in range(ny)], axis=1
        )

        def one(g, carry):
            rows = jnp.concatenate([lbuf[s, g] for s in range(ny)], axis=1)
            prod = nt(rows, right)
            for q in range(ch):
                part = prod[q * ROWS : (q + 1) * ROWS]
                abuf[side * nx + g, :, q * slab * ch : (q + 1) * slab * ch] = jnp.concatenate(
                    [part[:, t * slab * ch : (t + 1) * slab * ch] for t in range(njo)], axis=0
                ).astype(BF16)
            return carry

        lax.fori_loop(0, nx, one, 0)

    outer(c)
    cross.wait_recv()
    outer(1 - c)
    step = njo * ROWS
    mixer = abuf[...].reshape(NC * nx * step, slab * ch * ch)
    total = jnp.dot(mixer, bd[...], preferred_element_type=F32)

    arrived(pbuf.at[pl.ds(0, nx - 1)], psem.at[1])
    for g in range(nx):
        tiles = []
        for kk in range(thirds):
            h, flat = divmod(kk, NZ * jr)
            o, t = divmod(flat, slab)
            start = (h * nx + g) * step + o * ROWS
            tiles.append(total[start : start + ROWS, t * cz : (t + 1) * cz])
        u = pbuf[g].astype(F32) + jnp.concatenate(tiles, axis=0) * (1.0 / seqs)
        u = u.astype(BF16)
        usend[g] = u
        vbuf[g * thirds * ROWS : (g + 1) * thirds * ROWS] = u.astype(F32)

    for i in range(ROWS):
        norm = zscore(vbuf[pl.ds(i, width, stride=ROWS), :], 1).astype(BF16)
        four = nt(wt4[...], norm)
        lrscr[pl.ds(i, cz, stride=2 * ROWS), :] = jax.nn.sigmoid(four[:cz]) * four[cz : 2 * cz]
        lrscr[pl.ds(ROWS + i, cz, stride=2 * ROWS), :] = (
            jax.nn.sigmoid(four[2 * cz : 3 * cz]) * four[3 * cz :]
        )
    lrsend[...] = lrscr[...].reshape(cz, 2 * ROWS, width).astype(BF16)

    own = place(x, y, z)

    turns = sorted(range(nx), key=lambda k: -min(k, nx - k))

    def send_channel(turn):
        x2 = lax.rem(x + turn, nx)

        def send(k, carry):
            z2 = lax.rem(z + away(lax.div(k, ny), NZ), NZ)
            y2 = lax.rem(y + away(lax.rem(k, ny), ny), ny)
            remote(
                lrsend.at[place(x2, y2, z2)], lrbuf.at[own], asem.at[0, turn], asem.at[1, turn],
                device(x2, y2, z2, c),
            ).start()
            return carry

        lax.fori_loop(0, ny * NZ - (turn == 0), send, 0)

    for turn in turns:
        send_channel(turn)
    lrbuf[own] = lrsend[own]

    for g in range(nx):
        here = jnp.logical_and(x == g, y == x)

        @pl.when(here)
        def _():
            ubuf[y] = usend[g]

        @pl.when(jnp.logical_not(here))
        def _():
            remote(
                usend.at[g], ubuf.at[y], usend_sem.at[g], urecv_sem.at[y], device(g, x, z, c)
            ).start()

    group = lax.broadcasted_iota(jnp.int32, (zh * NC * ROWS, width), 1) // thirds
    swaps = []
    for turn in turns:
        base = lax.rem(x + nx - turn, nx) * ny * NZ
        arrived(lrbuf.at[pl.ds(0, ny * NZ - (turn == 0))], asem.at[1, turn])
        part = pl.ds(base, ny * NZ)
        swap = remote(
            lrbuf.at[part], lrsib.at[part], ssem.at[0, turn], ssem.at[1, turn], sibling
        )
        swap.start()
        swap.wait_recv()
        swaps.append(swap)
        for s in range(ny):
            mine = lrbuf[pl.ds(base + s * NZ, NZ)].astype(F32)
            other = lrsib[pl.ds(base + s * NZ, NZ)].astype(F32)
            m0, m1 = jnp.where(first, mine, other), jnp.where(first, other, mine)
            span = slice(s * width, (s + 1) * width)
            rows = []
            for z2 in range(NZ):
                at = z2 % 2 * zh + z2 // 2
                rows += [m0[at, ROWS:], m1[at, ROWS:]]
            right = jnp.concatenate(rows, axis=0)
            for m in range(nx):
                rolled = pltpu.roll(right, m * thirds, 1) if m else right
                rwide[m * width : (m + 1) * width, span] = rolled.astype(BF16)
            rows = []
            for m in (m0, m1):
                rows.append(jnp.where(first, m[:zh, :ROWS], m[zh:, :ROWS]))
            left = jnp.concatenate(rows, axis=1).reshape(zh * NC * ROWS, width)
            for g in range(nx):
                lwide[g * zh * NC * ROWS : (g + 1) * zh * NC * ROWS, span] = jnp.where(
                    group == g, left, 0.0
                ).astype(BF16)
        if turn == turns[0]:
            mixed[...] = nt(lwide[...], rwide[...])
        else:
            mixed[...] += nt(lwide[...], rwide[...])
    for g in range(nx):
        for m in range(nx):
            g2 = (g - m) % nx
            part = mixed[g * zh * NC * ROWS : (g + 1) * zh * NC * ROWS, m * width : (m + 1) * width]
            msend[(g2 * nx + g) * zh : (g2 * nx + g + 1) * zh] = part.reshape(
                zh, NC * ROWS, width
            ).astype(BF16)

    side = lax.rem(z, 2)
    home = (x * ny + y) * zh + lax.div(z, 2)
    stays = side == c

    def send_back(turn, k):
        x2 = lax.rem(x + turn, nx)
        zh2 = lax.rem(lax.div(z, 2) + away(lax.div(k, ny), zh), zh)
        y2 = lax.rem(y + away(lax.rem(k, ny), ny), ny)
        remote(
            msend.at[(y2 * nx + x2) * zh + zh2], mbuf.at[side, home],
            msem.at[0, turn], msem.at[1, turn], device(x2, y2, 2 * zh2 + c, side),
        ).start()

    def send_group(turn, count):
        def send(k, carry):
            send_back(turn, k)
            return carry

        lax.fori_loop(0, count, send, 0)

    for turn in turns:
        send_group(turn, ny * zh - (turn == 0))

    @pl.when(stays)
    def _():
        mbuf[side, home] = msend[(y * nx + x) * zh + lax.div(z, 2)]

    @pl.when(jnp.logical_not(stays))
    def _():
        send_back(0, ny * zh - 1)

    for s in range(ny):

        @pl.when(jnp.logical_not(jnp.logical_and(x == y, y == s)))
        def _():
            arrived(ubuf.at[s], urecv_sem.at[s])

        part = ubuf[s].astype(F32)
        for kk in range(thirds):
            h, flat = divmod(kk, NZ * jr)
            j = ((flat // jr) * NC + h) * ROWS + s * jr + flat % jr
            vbuf[j * ROWS : (j + 1) * ROWS, :] = part[kk * ROWS : (kk + 1) * ROWS]
    for i in range(ROWS):
        u = vbuf[pl.ds(i, width, stride=ROWS), :]
        upd[i] = u
        norm = zscore(u, 1).astype(BF16)
        gates[i] = jax.nn.sigmoid(jnp.dot(norm, fg_v[...], preferred_element_type=F32))

    finals = []
    for turn in turns:
        base = lax.rem(x + nx - turn, nx) * ny * zh
        if turn:
            arrived(mbuf.at[c, pl.ds(0, ny * zh)], msem.at[1, turn])
        else:

            @pl.when(stays)
            def _():
                arrived(mbuf.at[c, pl.ds(0, ny * zh - 1)], msem.at[1, 0])

            @pl.when(jnp.logical_not(stays))
            def _():
                arrived(mbuf.at[c, pl.ds(0, ny * zh)], msem.at[1, 0])

        part = mbuf.at[c, pl.ds(base, ny * zh)]
        final = remote(part, part, fsem.at[0, turn], fsem.at[1, turn], sibling)
        final.start()
        finals.append(final)
    for final in finals:
        final.wait_recv()

    full = mbuf[...].astype(F32)
    full = jnp.where(first, full[:, :, :ROWS], full[:, :, ROWS:])
    norm = zscore(full.reshape(cz, ROWS, width), 0)
    for p in range(2):
        for s in range(nyx):
            start = s * NZ + p * zh
            part = norm[(p * nyx + s) * zh : (p * nyx + s + 1) * zh]
            nscr[start * ROWS : (start + zh) * ROWS] = part.reshape(zh * ROWS, width)
    for i in range(ROWS):
        norm = nscr[pl.ds(i, cz, stride=ROWS), :].T.astype(BF16)
        proj = jnp.dot(norm, fp_v[...], preferred_element_type=F32)
        out_ref[i] = (upd[i] + gates[i] * proj).astype(BF16)

    arrived(lbuf.at[0, pl.ds(0, nx - 1), low], lsem.at[0])
    arrived(lbuf.at[pl.ds(0, ny - 1), 0, high], lsem.at[2])
    arrived(lbuf.at[pl.ds(0, ny - 1), :, low], lsem.at[4])
    arrived(lbuf.at[:, pl.ds(0, nx - 1), high], lsem.at[6])
    arrived(rbuf.at[0, pl.ds(0, ny * NZ - 1)], rsem.at[0])
    arrived(psend.at[pl.ds(0, nx - 1)], psem.at[0])
    cross.wait_send()
    for g in range(nx):

        @pl.when(jnp.logical_not(jnp.logical_and(x == g, y == x)))
        def _():
            arrived(usend.at[g], usend_sem.at[g])

    for turn in turns:
        arrived(lrbuf.at[pl.ds(0, ny * NZ - (turn == 0))], asem.at[0, turn])
        if turn:
            arrived(msend.at[pl.ds(0, ny * zh)], msem.at[0, turn])

    @pl.when(stays)
    def _():
        arrived(msend.at[pl.ds(0, ny * zh - 1)], msem.at[0, 0])

    @pl.when(jnp.logical_not(stays))
    def _():
        arrived(msend.at[pl.ds(0, ny * zh)], msem.at[0, 0])

    for copy in swaps + finals:
        copy.wait_send()


def shards(msa, pair, wl, wr, wo, *weights):
    ny = lax.axis_size("blk")
    nx = lax.axis_size("dap") // (NZ * NC)
    sd, _, cm = msa.shape
    ch, cz = wl.shape[1], wo.shape[1]
    columns = pair.shape[1]
    jr = ROWS // ny
    width = NZ * NC * ROWS
    thirds = NC * NZ * jr
    step = NZ * jr // 4 * ROWS
    peers = nx * ny * NZ
    vmem = pltpu.VMEM
    dma = pltpu.SemaphoreType.DMA
    scratch = [
        vmem((cm // 128 * sd * ROWS, 128), F32),
        vmem((ch * ROWS, sd), F32),
        vmem((ny, nx, ch * ROWS, sd), BF16),
        vmem((ny, jr * ch, sd), BF16),
        vmem((NC, ny * NZ, jr * ch, sd), BF16),
        vmem((NC * nx, step, 4 * ch * ch), BF16),
        vmem((4 * ch * ch, 4 * cz), BF16),
        vmem((ROWS, columns, cz), BF16),
        vmem((ROWS * columns, cz), F32),
        vmem((nx * thirds * ROWS, cz), F32),
        vmem((nx, thirds * ROWS, cz), BF16),
        vmem((nx, thirds * ROWS, cz), BF16),
        vmem((nx, thirds * ROWS, cz), BF16),
        vmem((ny, thirds * ROWS, cz), BF16),
        vmem((width * ROWS, cz), F32),
        vmem((ROWS, width, cz), F32),
        vmem((4 * cz, cz), BF16),
        vmem((cz * 2 * ROWS, width), F32),
        vmem((cz, 2 * ROWS, width), BF16),
        vmem((peers, 2 * ROWS, width), BF16),
        vmem((peers, 2 * ROWS, width), BF16),
        vmem((nx * NZ * ROWS, ny * width), BF16),
        vmem((nx * width, ny * width), BF16),
        vmem((nx * NZ * ROWS, nx * width), F32),
        vmem((peers // 2, 2 * ROWS, width), BF16),
        vmem((2, peers // 2, 2 * ROWS, width), BF16),
        vmem((cz * ROWS, width), F32),
        vmem((ROWS, width, cz), F32),
        vmem((sd * ROWS, cm), BF16),
        vmem((ch, cm), BF16),
        vmem((ch, cm), BF16),
        vmem((ch * ch, cz), BF16),
    ] + [vmem((cz, cz), BF16)] * 6 + [
        dma((10,)),
        dma,
        dma((8,)),
        dma((2,)),
        dma((2,)),
        dma((2,)),
        dma((nx,)),
        dma((ny,)),
        dma((2, nx)),
        dma((2, nx)),
        dma((2, nx)),
        dma((2, nx)),
    ]
    return pl.pallas_call(
        functools.partial(kernel, nx, ny, ny * sd),
        out_shape=jax.ShapeDtypeStruct((ROWS, width, cz), BF16),
        in_specs=[pl.BlockSpec(memory_space=pltpu.HBM)] * 11,
        out_specs=pl.BlockSpec(memory_space=pltpu.VMEM),
        scratch_shapes=scratch,
        compiler_params=pltpu.CompilerParams(
            collective_id=0, has_side_effects=True, vmem_limit_bytes=60 * 2**20
        ),
    )(msa.reshape(sd * ROWS, cm), pair, wl.T, wr.T, wo, *weights)


def solution(mesh):
    placed = (P("blk", "dap", None), P("dap", None, None)) + (P(),) * 9
    return jax.shard_map(
        shards, mesh=mesh, in_specs=placed, out_specs=P("dap", "blk", None), check_vma=False
    )
```

```python
import functools

import jax
import jax.numpy as jnp
from jax import lax
from jax.experimental import pallas as pl
from jax.experimental.pallas import tpu as pltpu
from jax.sharding import PartitionSpec as P

NZ = 8
NC = 2
ROWS = 8
EPS = 1e-5
MESH = pl.DeviceIdType.MESH
F32 = jnp.float32
BF16 = jnp.bfloat16


def nt(a, b):
    return lax.dot_general(a, b, (((1,), (1,)), ((), ())), preferred_element_type=F32)


def zscore(v, axis):
    centered = v - jnp.mean(v, axis=axis, keepdims=True)
    var = jnp.mean(centered * centered, axis=axis, keepdims=True)
    return centered * lax.rsqrt(var + EPS)


def device(x, y, z, c):
    return (x * NZ + z) * NC + c, y


def kernel(
    nx, ny, seqs,
    msa_ref, pair_ref, wl_ref, wr_ref, wo_ref, ag_ref, ap_ref, bg_ref, bp_ref, fg_ref, fp_ref,
    out_ref,
    xf, lscr, lbuf, rsend, rbuf, abuf, bd, pairv, pairf, pstage, psend, pbuf, usend, ubuf, vbuf, upd,
    wt4, lrscr, lrsend, lrbuf, lrsib, lwide, rwide, mixed, msend, mbuf, nscr, gates,
    msa_v, wl_v, wr_v, wo_v, ag_v, ap_v, bg_v, bp_v, fg_v, fp_v,
    load_sem, pair_sem, lsem, rsem, csem, psem, usend_sem, urecv_sem, asem, ssem, msem, fsem,
):
    local = (msa_v, wl_v, wr_v, wo_v, ag_v, ap_v, bg_v, bp_v, fg_v, fp_v)
    d = lax.axis_index("dap")
    y = lax.axis_index("blk")
    x, z, c = d // (NZ * NC), (d // NC) % NZ, d % NC
    sd = msa_ref.shape[0] // ROWS
    ch = wl_ref.shape[0]
    cz = wo_ref.shape[1]
    jr = ROWS // ny
    slab = 4
    njo = NZ * jr // slab
    thirds = NC * NZ * jr
    width = NZ * NC * ROWS
    nyx = ny * nx
    zh = NZ // 2
    sibling = device(x, y, z, 1 - c)
    first = c == 0

    def place(x1, y1, z1):
        return (x1 * ny + y1) * NZ + lax.rem(z1, 2) * zh + lax.div(z1, 2)

    xs = [lax.rem(x + k, nx) for k in range(nx)]
    ys = [lax.rem(y + k, ny) for k in range(ny)]
    zs = [lax.rem(z + k, NZ) for k in range(NZ)]
    xat = [v * (NZ * NC) + c for v in xs]
    zat = [v * NC for v in zs]
    xpart = [v * (ny * NZ) for v in xs]
    ypart = [v * NZ for v in ys]
    zpart = [place(0, 0, v) for v in zs]

    def outward(n):
        return sorted(range(n), key=lambda k: -min(k, n - k))

    def remote(source, target, send, recv, to):
        return pltpu.make_async_remote_copy(
            source, target, send, recv, device_id=to, device_id_type=MESH
        )

    def away(k, n):
        return lax.rem(n // 2 + jnp.where(lax.rem(k, 2) == 1, lax.div(k + 1, 2), n - lax.div(k, 2)), n)

    def arrived(part, sem):
        pltpu.make_async_copy(part, part, sem).wait()

    barrier = pltpu.get_barrier_semaphore()

    def greet(x2, y2, z2, c2):
        pl.semaphore_signal(barrier, inc=1, device_id=device(x2, y2, z2, c2), device_id_type=MESH)

    greet(x, y, z, 1 - c)
    for k in range(1, nx):
        greet(lax.rem(x + k, nx), y, z, c)
    for kz in (0, 1, 2, NZ - 2, NZ - 1):
        for ky in range(ny):
            if kz or ky:
                greet(x, ys[ky], zs[kz], c)

    sources = (msa_ref, wl_ref, wr_ref, wo_ref, ag_ref, ap_ref, bg_ref, bp_ref, fg_ref, fp_ref)
    loads = [
        pltpu.make_async_copy(source, target, load_sem.at[t])
        for t, (source, target) in enumerate(zip(sources, local))
    ]
    for load in loads:
        load.start()
    pair_copy = pltpu.make_async_copy(pair_ref, pairv, pair_sem)
    pair_copy.start()
    for load in loads[:3]:
        load.wait()

    lanes = xf.shape[1]
    blocks = msa_v.shape[1] // lanes
    for h in range(blocks):
        xf[h * sd * ROWS : (h + 1) * sd * ROWS] = msa_v[:, h * lanes : (h + 1) * lanes].astype(F32)
    wlr = jnp.concatenate([wl_v[...], wr_v[...]], axis=0)
    for i in range(ROWS):
        v = jnp.concatenate(
            [xf[pl.ds(h * sd * ROWS + i, sd, stride=ROWS), :] for h in range(blocks)], axis=1
        )
        v = zscore(v, 1).astype(BF16)
        proj = nt(wlr, v)
        lscr[pl.ds(i, ch, stride=ROWS), :] = proj[:ch]
        rsend[i // jr, (i % jr) * ch : (i % jr + 1) * ch, :] = proj[ch:].astype(BF16)
    lbuf[y, x] = lscr[...].astype(BF16)
    rbuf[c, y, z] = rsend[y]

    pl.semaphore_wait(barrier, ny * 5 + nx - 1)

    half = ch * ROWS // 2
    low, high = pl.ds(0, half), pl.ds(half, half)
    xfirst = lbuf.at[y, x, low]
    yfirst = lbuf.at[y, x, high]
    for k in range(1, nx):
        remote(xfirst, xfirst, lsem.at[0], lsem.at[1], device(lax.rem(x + k, nx), y, z, c)).start()
    for k in range(1, ny):
        remote(yfirst, yfirst, lsem.at[2], lsem.at[3], device(x, lax.rem(y + k, ny), z, c)).start()

    for kz, at in ((2, 0), (NZ - 2, 0), (1, 2), (NZ - 1, 2), (0, 6)):
        for ky in range(ny):
            if kz or ky:
                remote(
                    rsend.at[ys[ky]], rbuf.at[c, y, z], rsem.at[at], rsem.at[at + 1],
                    (xat[0] + zat[kz], ys[ky]),
                ).start()

    arrived(lbuf.at[0, pl.ds(0, nx - 1), low], lsem.at[1])
    ythen = lbuf.at[y, :, low]
    for k in range(1, ny):
        remote(ythen, ythen, lsem.at[4], lsem.at[5], device(x, lax.rem(y + k, ny), z, c)).start()
    arrived(lbuf.at[pl.ds(0, ny - 1), 0, high], lsem.at[3])
    xthen = lbuf.at[:, x, high]
    for k in range(1, nx):
        remote(xthen, xthen, lsem.at[6], lsem.at[7], device(lax.rem(x + k, nx), y, z, c)).start()

    arrived(rbuf.at[0, :, pl.ds(0, 2)], rsem.at[1])
    early, late = pl.ds(0, ny // 2), pl.ds(ny // 2, ny // 2)
    for part, kz in (
        (rbuf.at[c, early, zs[NZ - 2]], 2),
        (rbuf.at[c, late, zs[2]], NZ - 2),
        (rbuf.at[c, :, zs[NZ - 2]], 1),
        (rbuf.at[c, :, zs[2]], NZ - 1),
    ):
        remote(part, part, rsem.at[4], rsem.at[5], (xat[0] + zat[kz], y)).start()

    pair_copy.wait()
    columns = pairv.shape[1]
    pairf[...] = pairv[...].astype(F32).reshape(ROWS * columns, cz)
    for i in range(ROWS):
        for h in range(NC):
            for r in range(jr):
                v = pairf[pl.ds(i * columns + h * ROWS + y * jr + r, nx * NZ, stride=NC * ROWS), :]
                for g in range(nx):
                    start = (g * thirds + h * NZ * jr + r) * ROWS + i
                    pstage[pl.ds(start, NZ, stride=jr * ROWS), :] = v[g * NZ : (g + 1) * NZ]
    psend[...] = pstage[...].astype(BF16).reshape(nx, thirds * ROWS, cz)
    pbuf[x] = psend[x]
    for k in range(1, nx):
        x2 = lax.rem(x + k, nx)
        remote(psend.at[x2], pbuf.at[x], psem.at[0], psem.at[1], device(x2, y, z, c)).start()

    for load in loads[3:]:
        load.wait()
    bd[...] = jnp.zeros_like(bd)
    for q in range(ch):
        w = wo_v[q * ch : (q + 1) * ch, :]
        for t in range(slab):
            bd[(q * slab + t) * ch : (q * slab + t + 1) * ch, t * cz : (t + 1) * cz] = w
    for t, ref in enumerate((ag_v, ap_v, bg_v, bp_v)):
        wt4[t * cz : (t + 1) * cz, :] = ref[...].astype(F32).T.astype(BF16)

    arrived(rbuf.at[0, :, pl.ds(0, 2)], rsem.at[3])
    arrived(rbuf.at[0, pl.ds(0, ny - 1), 0], rsem.at[7])
    arrived(rbuf.at[0, :, pl.ds(0, NZ - 5)], rsem.at[5])
    cross = remote(rbuf.at[c], rbuf.at[c], csem.at[0], csem.at[1], sibling)
    cross.start()
    arrived(lbuf.at[pl.ds(0, ny - 1), :, low], lsem.at[5])
    arrived(lbuf.at[:, pl.ds(0, nx - 1), high], lsem.at[7])

    def outer(side):
        right = rbuf[side]
        right = jnp.concatenate(
            [right[s].reshape(NZ * jr * ch, sd) for s in range(ny)], axis=1
        )

        def one(g, carry):
            rows = jnp.concatenate([lbuf[s, g] for s in range(ny)], axis=1)
            prod = nt(rows, right)
            for q in range(ch):
                part = prod[q * ROWS : (q + 1) * ROWS]
                abuf[side * nx + g, :, q * slab * ch : (q + 1) * slab * ch] = jnp.concatenate(
                    [part[:, t * slab * ch : (t + 1) * slab * ch] for t in range(njo)], axis=0
                ).astype(BF16)
            return carry

        lax.fori_loop(0, nx, one, 0)

    outer(c)
    cross.wait_recv()
    outer(1 - c)
    step = njo * ROWS
    mixer = abuf[...].reshape(NC * nx * step, slab * ch * ch)
    total = jnp.dot(mixer, bd[...], preferred_element_type=F32)

    arrived(pbuf.at[pl.ds(0, nx - 1)], psem.at[1])
    for g in range(nx):
        tiles = []
        for kk in range(thirds):
            h, flat = divmod(kk, NZ * jr)
            o, t = divmod(flat, slab)
            start = (h * nx + g) * step + o * ROWS
            tiles.append(total[start : start + ROWS, t * cz : (t + 1) * cz])
        u = pbuf[g].astype(F32) + jnp.concatenate(tiles, axis=0) * (1.0 / seqs)
        u = u.astype(BF16)
        usend[g] = u
        vbuf[g * thirds * ROWS : (g + 1) * thirds * ROWS] = u.astype(F32)

    for i in range(ROWS):
        norm = zscore(vbuf[pl.ds(i, width, stride=ROWS), :], 1).astype(BF16)
        four = nt(wt4[...], norm)
        lrscr[pl.ds(i, cz, stride=2 * ROWS), :] = jax.nn.sigmoid(four[:cz]) * four[cz : 2 * cz]
        lrscr[pl.ds(ROWS + i, cz, stride=2 * ROWS), :] = (
            jax.nn.sigmoid(four[2 * cz : 3 * cz]) * four[3 * cz :]
        )
    lrsend[...] = lrscr[...].reshape(cz, 2 * ROWS, width).astype(BF16)

    own = place(x, y, z)

    turns = outward(nx)
    for turn in turns:
        for kz in outward(NZ):
            for ky in outward(ny):
                if turn or kz or ky:
                    remote(
                        lrsend.at[xpart[turn] + ypart[ky] + zpart[kz]], lrbuf.at[own],
                        asem.at[0, turn], asem.at[1, turn], (xat[turn] + zat[kz], ys[ky]),
                    ).start()
    lrbuf[own] = lrsend[own]

    for g in range(nx):
        here = jnp.logical_and(x == g, y == x)

        @pl.when(here)
        def _():
            ubuf[y] = usend[g]

        @pl.when(jnp.logical_not(here))
        def _():
            remote(
                usend.at[g], ubuf.at[y], usend_sem.at[g], urecv_sem.at[y], device(g, x, z, c)
            ).start()

    group = lax.broadcasted_iota(jnp.int32, (zh * NC * ROWS, width), 1) // thirds
    swaps = []
    for turn in turns:
        base = lax.rem(x + nx - turn, nx) * ny * NZ
        arrived(lrbuf.at[pl.ds(0, ny * NZ - (turn == 0))], asem.at[1, turn])
        part = pl.ds(base, ny * NZ)
        swap = remote(
            lrbuf.at[part], lrsib.at[part], ssem.at[0, turn], ssem.at[1, turn], sibling
        )
        swap.start()
        swap.wait_recv()
        swaps.append(swap)
        for s in range(ny):
            mine = lrbuf[pl.ds(base + s * NZ, NZ)].astype(F32)
            other = lrsib[pl.ds(base + s * NZ, NZ)].astype(F32)
            m0, m1 = jnp.where(first, mine, other), jnp.where(first, other, mine)
            span = slice(s * width, (s + 1) * width)
            rows = []
            for z2 in range(NZ):
                at = z2 % 2 * zh + z2 // 2
                rows += [m0[at, ROWS:], m1[at, ROWS:]]
            right = jnp.concatenate(rows, axis=0)
            for m in range(nx):
                rolled = pltpu.roll(right, m * thirds, 1) if m else right
                rwide[m * width : (m + 1) * width, span] = rolled.astype(BF16)
            rows = []
            for m in (m0, m1):
                rows.append(jnp.where(first, m[:zh, :ROWS], m[zh:, :ROWS]))
            left = jnp.concatenate(rows, axis=1).reshape(zh * NC * ROWS, width)
            for g in range(nx):
                lwide[g * zh * NC * ROWS : (g + 1) * zh * NC * ROWS, span] = jnp.where(
                    group == g, left, 0.0
                ).astype(BF16)
        if turn == turns[0]:
            mixed[...] = nt(lwide[...], rwide[...])
        else:
            mixed[...] += nt(lwide[...], rwide[...])
    for g in range(nx):
        for m in range(nx):
            g2 = (g - m) % nx
            part = mixed[g * zh * NC * ROWS : (g + 1) * zh * NC * ROWS, m * width : (m + 1) * width]
            msend[(g2 * nx + g) * zh : (g2 * nx + g + 1) * zh] = part.reshape(
                zh, NC * ROWS, width
            ).astype(BF16)

    side = lax.rem(z, 2)
    home = (x * ny + y) * zh + lax.div(z, 2)
    stays = side == c

    zhs = [lax.rem(lax.div(z, 2) + k, zh) for k in range(zh)]
    xback = [v * (NZ * NC) + side for v in xs]
    zback = [v * (2 * NC) + c * NC for v in zhs]
    ypart = [v * (nx * zh) for v in ys]
    xpart = [v * zh for v in xs]

    def send_back(turn, kz, ky):
        remote(
            msend.at[ypart[ky] + xpart[turn] + zhs[kz]], mbuf.at[side, home],
            msem.at[0, turn], msem.at[1, turn], (xback[turn] + zback[kz], ys[ky]),
        ).start()

    for turn in turns:
        for kz in outward(zh):
            for ky in outward(ny):
                if turn or kz or ky:
                    send_back(turn, kz, ky)

    @pl.when(stays)
    def _():
        mbuf[side, home] = msend[(y * nx + x) * zh + lax.div(z, 2)]

    @pl.when(jnp.logical_not(stays))
    def _():
        send_back(0, 0, 0)

    for s in range(ny):

        @pl.when(jnp.logical_not(jnp.logical_and(x == y, y == s)))
        def _():
            arrived(ubuf.at[s], urecv_sem.at[s])

        part = ubuf[s].astype(F32)
        for kk in range(thirds):
            h, flat = divmod(kk, NZ * jr)
            j = ((flat // jr) * NC + h) * ROWS + s * jr + flat % jr
            vbuf[j * ROWS : (j + 1) * ROWS, :] = part[kk * ROWS : (kk + 1) * ROWS]
    for i in range(ROWS):
        u = vbuf[pl.ds(i, width, stride=ROWS), :]
        upd[i] = u
        norm = zscore(u, 1).astype(BF16)
        gates[i] = jax.nn.sigmoid(jnp.dot(norm, fg_v[...], preferred_element_type=F32))

    finals = []
    for turn in turns:
        base = lax.rem(x + nx - turn, nx) * ny * zh
        if turn:
            arrived(mbuf.at[c, pl.ds(0, ny * zh)], msem.at[1, turn])
        else:

            @pl.when(stays)
            def _():
                arrived(mbuf.at[c, pl.ds(0, ny * zh - 1)], msem.at[1, 0])

            @pl.when(jnp.logical_not(stays))
            def _():
                arrived(mbuf.at[c, pl.ds(0, ny * zh)], msem.at[1, 0])

        part = mbuf.at[c, pl.ds(base, ny * zh)]
        final = remote(part, part, fsem.at[0, turn], fsem.at[1, turn], sibling)
        final.start()
        finals.append(final)
    for final in finals:
        final.wait_recv()

    full = mbuf[...].astype(F32)
    full = jnp.where(first, full[:, :, :ROWS], full[:, :, ROWS:])
    norm = zscore(full.reshape(cz, ROWS, width), 0)
    for p in range(2):
        for s in range(nyx):
            start = s * NZ + p * zh
            part = norm[(p * nyx + s) * zh : (p * nyx + s + 1) * zh]
            nscr[start * ROWS : (start + zh) * ROWS] = part.reshape(zh * ROWS, width)
    for i in range(ROWS):
        norm = nscr[pl.ds(i, cz, stride=ROWS), :].T.astype(BF16)
        proj = jnp.dot(norm, fp_v[...], preferred_element_type=F32)
        out_ref[i] = (upd[i] + gates[i] * proj).astype(BF16)

    arrived(lbuf.at[0, pl.ds(0, nx - 1), low], lsem.at[0])
    arrived(lbuf.at[pl.ds(0, ny - 1), 0, high], lsem.at[2])
    arrived(lbuf.at[pl.ds(0, ny - 1), :, low], lsem.at[4])
    arrived(lbuf.at[:, pl.ds(0, nx - 1), high], lsem.at[6])
    arrived(rbuf.at[0, :, pl.ds(0, 2)], rsem.at[0])
    arrived(rbuf.at[0, :, pl.ds(0, 2)], rsem.at[2])
    arrived(rbuf.at[0, pl.ds(0, ny - 1), 0], rsem.at[6])
    arrived(rbuf.at[0, :, pl.ds(0, NZ - 5)], rsem.at[4])
    arrived(psend.at[pl.ds(0, nx - 1)], psem.at[0])
    cross.wait_send()
    for g in range(nx):

        @pl.when(jnp.logical_not(jnp.logical_and(x == g, y == x)))
        def _():
            arrived(usend.at[g], usend_sem.at[g])

    for turn in turns:
        arrived(lrbuf.at[pl.ds(0, ny * NZ - (turn == 0))], asem.at[0, turn])
        if turn:
            arrived(msend.at[pl.ds(0, ny * zh)], msem.at[0, turn])

    @pl.when(stays)
    def _():
        arrived(msend.at[pl.ds(0, ny * zh - 1)], msem.at[0, 0])

    @pl.when(jnp.logical_not(stays))
    def _():
        arrived(msend.at[pl.ds(0, ny * zh)], msem.at[0, 0])

    for copy in swaps + finals:
        copy.wait_send()


def shards(msa, pair, wl, wr, wo, *weights):
    ny = lax.axis_size("blk")
    nx = lax.axis_size("dap") // (NZ * NC)
    sd, _, cm = msa.shape
    ch, cz = wl.shape[1], wo.shape[1]
    columns = pair.shape[1]
    jr = ROWS // ny
    width = NZ * NC * ROWS
    thirds = NC * NZ * jr
    step = NZ * jr // 4 * ROWS
    peers = nx * ny * NZ
    vmem = pltpu.VMEM
    dma = pltpu.SemaphoreType.DMA
    scratch = [
        vmem((cm // 128 * sd * ROWS, 128), F32),
        vmem((ch * ROWS, sd), F32),
        vmem((ny, nx, ch * ROWS, sd), BF16),
        vmem((ny, jr * ch, sd), BF16),
        vmem((NC, ny, NZ, jr * ch, sd), BF16),
        vmem((NC * nx, step, 4 * ch * ch), BF16),
        vmem((4 * ch * ch, 4 * cz), BF16),
        vmem((ROWS, columns, cz), BF16),
        vmem((ROWS * columns, cz), F32),
        vmem((nx * thirds * ROWS, cz), F32),
        vmem((nx, thirds * ROWS, cz), BF16),
        vmem((nx, thirds * ROWS, cz), BF16),
        vmem((nx, thirds * ROWS, cz), BF16),
        vmem((ny, thirds * ROWS, cz), BF16),
        vmem((width * ROWS, cz), F32),
        vmem((ROWS, width, cz), F32),
        vmem((4 * cz, cz), BF16),
        vmem((cz * 2 * ROWS, width), F32),
        vmem((cz, 2 * ROWS, width), BF16),
        vmem((peers, 2 * ROWS, width), BF16),
        vmem((peers, 2 * ROWS, width), BF16),
        vmem((nx * NZ * ROWS, ny * width), BF16),
        vmem((nx * width, ny * width), BF16),
        vmem((nx * NZ * ROWS, nx * width), F32),
        vmem((peers // 2, 2 * ROWS, width), BF16),
        vmem((2, peers // 2, 2 * ROWS, width), BF16),
        vmem((cz * ROWS, width), F32),
        vmem((ROWS, width, cz), F32),
        vmem((sd * ROWS, cm), BF16),
        vmem((ch, cm), BF16),
        vmem((ch, cm), BF16),
        vmem((ch * ch, cz), BF16),
    ] + [vmem((cz, cz), BF16)] * 6 + [
        dma((10,)),
        dma,
        dma((10,)),
        dma((8,)),
        dma((2,)),
        dma((2,)),
        dma((nx,)),
        dma((ny,)),
        dma((2, nx)),
        dma((2, nx)),
        dma((2, nx)),
        dma((2, nx)),
    ]
    return pl.pallas_call(
        functools.partial(kernel, nx, ny, ny * sd),
        out_shape=jax.ShapeDtypeStruct((ROWS, width, cz), BF16),
        in_specs=[pl.BlockSpec(memory_space=pltpu.HBM)] * 11,
        out_specs=pl.BlockSpec(memory_space=pltpu.VMEM),
        scratch_shapes=scratch,
        compiler_params=pltpu.CompilerParams(
            collective_id=0, has_side_effects=True, vmem_limit_bytes=60 * 2**20
        ),
    )(msa.reshape(sd * ROWS, cm), pair, wl.T, wr.T, wo, *weights)


def solution(mesh):
    placed = (P("blk", "dap", None), P("dap", None, None)) + (P(),) * 9
    return jax.shard_map(
        shards, mesh=mesh, in_specs=placed, out_specs=P("dap", "blk", None), check_vma=False
    )
```

```python
import functools

import jax
import jax.numpy as jnp
from jax import lax
from jax.experimental import pallas as pl
from jax.experimental.pallas import tpu as pltpu
from jax.sharding import PartitionSpec as P

NZ = 8
NC = 2
ROWS = 8
EPS = 1e-5
MESH = pl.DeviceIdType.MESH
F32 = jnp.float32
BF16 = jnp.bfloat16


def nt(a, b):
    return lax.dot_general(a, b, (((1,), (1,)), ((), ())), preferred_element_type=F32)


def zscore(v, axis):
    centered = v - jnp.mean(v, axis=axis, keepdims=True)
    var = jnp.mean(centered * centered, axis=axis, keepdims=True)
    return centered * lax.rsqrt(var + EPS)


def device(x, y, z, c):
    return (x * NZ + z) * NC + c, y


def kernel(
    nx, ny, seqs,
    msa_ref, pair_ref, wl_ref, wr_ref, wo_ref, ag_ref, ap_ref, bg_ref, bp_ref, fg_ref, fp_ref,
    out_ref,
    xf, lscr, lbuf, rsend, rbuf, abuf, bd, pairv, pairf, pstage, psend, pbuf, usend, ubuf, vbuf, upd,
    wt4, norm, lrscr, lrsend, lrbuf, lrsib, lwide, rwide, mixed, msend, mbuf, nscr, gates,
    msa_v, wl_v, wr_v, wo_v, ag_v, ap_v, bg_v, bp_v, fg_v, fp_v,
    load_sem, pair_sem, lsem, rsem, csem, psem, usend_sem, urecv_sem, asem, ssem, msem, fsem,
):
    local = (msa_v, wl_v, wr_v, wo_v, ag_v, ap_v, bg_v, bp_v, fg_v, fp_v)
    d = lax.axis_index("dap")
    y = lax.axis_index("blk")
    x, z, c = d // (NZ * NC), (d // NC) % NZ, d % NC
    sd = msa_ref.shape[0] // ROWS
    ch = wl_ref.shape[0]
    cz = wo_ref.shape[1]
    jr = ROWS // ny
    slab = 4
    njo = NZ * jr // slab
    thirds = NC * NZ * jr
    width = NZ * NC * ROWS
    nyx = ny * nx
    zh = NZ // 2
    sibling = device(x, y, z, 1 - c)
    first = c == 0

    def place(x1, y1, z1):
        return (x1 * ny + y1) * NZ + lax.rem(z1, 2) * zh + lax.div(z1, 2)

    xs = [lax.rem(x + k, nx) for k in range(nx)]
    ys = [lax.rem(y + k, ny) for k in range(ny)]
    zs = [lax.rem(z + k, NZ) for k in range(NZ)]
    xat = [v * (NZ * NC) + c for v in xs]
    zat = [v * NC for v in zs]
    xpart = [v * (ny * NZ) for v in xs]
    ypart = [v * NZ for v in ys]
    zpart = [place(0, 0, v) for v in zs]

    def outward(n):
        return sorted(range(n), key=lambda k: -min(k, n - k))

    def remote(source, target, send, recv, to):
        return pltpu.make_async_remote_copy(
            source, target, send, recv, device_id=to, device_id_type=MESH
        )

    def away(k, n):
        return lax.rem(n // 2 + jnp.where(lax.rem(k, 2) == 1, lax.div(k + 1, 2), n - lax.div(k, 2)), n)

    def arrived(part, sem):
        pltpu.make_async_copy(part, part, sem).wait()

    barrier = pltpu.get_barrier_semaphore()

    def greet(x2, y2, z2, c2):
        pl.semaphore_signal(barrier, inc=1, device_id=device(x2, y2, z2, c2), device_id_type=MESH)

    greet(x, y, z, 1 - c)
    for k in range(1, nx):
        greet(lax.rem(x + k, nx), y, z, c)
    for kz in (0, 1, 2, NZ - 2, NZ - 1):
        for ky in range(ny):
            if kz or ky:
                greet(x, ys[ky], zs[kz], c)

    sources = (msa_ref, wl_ref, wr_ref, wo_ref, ag_ref, ap_ref, bg_ref, bp_ref, fg_ref, fp_ref)
    loads = [
        pltpu.make_async_copy(source, target, load_sem.at[t])
        for t, (source, target) in enumerate(zip(sources, local))
    ]
    for load in loads:
        load.start()
    pair_copy = pltpu.make_async_copy(pair_ref, pairv, pair_sem)
    pair_copy.start()
    for load in loads[:3]:
        load.wait()

    lanes = xf.shape[1]
    blocks = msa_v.shape[1] // lanes
    for h in range(blocks):
        xf[h * sd * ROWS : (h + 1) * sd * ROWS] = msa_v[:, h * lanes : (h + 1) * lanes].astype(F32)
    wlr = jnp.concatenate([wl_v[...], wr_v[...]], axis=0)
    for i in range(ROWS):
        v = jnp.concatenate(
            [xf[pl.ds(h * sd * ROWS + i, sd, stride=ROWS), :] for h in range(blocks)], axis=1
        )
        v = zscore(v, 1).astype(BF16)
        proj = nt(wlr, v)
        lscr[pl.ds(i, ch, stride=ROWS), :] = proj[:ch]
        rsend[i // jr, (i % jr) * ch : (i % jr + 1) * ch, :] = proj[ch:].astype(BF16)
    lbuf[y, x] = lscr[...].astype(BF16)
    rbuf[c, y, z] = rsend[y]

    pl.semaphore_wait(barrier, ny * 5 + nx - 1)

    half = ch * ROWS // 2
    low, high = pl.ds(0, half), pl.ds(half, half)
    xfirst = lbuf.at[y, x, low]
    yfirst = lbuf.at[y, x, high]
    for k in range(1, nx):
        remote(xfirst, xfirst, lsem.at[0], lsem.at[1], device(lax.rem(x + k, nx), y, z, c)).start()
    for k in range(1, ny):
        remote(yfirst, yfirst, lsem.at[2], lsem.at[3], device(x, lax.rem(y + k, ny), z, c)).start()

    for kz, at in ((2, 0), (NZ - 2, 0), (1, 2), (NZ - 1, 2), (0, 6)):
        for ky in range(ny):
            if kz or ky:
                remote(
                    rsend.at[ys[ky]], rbuf.at[c, y, z], rsem.at[at], rsem.at[at + 1],
                    (xat[0] + zat[kz], ys[ky]),
                ).start()

    arrived(lbuf.at[0, pl.ds(0, nx - 1), low], lsem.at[1])
    ythen = lbuf.at[y, :, low]
    for k in range(1, ny):
        remote(ythen, ythen, lsem.at[4], lsem.at[5], device(x, lax.rem(y + k, ny), z, c)).start()
    arrived(lbuf.at[pl.ds(0, ny - 1), 0, high], lsem.at[3])
    xthen = lbuf.at[:, x, high]
    for k in range(1, nx):
        remote(xthen, xthen, lsem.at[6], lsem.at[7], device(lax.rem(x + k, nx), y, z, c)).start()

    arrived(rbuf.at[0, :, pl.ds(0, 2)], rsem.at[1])
    early, late = pl.ds(0, ny // 2), pl.ds(ny // 2, ny // 2)
    for part, kz in (
        (rbuf.at[c, early, zs[NZ - 2]], 2),
        (rbuf.at[c, late, zs[2]], NZ - 2),
        (rbuf.at[c, :, zs[NZ - 2]], 1),
        (rbuf.at[c, :, zs[2]], NZ - 1),
    ):
        remote(part, part, rsem.at[4], rsem.at[5], (xat[0] + zat[kz], y)).start()

    pair_copy.wait()
    columns = pairv.shape[1]
    pairf[...] = pairv[...].astype(F32).reshape(ROWS * columns, cz)
    for i in range(ROWS):
        for h in range(NC):
            for r in range(jr):
                v = pairf[pl.ds(i * columns + h * ROWS + y * jr + r, nx * NZ, stride=NC * ROWS), :]
                for g in range(nx):
                    start = (g * thirds + h * NZ * jr + r) * ROWS + i
                    pstage[pl.ds(start, NZ, stride=jr * ROWS), :] = v[g * NZ : (g + 1) * NZ]
    psend[...] = pstage[...].astype(BF16).reshape(nx, thirds * ROWS, cz)
    pbuf[x] = psend[x]
    for k in range(1, nx):
        x2 = lax.rem(x + k, nx)
        remote(psend.at[x2], pbuf.at[x], psem.at[0], psem.at[1], device(x2, y, z, c)).start()

    for load in loads[3:]:
        load.wait()
    bd[...] = jnp.zeros_like(bd)
    for q in range(ch):
        w = wo_v[q * ch : (q + 1) * ch, :]
        for t in range(slab):
            bd[(q * slab + t) * ch : (q * slab + t + 1) * ch, t * cz : (t + 1) * cz] = w
    for t, ref in enumerate((ag_v, ap_v, bg_v, bp_v)):
        wt4[t * cz : (t + 1) * cz, :] = ref[...].astype(F32).T.astype(BF16)

    arrived(rbuf.at[0, :, pl.ds(0, 2)], rsem.at[3])
    arrived(rbuf.at[0, pl.ds(0, ny - 1), 0], rsem.at[7])
    arrived(rbuf.at[0, :, pl.ds(0, NZ - 5)], rsem.at[5])
    cross = remote(rbuf.at[c], rbuf.at[c], csem.at[0], csem.at[1], sibling)
    cross.start()
    arrived(lbuf.at[pl.ds(0, ny - 1), :, low], lsem.at[5])
    arrived(lbuf.at[:, pl.ds(0, nx - 1), high], lsem.at[7])

    def outer(side):
        right = rbuf[side]
        right = jnp.concatenate(
            [right[s].reshape(NZ * jr * ch, sd) for s in range(ny)], axis=1
        )

        def one(g, carry):
            rows = jnp.concatenate([lbuf[s, g] for s in range(ny)], axis=1)
            prod = nt(rows, right)
            for q in range(ch):
                part = prod[q * ROWS : (q + 1) * ROWS]
                abuf[side * nx + g, :, q * slab * ch : (q + 1) * slab * ch] = jnp.concatenate(
                    [part[:, t * slab * ch : (t + 1) * slab * ch] for t in range(njo)], axis=0
                ).astype(BF16)
            return carry

        lax.fori_loop(0, nx, one, 0)

    outer(c)
    cross.wait_recv()
    outer(1 - c)
    step = njo * ROWS
    mixer = abuf[...].reshape(NC * nx * step, slab * ch * ch)
    total = jnp.dot(mixer, bd[...], preferred_element_type=F32)

    arrived(pbuf.at[pl.ds(0, nx - 1)], psem.at[1])
    for g in range(nx):
        tiles = []
        for kk in range(thirds):
            h, flat = divmod(kk, NZ * jr)
            o, t = divmod(flat, slab)
            start = (h * nx + g) * step + o * ROWS
            tiles.append(total[start : start + ROWS, t * cz : (t + 1) * cz])
        u = pbuf[g].astype(F32) + jnp.concatenate(tiles, axis=0) * (1.0 / seqs)
        u = u.astype(BF16)
        usend[g] = u
        vbuf[g * thirds * ROWS : (g + 1) * thirds * ROWS] = u.astype(F32)

    for i in range(ROWS):
        norm[i * width : (i + 1) * width] = zscore(
            vbuf[pl.ds(i, width, stride=ROWS), :], 1
        ).astype(BF16)
    own = place(x, y, z)
    turns = outward(nx)
    some = ny * NZ
    for turn in turns:
        weights = jnp.concatenate(
            [wt4[pl.ds(pl.multiple_of(t * cz + xpart[turn], some), some)] for t in range(4)], axis=0
        )
        four = nt(weights, norm[...])
        lhs = jax.nn.sigmoid(four[:some]) * four[some : 2 * some]
        rhs = jax.nn.sigmoid(four[2 * some : 3 * some]) * four[3 * some :]
        for i in range(ROWS):
            span = slice(i * width, (i + 1) * width)
            lrscr[pl.ds(i, some, stride=2 * ROWS), :] = lhs[:, span]
            lrscr[pl.ds(ROWS + i, some, stride=2 * ROWS), :] = rhs[:, span]
        lrsend[pl.ds(xpart[turn], some)] = lrscr[...].reshape(some, 2 * ROWS, width).astype(BF16)
        for kz in outward(NZ):
            for ky in outward(ny):
                if turn or kz or ky:
                    remote(
                        lrsend.at[xpart[turn] + ypart[ky] + zpart[kz]], lrbuf.at[own],
                        asem.at[0, turn], asem.at[1, turn], (xat[turn] + zat[kz], ys[ky]),
                    ).start()
    lrbuf[own] = lrsend[own]

    for g in range(nx):
        here = jnp.logical_and(x == g, y == x)

        @pl.when(here)
        def _():
            ubuf[y] = usend[g]

        @pl.when(jnp.logical_not(here))
        def _():
            remote(
                usend.at[g], ubuf.at[y], usend_sem.at[g], urecv_sem.at[y], device(g, x, z, c)
            ).start()

    group = lax.broadcasted_iota(jnp.int32, (zh * NC * ROWS, width), 1) // thirds
    swaps = []
    for turn in turns:
        base = lax.rem(x + nx - turn, nx) * ny * NZ
        arrived(lrbuf.at[pl.ds(0, ny * NZ - (turn == 0))], asem.at[1, turn])
        part = pl.ds(base, ny * NZ)
        swap = remote(
            lrbuf.at[part], lrsib.at[part], ssem.at[0, turn], ssem.at[1, turn], sibling
        )
        swap.start()
        swap.wait_recv()
        swaps.append(swap)
        for s in range(ny):
            mine = lrbuf[pl.ds(base + s * NZ, NZ)].astype(F32)
            other = lrsib[pl.ds(base + s * NZ, NZ)].astype(F32)
            m0, m1 = jnp.where(first, mine, other), jnp.where(first, other, mine)
            span = slice(s * width, (s + 1) * width)
            rows = []
            for z2 in range(NZ):
                at = z2 % 2 * zh + z2 // 2
                rows += [m0[at, ROWS:], m1[at, ROWS:]]
            right = jnp.concatenate(rows, axis=0)
            for m in range(nx):
                rolled = pltpu.roll(right, m * thirds, 1) if m else right
                rwide[m * width : (m + 1) * width, span] = rolled.astype(BF16)
            rows = []
            for m in (m0, m1):
                rows.append(jnp.where(first, m[:zh, :ROWS], m[zh:, :ROWS]))
            left = jnp.concatenate(rows, axis=1).reshape(zh * NC * ROWS, width)
            for g in range(nx):
                lwide[g * zh * NC * ROWS : (g + 1) * zh * NC * ROWS, span] = jnp.where(
                    group == g, left, 0.0
                ).astype(BF16)
        if turn == turns[0]:
            mixed[...] = nt(lwide[...], rwide[...])
        else:
            mixed[...] += nt(lwide[...], rwide[...])
    for g in range(nx):
        for m in range(nx):
            g2 = (g - m) % nx
            part = mixed[g * zh * NC * ROWS : (g + 1) * zh * NC * ROWS, m * width : (m + 1) * width]
            msend[(g2 * nx + g) * zh : (g2 * nx + g + 1) * zh] = part.reshape(
                zh, NC * ROWS, width
            ).astype(BF16)

    side = lax.rem(z, 2)
    home = (x * ny + y) * zh + lax.div(z, 2)
    stays = side == c

    zhs = [lax.rem(lax.div(z, 2) + k, zh) for k in range(zh)]
    xback = [v * (NZ * NC) + side for v in xs]
    zback = [v * (2 * NC) + c * NC for v in zhs]
    ypart = [v * (nx * zh) for v in ys]
    xpart = [v * zh for v in xs]

    def send_back(turn, kz, ky):
        remote(
            msend.at[ypart[ky] + xpart[turn] + zhs[kz]], mbuf.at[side, home],
            msem.at[0, turn], msem.at[1, turn], (xback[turn] + zback[kz], ys[ky]),
        ).start()

    for turn in turns:
        for kz in outward(zh):
            for ky in outward(ny):
                if turn or kz or ky:
                    send_back(turn, kz, ky)

    @pl.when(stays)
    def _():
        mbuf[side, home] = msend[(y * nx + x) * zh + lax.div(z, 2)]

    @pl.when(jnp.logical_not(stays))
    def _():
        send_back(0, 0, 0)

    for s in range(ny):

        @pl.when(jnp.logical_not(jnp.logical_and(x == y, y == s)))
        def _():
            arrived(ubuf.at[s], urecv_sem.at[s])

        part = ubuf[s].astype(F32)
        for kk in range(thirds):
            h, flat = divmod(kk, NZ * jr)
            j = ((flat // jr) * NC + h) * ROWS + s * jr + flat % jr
            vbuf[j * ROWS : (j + 1) * ROWS, :] = part[kk * ROWS : (kk + 1) * ROWS]
    for i in range(ROWS):
        u = vbuf[pl.ds(i, width, stride=ROWS), :]
        upd[i] = u
        unit = zscore(u, 1).astype(BF16)
        gates[i] = jax.nn.sigmoid(jnp.dot(unit, fg_v[...], preferred_element_type=F32))

    finals = []
    for turn in turns:
        base = lax.rem(x + nx - turn, nx) * ny * zh
        if turn:
            arrived(mbuf.at[c, pl.ds(0, ny * zh)], msem.at[1, turn])
        else:

            @pl.when(stays)
            def _():
                arrived(mbuf.at[c, pl.ds(0, ny * zh - 1)], msem.at[1, 0])

            @pl.when(jnp.logical_not(stays))
            def _():
                arrived(mbuf.at[c, pl.ds(0, ny * zh)], msem.at[1, 0])

        part = mbuf.at[c, pl.ds(base, ny * zh)]
        final = remote(part, part, fsem.at[0, turn], fsem.at[1, turn], sibling)
        final.start()
        finals.append(final)
    for final in finals:
        final.wait_recv()

    full = mbuf[...].astype(F32)
    full = jnp.where(first, full[:, :, :ROWS], full[:, :, ROWS:])
    unit = zscore(full.reshape(cz, ROWS, width), 0)
    for p in range(2):
        for s in range(nyx):
            start = s * NZ + p * zh
            part = unit[(p * nyx + s) * zh : (p * nyx + s + 1) * zh]
            nscr[start * ROWS : (start + zh) * ROWS] = part.reshape(zh * ROWS, width)
    for i in range(ROWS):
        unit = nscr[pl.ds(i, cz, stride=ROWS), :].T.astype(BF16)
        proj = jnp.dot(unit, fp_v[...], preferred_element_type=F32)
        out_ref[i] = (upd[i] + gates[i] * proj).astype(BF16)

    arrived(lbuf.at[0, pl.ds(0, nx - 1), low], lsem.at[0])
    arrived(lbuf.at[pl.ds(0, ny - 1), 0, high], lsem.at[2])
    arrived(lbuf.at[pl.ds(0, ny - 1), :, low], lsem.at[4])
    arrived(lbuf.at[:, pl.ds(0, nx - 1), high], lsem.at[6])
    arrived(rbuf.at[0, :, pl.ds(0, 2)], rsem.at[0])
    arrived(rbuf.at[0, :, pl.ds(0, 2)], rsem.at[2])
    arrived(rbuf.at[0, pl.ds(0, ny - 1), 0], rsem.at[6])
    arrived(rbuf.at[0, :, pl.ds(0, NZ - 5)], rsem.at[4])
    arrived(psend.at[pl.ds(0, nx - 1)], psem.at[0])
    cross.wait_send()
    for g in range(nx):

        @pl.when(jnp.logical_not(jnp.logical_and(x == g, y == x)))
        def _():
            arrived(usend.at[g], usend_sem.at[g])

    for turn in turns:
        arrived(lrbuf.at[pl.ds(0, ny * NZ - (turn == 0))], asem.at[0, turn])
        if turn:
            arrived(msend.at[pl.ds(0, ny * zh)], msem.at[0, turn])

    @pl.when(stays)
    def _():
        arrived(msend.at[pl.ds(0, ny * zh - 1)], msem.at[0, 0])

    @pl.when(jnp.logical_not(stays))
    def _():
        arrived(msend.at[pl.ds(0, ny * zh)], msem.at[0, 0])

    for copy in swaps + finals:
        copy.wait_send()


def shards(msa, pair, wl, wr, wo, *weights):
    ny = lax.axis_size("blk")
    nx = lax.axis_size("dap") // (NZ * NC)
    sd, _, cm = msa.shape
    ch, cz = wl.shape[1], wo.shape[1]
    columns = pair.shape[1]
    jr = ROWS // ny
    width = NZ * NC * ROWS
    thirds = NC * NZ * jr
    step = NZ * jr // 4 * ROWS
    peers = nx * ny * NZ
    vmem = pltpu.VMEM
    dma = pltpu.SemaphoreType.DMA
    scratch = [
        vmem((cm // 128 * sd * ROWS, 128), F32),
        vmem((ch * ROWS, sd), F32),
        vmem((ny, nx, ch * ROWS, sd), BF16),
        vmem((ny, jr * ch, sd), BF16),
        vmem((NC, ny, NZ, jr * ch, sd), BF16),
        vmem((NC * nx, step, 4 * ch * ch), BF16),
        vmem((4 * ch * ch, 4 * cz), BF16),
        vmem((ROWS, columns, cz), BF16),
        vmem((ROWS * columns, cz), F32),
        vmem((nx * thirds * ROWS, cz), F32),
        vmem((nx, thirds * ROWS, cz), BF16),
        vmem((nx, thirds * ROWS, cz), BF16),
        vmem((nx, thirds * ROWS, cz), BF16),
        vmem((ny, thirds * ROWS, cz), BF16),
        vmem((width * ROWS, cz), F32),
        vmem((ROWS, width, cz), F32),
        vmem((4 * cz, cz), BF16),
        vmem((ROWS * width, cz), BF16),
        vmem((ny * NZ * 2 * ROWS, width), F32),
        vmem((cz, 2 * ROWS, width), BF16),
        vmem((peers, 2 * ROWS, width), BF16),
        vmem((peers, 2 * ROWS, width), BF16),
        vmem((nx * NZ * ROWS, ny * width), BF16),
        vmem((nx * width, ny * width), BF16),
        vmem((nx * NZ * ROWS, nx * width), F32),
        vmem((peers // 2, 2 * ROWS, width), BF16),
        vmem((2, peers // 2, 2 * ROWS, width), BF16),
        vmem((cz * ROWS, width), F32),
        vmem((ROWS, width, cz), F32),
        vmem((sd * ROWS, cm), BF16),
        vmem((ch, cm), BF16),
        vmem((ch, cm), BF16),
        vmem((ch * ch, cz), BF16),
    ] + [vmem((cz, cz), BF16)] * 6 + [
        dma((10,)),
        dma,
        dma((10,)),
        dma((8,)),
        dma((2,)),
        dma((2,)),
        dma((nx,)),
        dma((ny,)),
        dma((2, nx)),
        dma((2, nx)),
        dma((2, nx)),
        dma((2, nx)),
    ]
    return pl.pallas_call(
        functools.partial(kernel, nx, ny, ny * sd),
        out_shape=jax.ShapeDtypeStruct((ROWS, width, cz), BF16),
        in_specs=[pl.BlockSpec(memory_space=pltpu.HBM)] * 11,
        out_specs=pl.BlockSpec(memory_space=pltpu.VMEM),
        scratch_shapes=scratch,
        compiler_params=pltpu.CompilerParams(
            collective_id=0, has_side_effects=True, vmem_limit_bytes=60 * 2**20
        ),
    )(msa.reshape(sd * ROWS, cm), pair, wl.T, wr.T, wo, *weights)


def solution(mesh):
    placed = (P("blk", "dap", None), P("dap", None, None)) + (P(),) * 9
    return jax.shard_map(
        shards, mesh=mesh, in_specs=placed, out_specs=P("dap", "blk", None), check_vma=False
    )
```

```python
import functools

import jax
import jax.numpy as jnp
from jax import lax
from jax.experimental import pallas as pl
from jax.experimental.pallas import tpu as pltpu
from jax.sharding import PartitionSpec as P

NZ = 8
NC = 2
ROWS = 8
EPS = 1e-5
MESH = pl.DeviceIdType.MESH
F32 = jnp.float32
BF16 = jnp.bfloat16


def nt(a, b):
    return lax.dot_general(a, b, (((1,), (1,)), ((), ())), preferred_element_type=F32)


def zscore(v, axis):
    centered = v - jnp.mean(v, axis=axis, keepdims=True)
    var = jnp.mean(centered * centered, axis=axis, keepdims=True)
    return centered * lax.rsqrt(var + EPS)


def device(x, y, z, c):
    return (x * NZ + z) * NC + c, y


def kernel(
    nx, ny, seqs,
    msa_ref, pair_ref, wl_ref, wr_ref, wo_ref, ag_ref, ap_ref, bg_ref, bp_ref, fg_ref, fp_ref,
    out_ref,
    xf, lscr, lbuf, rsend, rbuf, abuf, bd, pairv, pairf, pstage, psend, pbuf, usend, ubuf, vbuf, upd,
    wt4, norm, lrscr, lrsend, lrbuf, lrsib, lwide, rwide, mixed, msend, mbuf, nscr, gates,
    msa_v, wl_v, wr_v, wo_v, ag_v, ap_v, bg_v, bp_v, fg_v, fp_v,
    load_sem, pair_sem, lsem, rsem, csem, psem, usend_sem, urecv_sem, asem, ssem, msem, fsem,
):
    local = (msa_v, wl_v, wr_v, wo_v, ag_v, ap_v, bg_v, bp_v, fg_v, fp_v)
    d = lax.axis_index("dap")
    y = lax.axis_index("blk")
    x, z, c = d // (NZ * NC), (d // NC) % NZ, d % NC
    sd = msa_ref.shape[0] // ROWS
    ch = wl_ref.shape[0]
    cz = wo_ref.shape[1]
    jr = ROWS // ny
    slab = 4
    njo = NZ * jr // slab
    thirds = NC * NZ * jr
    width = NZ * NC * ROWS
    nyx = ny * nx
    zh = NZ // 2
    sibling = device(x, y, z, 1 - c)
    first = c == 0

    def place(x1, y1, z1):
        return (x1 * ny + y1) * NZ + lax.rem(z1, 2) * zh + lax.div(z1, 2)

    xs = [lax.rem(x + k, nx) for k in range(nx)]
    ys = [lax.rem(y + k, ny) for k in range(ny)]
    zs = [lax.rem(z + k, NZ) for k in range(NZ)]
    xat = [v * (NZ * NC) + c for v in xs]
    zat = [v * NC for v in zs]
    xpart = [v * (ny * NZ) for v in xs]
    ypart = [v * NZ for v in ys]
    zpart = [place(0, 0, v) for v in zs]

    def outward(n):
        return sorted(range(n), key=lambda k: -min(k, n - k))

    def remote(source, target, send, recv, to):
        return pltpu.make_async_remote_copy(
            source, target, send, recv, device_id=to, device_id_type=MESH
        )

    def away(k, n):
        return lax.rem(n // 2 + jnp.where(lax.rem(k, 2) == 1, lax.div(k + 1, 2), n - lax.div(k, 2)), n)

    def arrived(part, sem):
        pltpu.make_async_copy(part, part, sem).wait()

    barrier = pltpu.get_barrier_semaphore()

    def greet(x2, y2, z2, c2):
        pl.semaphore_signal(barrier, inc=1, device_id=device(x2, y2, z2, c2), device_id_type=MESH)

    greet(x, y, z, 1 - c)
    for k in range(1, nx):
        greet(lax.rem(x + k, nx), y, z, c)
    for kz in (0, 1, 2, NZ - 2, NZ - 1):
        for ky in range(ny):
            if kz or ky:
                greet(x, ys[ky], zs[kz], c)

    sources = (msa_ref, wl_ref, wr_ref, wo_ref, ag_ref, ap_ref, bg_ref, bp_ref, fg_ref, fp_ref)
    loads = [
        pltpu.make_async_copy(source, target, load_sem.at[t])
        for t, (source, target) in enumerate(zip(sources, local))
    ]
    for load in loads:
        load.start()
    pair_copy = pltpu.make_async_copy(pair_ref, pairv, pair_sem)
    pair_copy.start()
    for load in loads[:3]:
        load.wait()

    lanes = xf.shape[1]
    blocks = msa_v.shape[1] // lanes
    for h in range(blocks):
        xf[h * sd * ROWS : (h + 1) * sd * ROWS] = msa_v[:, h * lanes : (h + 1) * lanes].astype(F32)
    wlr = jnp.concatenate([wl_v[...], wr_v[...]], axis=0)
    for i in range(ROWS):
        v = jnp.concatenate(
            [xf[pl.ds(h * sd * ROWS + i, sd, stride=ROWS), :] for h in range(blocks)], axis=1
        )
        v = zscore(v, 1).astype(BF16)
        proj = nt(wlr, v)
        lscr[pl.ds(i, ch, stride=ROWS), :] = proj[:ch]
        rsend[i // jr, (i % jr) * ch : (i % jr + 1) * ch, :] = proj[ch:].astype(BF16)
    lbuf[y, x] = lscr[...].astype(BF16)
    rbuf[c, y, z] = rsend[y]

    pl.semaphore_wait(barrier, ny * 5 + nx - 1)

    half = ch * ROWS // 2
    low, high = pl.ds(0, half), pl.ds(half, half)
    xfirst = lbuf.at[y, x, low]
    yfirst = lbuf.at[y, x, high]
    for k in range(1, nx):
        remote(xfirst, xfirst, lsem.at[0], lsem.at[1], device(lax.rem(x + k, nx), y, z, c)).start()
    for k in range(1, ny):
        remote(yfirst, yfirst, lsem.at[2], lsem.at[3], device(x, lax.rem(y + k, ny), z, c)).start()

    for kz, at in ((2, 0), (NZ - 2, 0), (1, 2), (NZ - 1, 2), (0, 6)):
        for ky in range(ny):
            if kz or ky:
                remote(
                    rsend.at[ys[ky]], rbuf.at[c, y, z], rsem.at[at], rsem.at[at + 1],
                    (xat[0] + zat[kz], ys[ky]),
                ).start()

    arrived(lbuf.at[0, pl.ds(0, nx - 1), low], lsem.at[1])
    ythen = lbuf.at[y, :, low]
    for k in range(1, ny):
        remote(ythen, ythen, lsem.at[4], lsem.at[5], device(x, lax.rem(y + k, ny), z, c)).start()
    arrived(lbuf.at[pl.ds(0, ny - 1), 0, high], lsem.at[3])
    xthen = lbuf.at[:, x, high]
    for k in range(1, nx):
        remote(xthen, xthen, lsem.at[6], lsem.at[7], device(lax.rem(x + k, nx), y, z, c)).start()

    arrived(rbuf.at[0, :, pl.ds(0, 2)], rsem.at[1])
    early, late = pl.ds(0, ny // 2), pl.ds(ny // 2, ny // 2)
    for part, kz in (
        (rbuf.at[c, early, zs[NZ - 2]], 2),
        (rbuf.at[c, late, zs[2]], NZ - 2),
        (rbuf.at[c, :, zs[NZ - 2]], 1),
        (rbuf.at[c, :, zs[2]], NZ - 1),
    ):
        remote(part, part, rsem.at[4], rsem.at[5], (xat[0] + zat[kz], y)).start()

    pair_copy.wait()
    columns = pairv.shape[1]
    pairf[...] = pairv[...].astype(F32).reshape(ROWS * columns, cz)
    for i in range(ROWS):
        for h in range(NC):
            for r in range(jr):
                v = pairf[pl.ds(i * columns + h * ROWS + y * jr + r, nx * NZ, stride=NC * ROWS), :]
                for g in range(nx):
                    start = (g * thirds + h * NZ * jr + r) * ROWS + i
                    pstage[pl.ds(start, NZ, stride=jr * ROWS), :] = v[g * NZ : (g + 1) * NZ]
    psend[...] = pstage[...].astype(BF16).reshape(nx, thirds * ROWS, cz)
    pbuf[x] = psend[x]
    for k in range(1, nx):
        x2 = lax.rem(x + k, nx)
        remote(psend.at[x2], pbuf.at[x], psem.at[0], psem.at[1], device(x2, y, z, c)).start()

    for load in loads[3:]:
        load.wait()
    bd[...] = jnp.zeros_like(bd)
    for q in range(ch):
        w = wo_v[q * ch : (q + 1) * ch, :]
        for t in range(slab):
            bd[(q * slab + t) * ch : (q * slab + t + 1) * ch, t * cz : (t + 1) * cz] = w
    for t, ref in enumerate((ag_v, ap_v, bg_v, bp_v)):
        wt4[t * cz : (t + 1) * cz, :] = ref[...].astype(F32).T.astype(BF16)

    arrived(rbuf.at[0, :, pl.ds(0, 2)], rsem.at[3])
    arrived(rbuf.at[0, pl.ds(0, ny - 1), 0], rsem.at[7])
    arrived(rbuf.at[0, :, pl.ds(0, NZ - 5)], rsem.at[5])
    cross = remote(rbuf.at[c], rbuf.at[c], csem.at[0], csem.at[1], sibling)
    cross.start()
    arrived(lbuf.at[pl.ds(0, ny - 1), :, low], lsem.at[5])
    arrived(lbuf.at[:, pl.ds(0, nx - 1), high], lsem.at[7])

    def outer(side):
        right = rbuf[side]
        right = jnp.concatenate(
            [right[s].reshape(NZ * jr * ch, sd) for s in range(ny)], axis=1
        )

        def one(g, carry):
            rows = jnp.concatenate([lbuf[s, g] for s in range(ny)], axis=1)
            prod = nt(rows, right)
            for q in range(ch):
                part = prod[q * ROWS : (q + 1) * ROWS]
                abuf[side * nx + g, :, q * slab * ch : (q + 1) * slab * ch] = jnp.concatenate(
                    [part[:, t * slab * ch : (t + 1) * slab * ch] for t in range(njo)], axis=0
                ).astype(BF16)
            return carry

        lax.fori_loop(0, nx, one, 0)

    outer(c)
    cross.wait_recv()
    outer(1 - c)
    step = njo * ROWS
    mixer = abuf[...].reshape(NC * nx * step, slab * ch * ch)
    total = jnp.dot(mixer, bd[...], preferred_element_type=F32)

    arrived(pbuf.at[pl.ds(0, nx - 1)], psem.at[1])
    for g in range(nx):
        tiles = []
        for kk in range(thirds):
            h, flat = divmod(kk, NZ * jr)
            o, t = divmod(flat, slab)
            start = (h * nx + g) * step + o * ROWS
            tiles.append(total[start : start + ROWS, t * cz : (t + 1) * cz])
        u = pbuf[g].astype(F32) + jnp.concatenate(tiles, axis=0) * (1.0 / seqs)
        u = u.astype(BF16)
        usend[g] = u
        vbuf[g * thirds * ROWS : (g + 1) * thirds * ROWS] = u.astype(F32)

    for i in range(ROWS):
        norm[i * width : (i + 1) * width] = zscore(
            vbuf[pl.ds(i, width, stride=ROWS), :], 1
        ).astype(BF16)
    own = place(x, y, z)
    turns = outward(nx)
    some = ny * NZ
    for turn in turns:
        weights = jnp.concatenate(
            [wt4[pl.ds(pl.multiple_of(t * cz + xpart[turn], some), some)] for t in range(4)], axis=0
        )
        four = nt(weights, norm[...])
        lhs = jax.nn.sigmoid(four[:some]) * four[some : 2 * some]
        rhs = jax.nn.sigmoid(four[2 * some : 3 * some]) * four[3 * some :]
        for i in range(ROWS):
            span = slice(i * width, (i + 1) * width)
            lrscr[pl.ds(i, some, stride=2 * ROWS), :] = lhs[:, span]
            lrscr[pl.ds(ROWS + i, some, stride=2 * ROWS), :] = rhs[:, span]
        lrsend[pl.ds(xpart[turn], some)] = lrscr[...].reshape(some, 2 * ROWS, width).astype(BF16)
        for kz in outward(NZ):
            for ky in outward(ny):
                if turn or kz or ky:
                    remote(
                        lrsend.at[xpart[turn] + ypart[ky] + zpart[kz]], lrbuf.at[own],
                        asem.at[0, turn], asem.at[1, turn], (xat[turn] + zat[kz], ys[ky]),
                    ).start()
    lrbuf[own] = lrsend[own]

    for g in range(nx):
        here = jnp.logical_and(x == g, y == x)

        @pl.when(here)
        def _():
            ubuf[y] = usend[g]

        @pl.when(jnp.logical_not(here))
        def _():
            remote(
                usend.at[g], ubuf.at[y], usend_sem.at[g], urecv_sem.at[y], device(g, x, z, c)
            ).start()

    group = lax.broadcasted_iota(jnp.int32, (zh * NC * ROWS, width), 1) // thirds
    swaps = []
    for turn in turns:
        base = lax.rem(x + nx - turn, nx) * ny * NZ
        arrived(lrbuf.at[pl.ds(0, ny * NZ - (turn == 0))], asem.at[1, turn])
        part = pl.ds(base, ny * NZ)
        swap = remote(
            lrbuf.at[part], lrsib.at[part], ssem.at[0, turn], ssem.at[1, turn], sibling
        )
        swap.start()
        swap.wait_recv()
        swaps.append(swap)
        for s in range(ny):
            mine = lrbuf[pl.ds(base + s * NZ, NZ)].astype(F32)
            other = lrsib[pl.ds(base + s * NZ, NZ)].astype(F32)
            m0, m1 = jnp.where(first, mine, other), jnp.where(first, other, mine)
            span = slice(s * width, (s + 1) * width)
            rows = []
            for z2 in range(NZ):
                at = z2 % 2 * zh + z2 // 2
                rows += [m0[at, ROWS:], m1[at, ROWS:]]
            right = jnp.concatenate(rows, axis=0)
            for m in range(nx):
                rolled = pltpu.roll(right, m * thirds, 1) if m else right
                rwide[m * width : (m + 1) * width, span] = rolled.astype(BF16)
            rows = []
            for m in (m0, m1):
                rows.append(jnp.where(first, m[:zh, :ROWS], m[zh:, :ROWS]))
            left = jnp.concatenate(rows, axis=1).reshape(zh * NC * ROWS, width)
            for g in range(nx):
                lwide[g * zh * NC * ROWS : (g + 1) * zh * NC * ROWS, span] = jnp.where(
                    group == g, left, 0.0
                ).astype(BF16)
        if turn == turns[0]:
            mixed[...] = nt(lwide[...], rwide[...])
        else:
            mixed[...] += nt(lwide[...], rwide[...])
    for g in range(nx):
        for m in range(nx):
            g2 = (g - m) % nx
            part = mixed[g * zh * NC * ROWS : (g + 1) * zh * NC * ROWS, m * width : (m + 1) * width]
            msend[(g2 * nx + g) * zh : (g2 * nx + g + 1) * zh] = part.reshape(
                zh, NC * ROWS, width
            ).astype(BF16)

    side = lax.rem(z, 2)
    home = (x * ny + y) * zh + lax.div(z, 2)
    stays = side == c

    zhs = [lax.rem(lax.div(z, 2) + k, zh) for k in range(zh)]
    xback = [v * (NZ * NC) + side for v in xs]
    zback = [v * (2 * NC) + c * NC for v in zhs]
    ypart = [v * (nx * zh) for v in ys]
    xpart = [v * zh for v in xs]

    def send_back(turn, kz, ky):
        remote(
            msend.at[ypart[ky] + xpart[turn] + zhs[kz]], mbuf.at[side, home],
            msem.at[0, turn], msem.at[1, turn], (xback[turn] + zback[kz], ys[ky]),
        ).start()

    for turn in turns:
        for kz in outward(zh):
            for ky in outward(ny):
                if turn or kz or ky:
                    send_back(turn, kz, ky)

    @pl.when(stays)
    def _():
        mbuf[side, home] = msend[(y * nx + x) * zh + lax.div(z, 2)]

    @pl.when(jnp.logical_not(stays))
    def _():
        send_back(0, 0, 0)

    for s in range(ny):

        @pl.when(jnp.logical_not(jnp.logical_and(x == y, y == s)))
        def _():
            arrived(ubuf.at[s], urecv_sem.at[s])

        part = ubuf[s].astype(F32)
        for kk in range(thirds):
            h, flat = divmod(kk, NZ * jr)
            j = ((flat // jr) * NC + h) * ROWS + s * jr + flat % jr
            vbuf[j * ROWS : (j + 1) * ROWS, :] = part[kk * ROWS : (kk + 1) * ROWS]
    for i in range(ROWS):
        u = vbuf[pl.ds(i, width, stride=ROWS), :]
        upd[i] = u
        unit = zscore(u, 1).astype(BF16)
        gates[i] = jax.nn.sigmoid(jnp.dot(unit, fg_v[...], preferred_element_type=F32))

    arrived(lbuf.at[0, pl.ds(0, nx - 1), low], lsem.at[0])
    arrived(lbuf.at[pl.ds(0, ny - 1), 0, high], lsem.at[2])
    arrived(lbuf.at[pl.ds(0, ny - 1), :, low], lsem.at[4])
    arrived(lbuf.at[:, pl.ds(0, nx - 1), high], lsem.at[6])
    arrived(rbuf.at[0, :, pl.ds(0, 2)], rsem.at[0])
    arrived(rbuf.at[0, :, pl.ds(0, 2)], rsem.at[2])
    arrived(rbuf.at[0, pl.ds(0, ny - 1), 0], rsem.at[6])
    arrived(rbuf.at[0, :, pl.ds(0, NZ - 5)], rsem.at[4])
    arrived(psend.at[pl.ds(0, nx - 1)], psem.at[0])
    cross.wait_send()
    for g in range(nx):

        @pl.when(jnp.logical_not(jnp.logical_and(x == g, y == x)))
        def _():
            arrived(usend.at[g], usend_sem.at[g])

    for turn in turns:
        arrived(lrbuf.at[pl.ds(0, ny * NZ - (turn == 0))], asem.at[0, turn])
    for copy in swaps:
        copy.wait_send()

    finals = []
    for turn in turns:
        base = lax.rem(x + nx - turn, nx) * ny * zh
        if turn:
            arrived(mbuf.at[c, pl.ds(0, ny * zh)], msem.at[1, turn])
        else:

            @pl.when(stays)
            def _():
                arrived(mbuf.at[c, pl.ds(0, ny * zh - 1)], msem.at[1, 0])

            @pl.when(jnp.logical_not(stays))
            def _():
                arrived(mbuf.at[c, pl.ds(0, ny * zh)], msem.at[1, 0])

        part = mbuf.at[c, pl.ds(base, ny * zh)]
        final = remote(part, part, fsem.at[0, turn], fsem.at[1, turn], sibling)
        final.start()
        finals.append(final)
    for final in finals:
        final.wait_recv()

    full = mbuf[...].astype(F32)
    full = jnp.where(first, full[:, :, :ROWS], full[:, :, ROWS:])
    unit = zscore(full.reshape(cz, ROWS, width), 0)
    for p in range(2):
        for s in range(nyx):
            start = s * NZ + p * zh
            part = unit[(p * nyx + s) * zh : (p * nyx + s + 1) * zh]
            nscr[start * ROWS : (start + zh) * ROWS] = part.reshape(zh * ROWS, width)
    for i in range(ROWS):
        unit = nscr[pl.ds(i, cz, stride=ROWS), :].T.astype(BF16)
        proj = jnp.dot(unit, fp_v[...], preferred_element_type=F32)
        out_ref[i] = (upd[i] + gates[i] * proj).astype(BF16)

    for turn in turns:
        if turn:
            arrived(msend.at[pl.ds(0, ny * zh)], msem.at[0, turn])

    @pl.when(stays)
    def _():
        arrived(msend.at[pl.ds(0, ny * zh - 1)], msem.at[0, 0])

    @pl.when(jnp.logical_not(stays))
    def _():
        arrived(msend.at[pl.ds(0, ny * zh)], msem.at[0, 0])

    for copy in finals:
        copy.wait_send()


def shards(msa, pair, wl, wr, wo, *weights):
    ny = lax.axis_size("blk")
    nx = lax.axis_size("dap") // (NZ * NC)
    sd, _, cm = msa.shape
    ch, cz = wl.shape[1], wo.shape[1]
    columns = pair.shape[1]
    jr = ROWS // ny
    width = NZ * NC * ROWS
    thirds = NC * NZ * jr
    step = NZ * jr // 4 * ROWS
    peers = nx * ny * NZ
    vmem = pltpu.VMEM
    dma = pltpu.SemaphoreType.DMA
    scratch = [
        vmem((cm // 128 * sd * ROWS, 128), F32),
        vmem((ch * ROWS, sd), F32),
        vmem((ny, nx, ch * ROWS, sd), BF16),
        vmem((ny, jr * ch, sd), BF16),
        vmem((NC, ny, NZ, jr * ch, sd), BF16),
        vmem((NC * nx, step, 4 * ch * ch), BF16),
        vmem((4 * ch * ch, 4 * cz), BF16),
        vmem((ROWS, columns, cz), BF16),
        vmem((ROWS * columns, cz), F32),
        vmem((nx * thirds * ROWS, cz), F32),
        vmem((nx, thirds * ROWS, cz), BF16),
        vmem((nx, thirds * ROWS, cz), BF16),
        vmem((nx, thirds * ROWS, cz), BF16),
        vmem((ny, thirds * ROWS, cz), BF16),
        vmem((width * ROWS, cz), F32),
        vmem((ROWS, width, cz), F32),
        vmem((4 * cz, cz), BF16),
        vmem((ROWS * width, cz), BF16),
        vmem((ny * NZ * 2 * ROWS, width), F32),
        vmem((cz, 2 * ROWS, width), BF16),
        vmem((peers, 2 * ROWS, width), BF16),
        vmem((peers, 2 * ROWS, width), BF16),
        vmem((nx * NZ * ROWS, ny * width), BF16),
        vmem((nx * width, ny * width), BF16),
        vmem((nx * NZ * ROWS, nx * width), F32),
        vmem((peers // 2, 2 * ROWS, width), BF16),
        vmem((2, peers // 2, 2 * ROWS, width), BF16),
        vmem((cz * ROWS, width), F32),
        vmem((ROWS, width, cz), F32),
        vmem((sd * ROWS, cm), BF16),
        vmem((ch, cm), BF16),
        vmem((ch, cm), BF16),
        vmem((ch * ch, cz), BF16),
    ] + [vmem((cz, cz), BF16)] * 6 + [
        dma((10,)),
        dma,
        dma((10,)),
        dma((8,)),
        dma((2,)),
        dma((2,)),
        dma((nx,)),
        dma((ny,)),
        dma((2, nx)),
        dma((2, nx)),
        dma((2, nx)),
        dma((2, nx)),
    ]
    return pl.pallas_call(
        functools.partial(kernel, nx, ny, ny * sd),
        out_shape=pltpu.VMEM((ROWS, width, cz), BF16),
        in_specs=[pl.BlockSpec(memory_space=pltpu.HBM)] * 11,
        out_specs=pl.BlockSpec(memory_space=pltpu.VMEM),
        scratch_shapes=scratch,
        compiler_params=pltpu.CompilerParams(
            collective_id=0, has_side_effects=True, vmem_limit_bytes=48 * 2**20
        ),
    )(*[pltpu.with_memory_space_constraint(v, pltpu.HBM) for v in (msa.reshape(sd * ROWS, cm), pair, wl.T, wr.T, wo, *weights)])


def solution(mesh):
    placed = (P("blk", "dap", None), P("dap", None, None)) + (P(),) * 9
    return jax.shard_map(
        shards, mesh=mesh, in_specs=placed, out_specs=P("dap", "blk", None), check_vma=False
    )
```

```python
import functools

import jax
import jax.numpy as jnp
from jax import lax
from jax.experimental import pallas as pl
from jax.experimental.pallas import tpu as pltpu
from jax.sharding import PartitionSpec as P

NZ = 8
NC = 2
ROWS = 8
EPS = 1e-5
MESH = pl.DeviceIdType.MESH
F32 = jnp.float32
BF16 = jnp.bfloat16


def nt(a, b):
    return lax.dot_general(a, b, (((1,), (1,)), ((), ())), preferred_element_type=F32)


def zscore(v, axis):
    centered = v - jnp.mean(v, axis=axis, keepdims=True)
    var = jnp.mean(centered * centered, axis=axis, keepdims=True)
    return centered * lax.rsqrt(var + EPS)


def device(x, y, z, c):
    return (x * NZ + z) * NC + c, y


def kernel(
    nx, ny, seqs,
    msa_ref, pair_ref, wl_ref, wr_ref, wo_ref, ag_ref, ap_ref, bg_ref, bp_ref, fg_ref, fp_ref,
    out_ref,
    xf, lscr, lbuf, rsend, rbuf, abuf, bd, pairv, pairf, pstage, psend, pbuf, usend, ubuf, vbuf, upd,
    wt4, norm, lrscr, lrsend, lrbuf, lrsib, lwide, rwide, mixed, msend, mbuf, nscr, gates,
    msa_v, wl_v, wr_v, wo_v, ag_v, ap_v, bg_v, bp_v, fg_v, fp_v,
    load_sem, pair_sem, lsem, rsem, csem, psem, usend_sem, urecv_sem, asem, ssem, msem, fsem,
):
    local = (msa_v, wl_v, wr_v, wo_v, ag_v, ap_v, bg_v, bp_v, fg_v, fp_v)
    d = lax.axis_index("dap")
    y = lax.axis_index("blk")
    x, z, c = d // (NZ * NC), (d // NC) % NZ, d % NC
    sd = msa_ref.shape[0] // ROWS
    ch = wl_ref.shape[0]
    cz = wo_ref.shape[1]
    jr = ROWS // ny
    slab = 4
    njo = NZ * jr // slab
    thirds = NC * NZ * jr
    width = NZ * NC * ROWS
    nyx = ny * nx
    zh = NZ // 2
    sibling = device(x, y, z, 1 - c)
    first = c == 0

    def place(x1, y1, z1):
        return (x1 * ny + y1) * NZ + lax.rem(z1, 2) * zh + lax.div(z1, 2)

    xs = [lax.rem(x + k, nx) for k in range(nx)]
    ys = [lax.rem(y + k, ny) for k in range(ny)]
    zs = [lax.rem(z + k, NZ) for k in range(NZ)]
    xat = [v * (NZ * NC) + c for v in xs]
    zat = [v * NC for v in zs]
    xpart = [v * (ny * NZ) for v in xs]
    ypart = [v * NZ for v in ys]
    zpart = [place(0, 0, v) for v in zs]

    def outward(n):
        return sorted(range(n), key=lambda k: -min(k, n - k))

    def remote(source, target, send, recv, to):
        return pltpu.make_async_remote_copy(
            source, target, send, recv, device_id=to, device_id_type=MESH
        )

    def away(k, n):
        return lax.rem(n // 2 + jnp.where(lax.rem(k, 2) == 1, lax.div(k + 1, 2), n - lax.div(k, 2)), n)

    def arrived(part, sem):
        pltpu.make_async_copy(part, part, sem).wait()

    barrier = pltpu.get_barrier_semaphore()

    def greet(x2, y2, z2, c2):
        pl.semaphore_signal(barrier, inc=1, device_id=device(x2, y2, z2, c2), device_id_type=MESH)

    greet(x, y, z, 1 - c)
    for k in range(1, nx):
        greet(lax.rem(x + k, nx), y, z, c)
    for kz in (0, 1, 2, NZ - 2, NZ - 1):
        for ky in range(ny):
            if kz or ky:
                greet(x, ys[ky], zs[kz], c)

    sources = (msa_ref, wl_ref, wr_ref, wo_ref, ag_ref, ap_ref, bg_ref, bp_ref, fg_ref, fp_ref)
    loads = [
        pltpu.make_async_copy(source, target, load_sem.at[t])
        for t, (source, target) in enumerate(zip(sources, local))
    ]
    for load in loads:
        load.start()
    pair_copy = pltpu.make_async_copy(pair_ref, pairv, pair_sem)
    pair_copy.start()
    for load in loads[:3]:
        load.wait()

    lanes = xf.shape[1]
    blocks = msa_v.shape[1] // lanes
    for h in range(blocks):
        xf[h * sd * ROWS : (h + 1) * sd * ROWS] = msa_v[:, h * lanes : (h + 1) * lanes].astype(F32)
    wlr = jnp.concatenate([wl_v[...], wr_v[...]], axis=0)
    for i in range(ROWS):
        v = jnp.concatenate(
            [xf[pl.ds(h * sd * ROWS + i, sd, stride=ROWS), :] for h in range(blocks)], axis=1
        )
        v = zscore(v, 1).astype(BF16)
        proj = nt(wlr, v)
        lscr[pl.ds(i, ch, stride=ROWS), :] = proj[:ch]
        rsend[i // jr, (i % jr) * ch : (i % jr + 1) * ch, :] = proj[ch:].astype(BF16)
    lbuf[y, x] = lscr[: ch * ROWS].astype(BF16)
    rbuf[c, y, z] = rsend[y]

    pl.semaphore_wait(barrier, ny * 5 + nx - 1)

    half = ch * ROWS // 2
    low, high = pl.ds(0, half), pl.ds(half, half)
    xfirst = lbuf.at[y, x, low]
    yfirst = lbuf.at[y, x, high]
    for k in range(1, nx):
        remote(xfirst, xfirst, lsem.at[0], lsem.at[1], device(lax.rem(x + k, nx), y, z, c)).start()
    for k in range(1, ny):
        remote(yfirst, yfirst, lsem.at[2], lsem.at[3], device(x, lax.rem(y + k, ny), z, c)).start()

    for kz, at in ((2, 0), (NZ - 2, 0), (1, 2), (NZ - 1, 2), (0, 6)):
        for ky in range(ny):
            if kz or ky:
                remote(
                    rsend.at[ys[ky]], rbuf.at[c, y, z], rsem.at[at], rsem.at[at + 1],
                    (xat[0] + zat[kz], ys[ky]),
                ).start()

    arrived(lbuf.at[0, pl.ds(0, nx - 1), low], lsem.at[1])
    ythen = lbuf.at[y, :, low]
    for k in range(1, ny):
        remote(ythen, ythen, lsem.at[4], lsem.at[5], device(x, lax.rem(y + k, ny), z, c)).start()
    arrived(lbuf.at[pl.ds(0, ny - 1), 0, high], lsem.at[3])
    xthen = lbuf.at[:, x, high]
    for k in range(1, nx):
        remote(xthen, xthen, lsem.at[6], lsem.at[7], device(lax.rem(x + k, nx), y, z, c)).start()

    arrived(rbuf.at[0, :, pl.ds(0, 2)], rsem.at[1])
    early, late = pl.ds(0, ny // 2), pl.ds(ny // 2, ny // 2)
    for part, kz in (
        (rbuf.at[c, early, zs[NZ - 2]], 2),
        (rbuf.at[c, late, zs[2]], NZ - 2),
        (rbuf.at[c, :, zs[NZ - 2]], 1),
        (rbuf.at[c, :, zs[2]], NZ - 1),
    ):
        remote(part, part, rsem.at[4], rsem.at[5], (xat[0] + zat[kz], y)).start()

    pair_copy.wait()
    columns = pairv.shape[1]
    pairf[: ROWS * columns] = pairv[...].astype(F32).reshape(ROWS * columns, cz)
    for i in range(ROWS):
        for h in range(NC):
            for r in range(jr):
                v = pairf[pl.ds(i * columns + h * ROWS + y * jr + r, nx * NZ, stride=NC * ROWS), :]
                for g in range(nx):
                    start = (g * thirds + h * NZ * jr + r) * ROWS + i
                    pstage[pl.ds(start, NZ, stride=jr * ROWS), :] = v[g * NZ : (g + 1) * NZ]
    staged = pstage[: nx * thirds * ROWS].astype(BF16)
    psend[...] = staged.reshape(nx, thirds * ROWS, cz)
    pbuf[x] = psend[x]
    for k in range(1, nx):
        x2 = lax.rem(x + k, nx)
        remote(psend.at[x2], pbuf.at[x], psem.at[0], psem.at[1], device(x2, y, z, c)).start()

    for load in loads[3:]:
        load.wait()
    bd[...] = jnp.zeros_like(bd)
    for q in range(ch):
        w = wo_v[q * ch : (q + 1) * ch, :]
        for t in range(slab):
            bd[(q * slab + t) * ch : (q * slab + t + 1) * ch, t * cz : (t + 1) * cz] = w
    for t, ref in enumerate((ag_v, ap_v, bg_v, bp_v)):
        wt4[t * cz : (t + 1) * cz, :] = ref[...].astype(F32).T.astype(BF16)

    arrived(rbuf.at[0, :, pl.ds(0, 2)], rsem.at[3])
    arrived(rbuf.at[0, pl.ds(0, ny - 1), 0], rsem.at[7])
    arrived(rbuf.at[0, :, pl.ds(0, NZ - 5)], rsem.at[5])
    cross = remote(rbuf.at[c], rbuf.at[c], csem.at[0], csem.at[1], sibling)
    cross.start()
    arrived(lbuf.at[pl.ds(0, ny - 1), :, low], lsem.at[5])
    arrived(lbuf.at[:, pl.ds(0, nx - 1), high], lsem.at[7])

    def outer(side):
        right = rbuf[side]
        right = jnp.concatenate(
            [right[s].reshape(NZ * jr * ch, sd) for s in range(ny)], axis=1
        )

        def one(g, carry):
            rows = jnp.concatenate([lbuf[s, g] for s in range(ny)], axis=1)
            prod = nt(rows, right)
            for q in range(ch):
                part = prod[q * ROWS : (q + 1) * ROWS]
                abuf[side * nx + g, :, q * slab * ch : (q + 1) * slab * ch] = jnp.concatenate(
                    [part[:, t * slab * ch : (t + 1) * slab * ch] for t in range(njo)], axis=0
                ).astype(BF16)
            return carry

        lax.fori_loop(0, nx, one, 0)

    outer(c)
    cross.wait_recv()
    outer(1 - c)
    step = njo * ROWS
    mixer = abuf[...].reshape(NC * nx * step, slab * ch * ch)
    total = jnp.dot(mixer, bd[...], preferred_element_type=F32)

    arrived(pbuf.at[pl.ds(0, nx - 1)], psem.at[1])
    for g in range(nx):
        tiles = []
        for kk in range(thirds):
            h, flat = divmod(kk, NZ * jr)
            o, t = divmod(flat, slab)
            start = (h * nx + g) * step + o * ROWS
            tiles.append(total[start : start + ROWS, t * cz : (t + 1) * cz])
        u = pbuf[g].astype(F32) + jnp.concatenate(tiles, axis=0) * (1.0 / seqs)
        u = u.astype(BF16)
        usend[g] = u
        vbuf[g * thirds * ROWS : (g + 1) * thirds * ROWS] = u.astype(F32)

    for i in range(ROWS):
        norm[i * width : (i + 1) * width] = zscore(
            vbuf[pl.ds(i, width, stride=ROWS), :], 1
        ).astype(BF16)
    own = place(x, y, z)
    turns = outward(nx)
    some = ny * NZ
    for turn in turns:
        weights = jnp.concatenate(
            [wt4[pl.ds(pl.multiple_of(t * cz + xpart[turn], some), some)] for t in range(4)], axis=0
        )
        four = nt(weights, norm[...])
        lhs = jax.nn.sigmoid(four[:some]) * four[some : 2 * some]
        rhs = jax.nn.sigmoid(four[2 * some : 3 * some]) * four[3 * some :]
        for i in range(ROWS):
            span = slice(i * width, (i + 1) * width)
            lrscr[pl.ds(i, some, stride=2 * ROWS), :] = lhs[:, span]
            lrscr[pl.ds(ROWS + i, some, stride=2 * ROWS), :] = rhs[:, span]
        tiles = lrscr[: some * 2 * ROWS].reshape(some, 2 * ROWS, width)
        lrsend[pl.ds(xpart[turn], some)] = tiles.astype(BF16)
        for kz in outward(NZ):
            for ky in outward(ny):
                if turn or kz or ky:
                    remote(
                        lrsend.at[xpart[turn] + ypart[ky] + zpart[kz]], lrbuf.at[own],
                        asem.at[0, turn], asem.at[1, turn], (xat[turn] + zat[kz], ys[ky]),
                    ).start()
    lrbuf[own] = lrsend[own]

    for g in range(nx):
        here = jnp.logical_and(x == g, y == x)

        @pl.when(here)
        def _():
            ubuf[y] = usend[g]

        @pl.when(jnp.logical_not(here))
        def _():
            remote(
                usend.at[g], ubuf.at[y], usend_sem.at[g], urecv_sem.at[y], device(g, x, z, c)
            ).start()

    group = lax.broadcasted_iota(jnp.int32, (zh * NC * ROWS, width), 1) // thirds
    swaps = []
    for turn in turns:
        base = lax.rem(x + nx - turn, nx) * ny * NZ
        arrived(lrbuf.at[pl.ds(0, ny * NZ - (turn == 0))], asem.at[1, turn])
        part = pl.ds(base, ny * NZ)
        swap = remote(
            lrbuf.at[part], lrsib.at[part], ssem.at[0, turn], ssem.at[1, turn], sibling
        )
        swap.start()
        swap.wait_recv()
        swaps.append(swap)
        for s in range(ny):
            mine = lrbuf[pl.ds(base + s * NZ, NZ)].astype(F32)
            other = lrsib[pl.ds(base + s * NZ, NZ)].astype(F32)
            m0, m1 = jnp.where(first, mine, other), jnp.where(first, other, mine)
            span = slice(s * width, (s + 1) * width)
            rows = []
            for z2 in range(NZ):
                at = z2 % 2 * zh + z2 // 2
                rows += [m0[at, ROWS:], m1[at, ROWS:]]
            right = jnp.concatenate(rows, axis=0)
            for m in range(nx):
                rolled = pltpu.roll(right, m * thirds, 1) if m else right
                rwide[m * width : (m + 1) * width, span] = rolled.astype(BF16)
            rows = []
            for m in (m0, m1):
                rows.append(jnp.where(first, m[:zh, :ROWS], m[zh:, :ROWS]))
            left = jnp.concatenate(rows, axis=1).reshape(zh * NC * ROWS, width)
            for g in range(nx):
                lwide[g * zh * NC * ROWS : (g + 1) * zh * NC * ROWS, span] = jnp.where(
                    group == g, left, 0.0
                ).astype(BF16)
        if turn == turns[0]:
            mixed[...] = nt(lwide[...], rwide[...])
        else:
            mixed[...] += nt(lwide[...], rwide[...])
    for g in range(nx):
        for m in range(nx):
            g2 = (g - m) % nx
            part = mixed[g * zh * NC * ROWS : (g + 1) * zh * NC * ROWS, m * width : (m + 1) * width]
            msend[(g2 * nx + g) * zh : (g2 * nx + g + 1) * zh] = part.reshape(
                zh, NC * ROWS, width
            ).astype(BF16)

    side = lax.rem(z, 2)
    home = (x * ny + y) * zh + lax.div(z, 2)
    stays = side == c

    zhs = [lax.rem(lax.div(z, 2) + k, zh) for k in range(zh)]
    xback = [v * (NZ * NC) + side for v in xs]
    zback = [v * (2 * NC) + c * NC for v in zhs]
    ypart = [v * (nx * zh) for v in ys]
    xpart = [v * zh for v in xs]

    def send_back(turn, kz, ky):
        remote(
            msend.at[ypart[ky] + xpart[turn] + zhs[kz]], mbuf.at[side, home],
            msem.at[0, turn], msem.at[1, turn], (xback[turn] + zback[kz], ys[ky]),
        ).start()

    for turn in turns:
        for kz in outward(zh):
            for ky in outward(ny):
                if turn or kz or ky:
                    send_back(turn, kz, ky)

    @pl.when(stays)
    def _():
        mbuf[side, home] = msend[(y * nx + x) * zh + lax.div(z, 2)]

    @pl.when(jnp.logical_not(stays))
    def _():
        send_back(0, 0, 0)

    for s in range(ny):

        @pl.when(jnp.logical_not(jnp.logical_and(x == y, y == s)))
        def _():
            arrived(ubuf.at[s], urecv_sem.at[s])

        part = ubuf[s].astype(F32)
        for kk in range(thirds):
            h, flat = divmod(kk, NZ * jr)
            j = ((flat // jr) * NC + h) * ROWS + s * jr + flat % jr
            vbuf[j * ROWS : (j + 1) * ROWS, :] = part[kk * ROWS : (kk + 1) * ROWS]
    for i in range(ROWS):
        u = vbuf[pl.ds(i, width, stride=ROWS), :]
        upd[i] = u
        unit = zscore(u, 1).astype(BF16)
        gates[i] = jax.nn.sigmoid(jnp.dot(unit, fg_v[...], preferred_element_type=F32))

    arrived(lbuf.at[0, pl.ds(0, nx - 1), low], lsem.at[0])
    arrived(lbuf.at[pl.ds(0, ny - 1), 0, high], lsem.at[2])
    arrived(lbuf.at[pl.ds(0, ny - 1), :, low], lsem.at[4])
    arrived(lbuf.at[:, pl.ds(0, nx - 1), high], lsem.at[6])
    arrived(rbuf.at[0, :, pl.ds(0, 2)], rsem.at[0])
    arrived(rbuf.at[0, :, pl.ds(0, 2)], rsem.at[2])
    arrived(rbuf.at[0, pl.ds(0, ny - 1), 0], rsem.at[6])
    arrived(rbuf.at[0, :, pl.ds(0, NZ - 5)], rsem.at[4])
    arrived(psend.at[pl.ds(0, nx - 1)], psem.at[0])
    cross.wait_send()
    for g in range(nx):

        @pl.when(jnp.logical_not(jnp.logical_and(x == g, y == x)))
        def _():
            arrived(usend.at[g], usend_sem.at[g])

    for turn in turns:
        arrived(lrbuf.at[pl.ds(0, ny * NZ - (turn == 0))], asem.at[0, turn])
    for copy in swaps:
        copy.wait_send()

    finals = []
    for turn in turns:
        base = lax.rem(x + nx - turn, nx) * ny * zh
        if turn:
            arrived(mbuf.at[c, pl.ds(0, ny * zh)], msem.at[1, turn])
        else:

            @pl.when(stays)
            def _():
                arrived(mbuf.at[c, pl.ds(0, ny * zh - 1)], msem.at[1, 0])

            @pl.when(jnp.logical_not(stays))
            def _():
                arrived(mbuf.at[c, pl.ds(0, ny * zh)], msem.at[1, 0])

        part = mbuf.at[c, pl.ds(base, ny * zh)]
        final = remote(part, part, fsem.at[0, turn], fsem.at[1, turn], sibling)
        final.start()
        finals.append(final)
    for final in finals:
        final.wait_recv()

    full = mbuf[...].astype(F32)
    full = jnp.where(first, full[:, :, :ROWS], full[:, :, ROWS:])
    unit = zscore(full.reshape(cz, ROWS, width), 0)
    for p in range(2):
        for s in range(nyx):
            start = s * NZ + p * zh
            part = unit[(p * nyx + s) * zh : (p * nyx + s + 1) * zh]
            nscr[start * ROWS : (start + zh) * ROWS] = part.reshape(zh * ROWS, width)
    for i in range(ROWS):
        unit = nscr[pl.ds(i, cz, stride=ROWS), :].T.astype(BF16)
        proj = jnp.dot(unit, fp_v[...], preferred_element_type=F32)
        out_ref[i] = (upd[i] + gates[i] * proj).astype(BF16)

    for turn in turns:
        if turn:
            arrived(msend.at[pl.ds(0, ny * zh)], msem.at[0, turn])

    @pl.when(stays)
    def _():
        arrived(msend.at[pl.ds(0, ny * zh - 1)], msem.at[0, 0])

    @pl.when(jnp.logical_not(stays))
    def _():
        arrived(msend.at[pl.ds(0, ny * zh)], msem.at[0, 0])

    for copy in finals:
        copy.wait_send()


def shards(msa, pair, wl, wr, wo, *weights):
    ny = lax.axis_size("blk")
    nx = lax.axis_size("dap") // (NZ * NC)
    sd, _, cm = msa.shape
    ch, cz = wl.shape[1], wo.shape[1]
    columns = pair.shape[1]
    jr = ROWS // ny
    width = NZ * NC * ROWS
    thirds = NC * NZ * jr
    step = NZ * jr // 4 * ROWS
    peers = nx * ny * NZ
    vmem = pltpu.VMEM
    dma = pltpu.SemaphoreType.DMA
    scratch = [
        vmem((cm // 128 * sd * ROWS + ROWS, 128), F32),
        vmem((ch * ROWS + ROWS, sd), F32),
        vmem((ny, nx, ch * ROWS, sd), BF16),
        vmem((ny, jr * ch, sd), BF16),
        vmem((NC, ny, NZ, jr * ch, sd), BF16),
        vmem((NC * nx, step, 4 * ch * ch), BF16),
        vmem((4 * ch * ch, 4 * cz), BF16),
        vmem((ROWS, columns, cz), BF16),
        vmem((ROWS * columns + 2 * ROWS, cz), F32),
        vmem((nx * thirds * ROWS + 2 * ROWS, cz), F32),
        vmem((nx, thirds * ROWS, cz), BF16),
        vmem((nx, thirds * ROWS, cz), BF16),
        vmem((nx, thirds * ROWS, cz), BF16),
        vmem((ny, thirds * ROWS, cz), BF16),
        vmem((width * ROWS + ROWS, cz), F32),
        vmem((ROWS, width, cz), F32),
        vmem((4 * cz, cz), BF16),
        vmem((ROWS * width, cz), BF16),
        vmem((ny * NZ * 2 * ROWS + 2 * ROWS, width), F32),
        vmem((cz, 2 * ROWS, width), BF16),
        vmem((peers, 2 * ROWS, width), BF16),
        vmem((peers, 2 * ROWS, width), BF16),
        vmem((nx * NZ * ROWS, ny * width), BF16),
        vmem((nx * width, ny * width), BF16),
        vmem((nx * NZ * ROWS, nx * width), F32),
        vmem((peers // 2, 2 * ROWS, width), BF16),
        vmem((2, peers // 2, 2 * ROWS, width), BF16),
        vmem((cz * ROWS + ROWS, width), F32),
        vmem((ROWS, width, cz), F32),
        vmem((sd * ROWS, cm), BF16),
        vmem((ch, cm), BF16),
        vmem((ch, cm), BF16),
        vmem((ch * ch, cz), BF16),
    ] + [vmem((cz, cz), BF16)] * 6 + [
        dma((10,)),
        dma,
        dma((10,)),
        dma((8,)),
        dma((2,)),
        dma((2,)),
        dma((nx,)),
        dma((ny,)),
        dma((2, nx)),
        dma((2, nx)),
        dma((2, nx)),
        dma((2, nx)),
    ]
    return pl.pallas_call(
        functools.partial(kernel, nx, ny, ny * sd),
        out_shape=pltpu.VMEM((ROWS, width, cz), BF16),
        in_specs=[pl.BlockSpec(memory_space=pltpu.HBM)] * 11,
        out_specs=pl.BlockSpec(memory_space=pltpu.VMEM),
        scratch_shapes=scratch,
        compiler_params=pltpu.CompilerParams(
            collective_id=0, has_side_effects=True, vmem_limit_bytes=48 * 2**20
        ),
    )(*[pltpu.with_memory_space_constraint(v, pltpu.HBM) for v in (msa.reshape(sd * ROWS, cm), pair, wl.T, wr.T, wo, *weights)])


def solution(mesh):
    placed = (P("blk", "dap", None), P("dap", None, None)) + (P(),) * 9
    return jax.shard_map(
        shards, mesh=mesh, in_specs=placed, out_specs=P("dap", "blk", None), check_vma=False
    )
```

```python
import functools

import jax
import jax.numpy as jnp
from jax import lax
from jax.experimental import pallas as pl
from jax.experimental.pallas import tpu as pltpu
from jax.sharding import PartitionSpec as P

NZ = 8
NC = 2
ROWS = 8
EPS = 1e-5
MESH = pl.DeviceIdType.MESH
F32 = jnp.float32
BF16 = jnp.bfloat16


def nt(a, b):
    return lax.dot_general(a, b, (((1,), (1,)), ((), ())), preferred_element_type=F32)


def zscore(v, axis):
    centered = v - jnp.mean(v, axis=axis, keepdims=True)
    var = jnp.mean(centered * centered, axis=axis, keepdims=True)
    return centered * lax.rsqrt(var + EPS)


def device(x, y, z, c):
    return (x * NZ + z) * NC + c, y


def kernel(
    nx, ny, seqs,
    msa_ref, pair_ref, wl_ref, wr_ref, wo_ref, ag_ref, ap_ref, bg_ref, bp_ref, fg_ref, fp_ref,
    out_ref,
    xf, lscr, lbuf, rsend, rbuf, abuf, bd, pairv, pairf, pstage, psend, pbuf, usend, ubuf, vbuf, upd,
    wt4, norm, lrscr, lrsend, lrbuf, lrsib, lwide, rwide, mixed, msend, mbuf, nscr, gates,
    msa_v, wl_v, wr_v, wo_v, ag_v, ap_v, bg_v, bp_v, fg_v, fp_v,
    load_sem, pair_sem, lsem, rsem, csem, psem, usend_sem, urecv_sem, asem, ssem, msem, fsem,
):
    local = (msa_v, wl_v, wr_v, wo_v, ag_v, ap_v, bg_v, bp_v, fg_v, fp_v)
    d = lax.axis_index("dap")
    y = lax.axis_index("blk")
    x, z, c = d // (NZ * NC), (d // NC) % NZ, d % NC
    sd = msa_ref.shape[0] // ROWS
    ch = wl_ref.shape[0]
    cz = wo_ref.shape[1]
    jr = ROWS // ny
    slab = 4
    njo = NZ * jr // slab
    thirds = NC * NZ * jr
    width = NZ * NC * ROWS
    nyx = ny * nx
    zh = NZ // 2
    sibling = device(x, y, z, 1 - c)
    first = c == 0

    def place(x1, y1, z1):
        return (x1 * ny + y1) * NZ + lax.rem(z1, 2) * zh + lax.div(z1, 2)

    xs = [lax.rem(x + k, nx) for k in range(nx)]
    ys = [lax.rem(y + k, ny) for k in range(ny)]
    zs = [lax.rem(z + k, NZ) for k in range(NZ)]
    xat = [v * (NZ * NC) + c for v in xs]
    zat = [v * NC for v in zs]
    xpart = [v * (ny * NZ) for v in xs]
    ypart = [v * NZ for v in ys]
    zpart = [place(0, 0, v) for v in zs]

    def outward(n):
        return sorted(range(n), key=lambda k: -min(k, n - k))

    def remote(source, target, send, recv, to):
        return pltpu.make_async_remote_copy(
            source, target, send, recv, device_id=to, device_id_type=MESH
        )

    def away(k, n):
        return lax.rem(n // 2 + jnp.where(lax.rem(k, 2) == 1, lax.div(k + 1, 2), n - lax.div(k, 2)), n)

    def arrived(part, sem):
        pltpu.make_async_copy(part, part, sem).wait()

    barrier = pltpu.get_barrier_semaphore()

    def greet(x2, y2, z2, c2):
        pl.semaphore_signal(barrier, inc=1, device_id=device(x2, y2, z2, c2), device_id_type=MESH)

    greet(x, y, z, 1 - c)
    for k in range(1, nx):
        greet(lax.rem(x + k, nx), y, z, c)
    for kz in (0, 1, 2, NZ - 2, NZ - 1):
        for ky in range(ny):
            if kz or ky:
                greet(x, ys[ky], zs[kz], c)

    sources = (msa_ref, wl_ref, wr_ref, wo_ref, ag_ref, ap_ref, bg_ref, bp_ref, fg_ref, fp_ref)
    loads = [
        pltpu.make_async_copy(source, target, load_sem.at[t])
        for t, (source, target) in enumerate(zip(sources, local))
    ]
    for load in loads:
        load.start()
    pair_copy = pltpu.make_async_copy(pair_ref, pairv, pair_sem)
    pair_copy.start()
    for load in loads[:3]:
        load.wait()

    lanes = xf.shape[1]
    blocks = msa_v.shape[1] // lanes
    for h in range(blocks):
        xf[h * sd * ROWS : (h + 1) * sd * ROWS] = msa_v[:, h * lanes : (h + 1) * lanes].astype(F32)
    wlr = jnp.concatenate([wl_v[...], wr_v[...]], axis=0)
    for i in range(ROWS):
        v = jnp.concatenate(
            [xf[pl.ds(h * sd * ROWS + i, sd, stride=ROWS), :] for h in range(blocks)], axis=1
        )
        v = zscore(v, 1).astype(BF16)
        proj = nt(wlr, v)
        lscr[pl.ds(i, ch, stride=ROWS), :] = proj[:ch]
        rsend[i // jr, (i % jr) * ch : (i % jr + 1) * ch, :] = proj[ch:].astype(BF16)
    lbuf[y, x] = lscr[: ch * ROWS].astype(BF16)
    rbuf[c, y, z] = rsend[y]

    pl.semaphore_wait(barrier, ny * 5 + nx - 1)

    half = ch * ROWS // 2
    low, high = pl.ds(0, half), pl.ds(half, half)
    xfirst = lbuf.at[y, x, low]
    yfirst = lbuf.at[y, x, high]
    for k in range(1, nx):
        remote(xfirst, xfirst, lsem.at[0], lsem.at[1], device(lax.rem(x + k, nx), y, z, c)).start()
    for k in range(1, ny):
        remote(yfirst, yfirst, lsem.at[2], lsem.at[3], device(x, lax.rem(y + k, ny), z, c)).start()

    for kz, at in ((2, 0), (NZ - 2, 0), (1, 2), (NZ - 1, 2), (0, 6)):
        for ky in range(ny):
            if kz or ky:
                remote(
                    rsend.at[ys[ky]], rbuf.at[c, y, z], rsem.at[at], rsem.at[at + 1],
                    (xat[0] + zat[kz], ys[ky]),
                ).start()

    pair_copy.wait()
    columns = pairv.shape[1]
    pairf[: ROWS * columns] = pairv[...].astype(F32).reshape(ROWS * columns, cz)
    for i in range(ROWS):
        for h in range(NC):
            for r in range(jr):
                v = pairf[pl.ds(i * columns + h * ROWS + y * jr + r, nx * NZ, stride=NC * ROWS), :]
                for g in range(nx):
                    start = (g * thirds + h * NZ * jr + r) * ROWS + i
                    pstage[pl.ds(start, NZ, stride=jr * ROWS), :] = v[g * NZ : (g + 1) * NZ]
    staged = pstage[: nx * thirds * ROWS].astype(BF16)
    psend[...] = staged.reshape(nx, thirds * ROWS, cz)
    pbuf[x] = psend[x]
    for k in range(1, nx):
        x2 = lax.rem(x + k, nx)
        remote(psend.at[x2], pbuf.at[x], psem.at[0], psem.at[1], device(x2, y, z, c)).start()

    arrived(lbuf.at[0, pl.ds(0, nx - 1), low], lsem.at[1])
    ythen = lbuf.at[y, :, low]
    for k in range(1, ny):
        remote(ythen, ythen, lsem.at[4], lsem.at[5], device(x, lax.rem(y + k, ny), z, c)).start()
    arrived(lbuf.at[pl.ds(0, ny - 1), 0, high], lsem.at[3])
    xthen = lbuf.at[:, x, high]
    for k in range(1, nx):
        remote(xthen, xthen, lsem.at[6], lsem.at[7], device(lax.rem(x + k, nx), y, z, c)).start()

    arrived(rbuf.at[0, :, pl.ds(0, 2)], rsem.at[1])
    early, late = pl.ds(0, ny // 2), pl.ds(ny // 2, ny // 2)
    for part, kz in (
        (rbuf.at[c, early, zs[NZ - 2]], 2),
        (rbuf.at[c, late, zs[2]], NZ - 2),
        (rbuf.at[c, :, zs[NZ - 2]], 1),
        (rbuf.at[c, :, zs[2]], NZ - 1),
    ):
        remote(part, part, rsem.at[4], rsem.at[5], (xat[0] + zat[kz], y)).start()

    for load in loads[3:]:
        load.wait()
    bd[...] = jnp.zeros_like(bd)
    for q in range(ch):
        w = wo_v[q * ch : (q + 1) * ch, :]
        for t in range(slab):
            bd[(q * slab + t) * ch : (q * slab + t + 1) * ch, t * cz : (t + 1) * cz] = w
    for t, ref in enumerate((ag_v, ap_v, bg_v, bp_v)):
        wt4[t * cz : (t + 1) * cz, :] = ref[...].astype(F32).T.astype(BF16)

    arrived(rbuf.at[0, :, pl.ds(0, 2)], rsem.at[3])
    arrived(rbuf.at[0, pl.ds(0, ny - 1), 0], rsem.at[7])
    arrived(rbuf.at[0, :, pl.ds(0, NZ - 5)], rsem.at[5])
    cross = remote(rbuf.at[c], rbuf.at[c], csem.at[0], csem.at[1], sibling)
    cross.start()
    arrived(lbuf.at[pl.ds(0, ny - 1), :, low], lsem.at[5])
    arrived(lbuf.at[:, pl.ds(0, nx - 1), high], lsem.at[7])

    def outer(side):
        right = rbuf[side]
        right = jnp.concatenate(
            [right[s].reshape(NZ * jr * ch, sd) for s in range(ny)], axis=1
        )

        def one(g, carry):
            rows = jnp.concatenate([lbuf[s, g] for s in range(ny)], axis=1)
            prod = nt(rows, right)
            for q in range(ch):
                part = prod[q * ROWS : (q + 1) * ROWS]
                abuf[side * nx + g, :, q * slab * ch : (q + 1) * slab * ch] = jnp.concatenate(
                    [part[:, t * slab * ch : (t + 1) * slab * ch] for t in range(njo)], axis=0
                ).astype(BF16)
            return carry

        lax.fori_loop(0, nx, one, 0)

    outer(c)
    cross.wait_recv()
    outer(1 - c)
    step = njo * ROWS
    mixer = abuf[...].reshape(NC * nx * step, slab * ch * ch)
    total = jnp.dot(mixer, bd[...], preferred_element_type=F32)

    arrived(pbuf.at[pl.ds(0, nx - 1)], psem.at[1])
    for g in range(nx):
        tiles = []
        for kk in range(thirds):
            h, flat = divmod(kk, NZ * jr)
            o, t = divmod(flat, slab)
            start = (h * nx + g) * step + o * ROWS
            tiles.append(total[start : start + ROWS, t * cz : (t + 1) * cz])
        u = pbuf[g].astype(F32) + jnp.concatenate(tiles, axis=0) * (1.0 / seqs)
        u = u.astype(BF16)
        usend[g] = u
        vbuf[g * thirds * ROWS : (g + 1) * thirds * ROWS] = u.astype(F32)

    for i in range(ROWS):
        norm[i * width : (i + 1) * width] = zscore(
            vbuf[pl.ds(i, width, stride=ROWS), :], 1
        ).astype(BF16)
    own = place(x, y, z)
    turns = outward(nx)
    some = ny * NZ
    for turn in turns:
        weights = jnp.concatenate(
            [wt4[pl.ds(pl.multiple_of(t * cz + xpart[turn], some), some)] for t in range(4)], axis=0
        )
        four = nt(weights, norm[...])
        lhs = jax.nn.sigmoid(four[:some]) * four[some : 2 * some]
        rhs = jax.nn.sigmoid(four[2 * some : 3 * some]) * four[3 * some :]
        for i in range(ROWS):
            span = slice(i * width, (i + 1) * width)
            lrscr[pl.ds(i, some, stride=2 * ROWS), :] = lhs[:, span]
            lrscr[pl.ds(ROWS + i, some, stride=2 * ROWS), :] = rhs[:, span]
        tiles = lrscr[: some * 2 * ROWS].reshape(some, 2 * ROWS, width)
        lrsend[pl.ds(xpart[turn], some)] = tiles.astype(BF16)
        for kz in outward(NZ):
            for ky in outward(ny):
                if turn or kz or ky:
                    remote(
                        lrsend.at[xpart[turn] + ypart[ky] + zpart[kz]], lrbuf.at[own],
                        asem.at[0, turn], asem.at[1, turn], (xat[turn] + zat[kz], ys[ky]),
                    ).start()
    lrbuf[own] = lrsend[own]

    for g in range(nx):
        here = jnp.logical_and(x == g, y == x)

        @pl.when(here)
        def _():
            ubuf[y] = usend[g]

        @pl.when(jnp.logical_not(here))
        def _():
            remote(
                usend.at[g], ubuf.at[y], usend_sem.at[g], urecv_sem.at[y], device(g, x, z, c)
            ).start()

    group = lax.broadcasted_iota(jnp.int32, (zh * NC * ROWS, width), 1) // thirds
    swaps = []
    for turn in turns:
        base = lax.rem(x + nx - turn, nx) * ny * NZ
        arrived(lrbuf.at[pl.ds(0, ny * NZ - (turn == 0))], asem.at[1, turn])
        part = pl.ds(base, ny * NZ)
        swap = remote(
            lrbuf.at[part], lrsib.at[part], ssem.at[0, turn], ssem.at[1, turn], sibling
        )
        swap.start()
        swap.wait_recv()
        swaps.append(swap)
        for s in range(ny):
            mine = lrbuf[pl.ds(base + s * NZ, NZ)].astype(F32)
            other = lrsib[pl.ds(base + s * NZ, NZ)].astype(F32)
            m0, m1 = jnp.where(first, mine, other), jnp.where(first, other, mine)
            span = slice(s * width, (s + 1) * width)
            rows = []
            for z2 in range(NZ):
                at = z2 % 2 * zh + z2 // 2
                rows += [m0[at, ROWS:], m1[at, ROWS:]]
            right = jnp.concatenate(rows, axis=0)
            for m in range(nx):
                rolled = pltpu.roll(right, m * thirds, 1) if m else right
                rwide[m * width : (m + 1) * width, span] = rolled.astype(BF16)
            rows = []
            for m in (m0, m1):
                rows.append(jnp.where(first, m[:zh, :ROWS], m[zh:, :ROWS]))
            left = jnp.concatenate(rows, axis=1).reshape(zh * NC * ROWS, width)
            for g in range(nx):
                lwide[g * zh * NC * ROWS : (g + 1) * zh * NC * ROWS, span] = jnp.where(
                    group == g, left, 0.0
                ).astype(BF16)
        if turn == turns[0]:
            mixed[...] = nt(lwide[...], rwide[...])
        else:
            mixed[...] += nt(lwide[...], rwide[...])
    for g in range(nx):
        for m in range(nx):
            g2 = (g - m) % nx
            part = mixed[g * zh * NC * ROWS : (g + 1) * zh * NC * ROWS, m * width : (m + 1) * width]
            msend[(g2 * nx + g) * zh : (g2 * nx + g + 1) * zh] = part.reshape(
                zh, NC * ROWS, width
            ).astype(BF16)

    side = lax.rem(z, 2)
    home = (x * ny + y) * zh + lax.div(z, 2)
    stays = side == c

    zhs = [lax.rem(lax.div(z, 2) + k, zh) for k in range(zh)]
    xback = [v * (NZ * NC) + side for v in xs]
    zback = [v * (2 * NC) + c * NC for v in zhs]
    ypart = [v * (nx * zh) for v in ys]
    xpart = [v * zh for v in xs]

    def send_back(turn, kz, ky):
        remote(
            msend.at[ypart[ky] + xpart[turn] + zhs[kz]], mbuf.at[side, home],
            msem.at[0, turn], msem.at[1, turn], (xback[turn] + zback[kz], ys[ky]),
        ).start()

    for turn in turns:
        for kz in outward(zh):
            for ky in outward(ny):
                if turn or kz or ky:
                    send_back(turn, kz, ky)

    @pl.when(stays)
    def _():
        mbuf[side, home] = msend[(y * nx + x) * zh + lax.div(z, 2)]

    @pl.when(jnp.logical_not(stays))
    def _():
        send_back(0, 0, 0)

    for s in range(ny):

        @pl.when(jnp.logical_not(jnp.logical_and(x == y, y == s)))
        def _():
            arrived(ubuf.at[s], urecv_sem.at[s])

        part = ubuf[s].astype(F32)
        for kk in range(thirds):
            h, flat = divmod(kk, NZ * jr)
            j = ((flat // jr) * NC + h) * ROWS + s * jr + flat % jr
            vbuf[j * ROWS : (j + 1) * ROWS, :] = part[kk * ROWS : (kk + 1) * ROWS]
    for i in range(ROWS):
        u = vbuf[pl.ds(i, width, stride=ROWS), :]
        upd[i] = u
        unit = zscore(u, 1).astype(BF16)
        gates[i] = jax.nn.sigmoid(jnp.dot(unit, fg_v[...], preferred_element_type=F32))

    arrived(lbuf.at[0, pl.ds(0, nx - 1), low], lsem.at[0])
    arrived(lbuf.at[pl.ds(0, ny - 1), 0, high], lsem.at[2])
    arrived(lbuf.at[pl.ds(0, ny - 1), :, low], lsem.at[4])
    arrived(lbuf.at[:, pl.ds(0, nx - 1), high], lsem.at[6])
    arrived(rbuf.at[0, :, pl.ds(0, 2)], rsem.at[0])
    arrived(rbuf.at[0, :, pl.ds(0, 2)], rsem.at[2])
    arrived(rbuf.at[0, pl.ds(0, ny - 1), 0], rsem.at[6])
    arrived(rbuf.at[0, :, pl.ds(0, NZ - 5)], rsem.at[4])
    arrived(psend.at[pl.ds(0, nx - 1)], psem.at[0])
    cross.wait_send()
    for g in range(nx):

        @pl.when(jnp.logical_not(jnp.logical_and(x == g, y == x)))
        def _():
            arrived(usend.at[g], usend_sem.at[g])

    for turn in turns:
        arrived(lrbuf.at[pl.ds(0, ny * NZ - (turn == 0))], asem.at[0, turn])
    for copy in swaps:
        copy.wait_send()

    finals = []
    for turn in turns:
        base = lax.rem(x + nx - turn, nx) * ny * zh
        if turn:
            arrived(mbuf.at[c, pl.ds(0, ny * zh)], msem.at[1, turn])
        else:

            @pl.when(stays)
            def _():
                arrived(mbuf.at[c, pl.ds(0, ny * zh - 1)], msem.at[1, 0])

            @pl.when(jnp.logical_not(stays))
            def _():
                arrived(mbuf.at[c, pl.ds(0, ny * zh)], msem.at[1, 0])

        part = mbuf.at[c, pl.ds(base, ny * zh)]
        final = remote(part, part, fsem.at[0, turn], fsem.at[1, turn], sibling)
        final.start()
        finals.append(final)
    for final in finals:
        final.wait_recv()

    full = mbuf[...].astype(F32)
    full = jnp.where(first, full[:, :, :ROWS], full[:, :, ROWS:])
    unit = zscore(full.reshape(cz, ROWS, width), 0)
    for p in range(2):
        for s in range(nyx):
            start = s * NZ + p * zh
            part = unit[(p * nyx + s) * zh : (p * nyx + s + 1) * zh]
            nscr[start * ROWS : (start + zh) * ROWS] = part.reshape(zh * ROWS, width)
    for i in range(ROWS):
        unit = nscr[pl.ds(i, cz, stride=ROWS), :].T.astype(BF16)
        proj = jnp.dot(unit, fp_v[...], preferred_element_type=F32)
        out_ref[i] = (upd[i] + gates[i] * proj).astype(BF16)

    for turn in turns:
        if turn:
            arrived(msend.at[pl.ds(0, ny * zh)], msem.at[0, turn])

    @pl.when(stays)
    def _():
        arrived(msend.at[pl.ds(0, ny * zh - 1)], msem.at[0, 0])

    @pl.when(jnp.logical_not(stays))
    def _():
        arrived(msend.at[pl.ds(0, ny * zh)], msem.at[0, 0])

    for copy in finals:
        copy.wait_send()


def shards(msa, pair, wl, wr, wo, *weights):
    ny = lax.axis_size("blk")
    nx = lax.axis_size("dap") // (NZ * NC)
    sd, _, cm = msa.shape
    ch, cz = wl.shape[1], wo.shape[1]
    columns = pair.shape[1]
    jr = ROWS // ny
    width = NZ * NC * ROWS
    thirds = NC * NZ * jr
    step = NZ * jr // 4 * ROWS
    peers = nx * ny * NZ
    vmem = pltpu.VMEM
    dma = pltpu.SemaphoreType.DMA
    scratch = [
        vmem((cm // 128 * sd * ROWS + ROWS, 128), F32),
        vmem((ch * ROWS + ROWS, sd), F32),
        vmem((ny, nx, ch * ROWS, sd), BF16),
        vmem((ny, jr * ch, sd), BF16),
        vmem((NC, ny, NZ, jr * ch, sd), BF16),
        vmem((NC * nx, step, 4 * ch * ch), BF16),
        vmem((4 * ch * ch, 4 * cz), BF16),
        vmem((ROWS, columns, cz), BF16),
        vmem((ROWS * columns + 2 * ROWS, cz), F32),
        vmem((nx * thirds * ROWS + 2 * ROWS, cz), F32),
        vmem((nx, thirds * ROWS, cz), BF16),
        vmem((nx, thirds * ROWS, cz), BF16),
        vmem((nx, thirds * ROWS, cz), BF16),
        vmem((ny, thirds * ROWS, cz), BF16),
        vmem((width * ROWS + ROWS, cz), F32),
        vmem((ROWS, width, cz), F32),
        vmem((4 * cz, cz), BF16),
        vmem((ROWS * width, cz), BF16),
        vmem((ny * NZ * 2 * ROWS + 2 * ROWS, width), F32),
        vmem((cz, 2 * ROWS, width), BF16),
        vmem((peers, 2 * ROWS, width), BF16),
        vmem((peers, 2 * ROWS, width), BF16),
        vmem((nx * NZ * ROWS, ny * width), BF16),
        vmem((nx * width, ny * width), BF16),
        vmem((nx * NZ * ROWS, nx * width), F32),
        vmem((peers // 2, 2 * ROWS, width), BF16),
        vmem((2, peers // 2, 2 * ROWS, width), BF16),
        vmem((cz * ROWS + ROWS, width), F32),
        vmem((ROWS, width, cz), F32),
        vmem((sd * ROWS, cm), BF16),
        vmem((ch, cm), BF16),
        vmem((ch, cm), BF16),
        vmem((ch * ch, cz), BF16),
    ] + [vmem((cz, cz), BF16)] * 6 + [
        dma((10,)),
        dma,
        dma((10,)),
        dma((8,)),
        dma((2,)),
        dma((2,)),
        dma((nx,)),
        dma((ny,)),
        dma((2, nx)),
        dma((2, nx)),
        dma((2, nx)),
        dma((2, nx)),
    ]
    return pl.pallas_call(
        functools.partial(kernel, nx, ny, ny * sd),
        out_shape=pltpu.VMEM((ROWS, width, cz), BF16),
        in_specs=[pl.BlockSpec(memory_space=pltpu.HBM)] * 11,
        out_specs=pl.BlockSpec(memory_space=pltpu.VMEM),
        scratch_shapes=scratch,
        compiler_params=pltpu.CompilerParams(
            collective_id=0, has_side_effects=True, vmem_limit_bytes=48 * 2**20
        ),
    )(*[pltpu.with_memory_space_constraint(v, pltpu.HBM) for v in (msa.reshape(sd * ROWS, cm), pair, wl.T, wr.T, wo, *weights)])


def solution(mesh):
    placed = (P("blk", "dap", None), P("dap", None, None)) + (P(),) * 9
    return jax.shard_map(
        shards, mesh=mesh, in_specs=placed, out_specs=P("dap", "blk", None), check_vma=False
    )
```

```python
import functools

import jax
import jax.numpy as jnp
from jax import lax
from jax.experimental import pallas as pl
from jax.experimental.pallas import tpu as pltpu
from jax.sharding import PartitionSpec as P

NZ = 8
NC = 2
ROWS = 8
EPS = 1e-5
MESH = pl.DeviceIdType.MESH
F32 = jnp.float32
BF16 = jnp.bfloat16


def nt(a, b):
    return lax.dot_general(a, b, (((1,), (1,)), ((), ())), preferred_element_type=F32)


def zscore(v, axis):
    centered = v - jnp.mean(v, axis=axis, keepdims=True)
    var = jnp.mean(centered * centered, axis=axis, keepdims=True)
    return centered * lax.rsqrt(var + EPS)


def device(x, y, z, c):
    return (x * NZ + z) * NC + c, y


def kernel(
    nx, ny, seqs,
    msa_ref, pair_ref, wl_ref, wr_ref, wo_ref, ag_ref, ap_ref, bg_ref, bp_ref, fg_ref, fp_ref,
    out_ref,
    xf, lscr, lbuf, rsend, rbuf, abuf, bd, pairv, pairf, pstage, psend, pbuf, usend, ubuf, vbuf, upd,
    wt4, norm, lrscr, lrsend, lrbuf, lrsib, lwide, rwide, mixed, msend, mbuf, nscr, gates,
    msa_v, wl_v, wr_v, wo_v, ag_v, ap_v, bg_v, bp_v, fg_v, fp_v,
    load_sem, pair_sem, lsem, rsem, csem, psem, usend_sem, urecv_sem, asem, ssem, msem, fsem,
):
    local = (msa_v, wl_v, wr_v, wo_v, ag_v, ap_v, bg_v, bp_v, fg_v, fp_v)
    d = lax.axis_index("dap")
    y = lax.axis_index("blk")
    x, z, c = d // (NZ * NC), (d // NC) % NZ, d % NC
    sd = msa_ref.shape[0] // ROWS
    ch = wl_ref.shape[0]
    cz = wo_ref.shape[1]
    jr = ROWS // ny
    slab = 4
    njo = NZ * jr // slab
    thirds = NC * NZ * jr
    width = NZ * NC * ROWS
    nyx = ny * nx
    zh = NZ // 2
    sibling = device(x, y, z, 1 - c)
    first = c == 0

    def place(x1, y1, z1):
        return (x1 * ny + y1) * NZ + lax.rem(z1, 2) * zh + lax.div(z1, 2)

    xs = [lax.rem(x + k, nx) for k in range(nx)]
    ys = [lax.rem(y + k, ny) for k in range(ny)]
    zs = [lax.rem(z + k, NZ) for k in range(NZ)]
    xat = [v * (NZ * NC) + c for v in xs]
    zat = [v * NC for v in zs]
    xpart = [v * (ny * NZ) for v in xs]
    ypart = [v * NZ for v in ys]
    zpart = [place(0, 0, v) for v in zs]

    def outward(n):
        return sorted(range(n), key=lambda k: -min(k, n - k))

    def remote(source, target, send, recv, to):
        return pltpu.make_async_remote_copy(
            source, target, send, recv, device_id=to, device_id_type=MESH
        )

    def away(k, n):
        return lax.rem(n // 2 + jnp.where(lax.rem(k, 2) == 1, lax.div(k + 1, 2), n - lax.div(k, 2)), n)

    def arrived(part, sem):
        pltpu.make_async_copy(part, part, sem).wait()

    barrier = pltpu.get_barrier_semaphore()

    def greet(x2, y2, z2, c2):
        pl.semaphore_signal(barrier, inc=1, device_id=device(x2, y2, z2, c2), device_id_type=MESH)

    greet(x, y, z, 1 - c)
    for k in range(1, nx):
        greet(lax.rem(x + k, nx), y, z, c)
    for kz in (0, 1, 2, NZ - 2, NZ - 1):
        for ky in range(ny):
            if kz or ky:
                greet(x, ys[ky], zs[kz], c)

    sources = (msa_ref, wl_ref, wr_ref, wo_ref, ag_ref, ap_ref, bg_ref, bp_ref, fg_ref, fp_ref)
    loads = [
        pltpu.make_async_copy(source, target, load_sem.at[t])
        for t, (source, target) in enumerate(zip(sources, local))
    ]
    for load in loads:
        load.start()
    pair_copy = pltpu.make_async_copy(pair_ref, pairv, pair_sem)
    pair_copy.start()
    for load in loads[:3]:
        load.wait()

    lanes = xf.shape[1]
    blocks = msa_v.shape[1] // lanes
    for h in range(blocks):
        xf[h * sd * ROWS : (h + 1) * sd * ROWS] = msa_v[:, h * lanes : (h + 1) * lanes].astype(F32)
    wlr = jnp.concatenate([wl_v[...], wr_v[...]], axis=0)
    for i in range(ROWS):
        v = jnp.concatenate(
            [xf[pl.ds(h * sd * ROWS + i, sd, stride=ROWS), :] for h in range(blocks)], axis=1
        )
        v = zscore(v, 1).astype(BF16)
        proj = nt(wlr, v)
        lscr[pl.ds(i, ch, stride=ROWS), :] = proj[:ch]
        rsend[i // jr, (i % jr) * ch : (i % jr + 1) * ch, :] = proj[ch:].astype(BF16)
    lbuf[y, x] = lscr[: ch * ROWS].astype(BF16)
    rbuf[c, y, z] = rsend[y]

    pl.semaphore_wait(barrier, ny * 5 + nx - 1)

    half = ch * ROWS // 2
    low, high = pl.ds(0, half), pl.ds(half, half)
    xfirst = lbuf.at[y, x, low]
    yfirst = lbuf.at[y, x, high]
    for k in range(1, nx):
        remote(xfirst, xfirst, lsem.at[0], lsem.at[1], device(lax.rem(x + k, nx), y, z, c)).start()
    for k in range(1, ny):
        remote(yfirst, yfirst, lsem.at[2], lsem.at[3], device(x, lax.rem(y + k, ny), z, c)).start()

    for kz, at in ((2, 0), (NZ - 2, 0), (1, 2), (NZ - 1, 2), (0, 6)):
        for ky in range(ny):
            if kz or ky:
                remote(
                    rsend.at[ys[ky]], rbuf.at[c, y, z], rsem.at[at], rsem.at[at + 1],
                    (xat[0] + zat[kz], ys[ky]),
                ).start()

    pair_copy.wait()
    columns = pairv.shape[1]
    pairf[: ROWS * columns] = pairv[...].astype(F32).reshape(ROWS * columns, cz)
    for i in range(ROWS):
        for h in range(NC):
            for r in range(jr):
                v = pairf[pl.ds(i * columns + h * ROWS + y * jr + r, nx * NZ, stride=NC * ROWS), :]
                for g in range(nx):
                    start = (g * thirds + h * NZ * jr + r) * ROWS + i
                    pstage[pl.ds(start, NZ, stride=jr * ROWS), :] = v[g * NZ : (g + 1) * NZ]
    staged = pstage[: nx * thirds * ROWS].astype(BF16)
    psend[...] = staged.reshape(nx, thirds * ROWS, cz)
    pbuf[x] = psend[x]
    for k in range(1, nx):
        x2 = lax.rem(x + k, nx)
        remote(psend.at[x2], pbuf.at[x], psem.at[0], psem.at[1], device(x2, y, z, c)).start()

    arrived(lbuf.at[0, pl.ds(0, nx - 1), low], lsem.at[1])
    ythen = lbuf.at[y, :, low]
    for k in range(1, ny):
        remote(ythen, ythen, lsem.at[4], lsem.at[5], device(x, lax.rem(y + k, ny), z, c)).start()
    arrived(lbuf.at[pl.ds(0, ny - 1), 0, high], lsem.at[3])
    xthen = lbuf.at[:, x, high]
    for k in range(1, nx):
        remote(xthen, xthen, lsem.at[6], lsem.at[7], device(lax.rem(x + k, nx), y, z, c)).start()

    arrived(rbuf.at[0, :, pl.ds(0, 2)], rsem.at[1])
    early, late = pl.ds(0, ny // 2), pl.ds(ny // 2, ny // 2)
    for part, kz in (
        (rbuf.at[c, early, zs[NZ - 2]], 2),
        (rbuf.at[c, late, zs[2]], NZ - 2),
        (rbuf.at[c, :, zs[NZ - 2]], 1),
        (rbuf.at[c, :, zs[2]], NZ - 1),
    ):
        remote(part, part, rsem.at[4], rsem.at[5], (xat[0] + zat[kz], y)).start()

    for load in loads[3:]:
        load.wait()
    bd[...] = jnp.zeros_like(bd)
    for q in range(ch):
        w = wo_v[q * ch : (q + 1) * ch, :]
        for t in range(slab):
            bd[(q * slab + t) * ch : (q * slab + t + 1) * ch, t * cz : (t + 1) * cz] = w
    for t, ref in enumerate((ag_v, ap_v, bg_v, bp_v)):
        wt4[t * cz : (t + 1) * cz, :] = ref[...].astype(F32).T.astype(BF16)

    arrived(rbuf.at[0, :, pl.ds(0, 2)], rsem.at[3])
    arrived(rbuf.at[0, pl.ds(0, ny - 1), 0], rsem.at[7])
    arrived(rbuf.at[0, :, pl.ds(0, NZ - 5)], rsem.at[5])
    cross = remote(rbuf.at[c], rbuf.at[c], csem.at[0], csem.at[1], sibling)
    cross.start()
    arrived(lbuf.at[pl.ds(0, ny - 1), :, low], lsem.at[5])
    arrived(lbuf.at[:, pl.ds(0, nx - 1), high], lsem.at[7])

    def outer(side):
        right = rbuf[side]
        right = jnp.concatenate(
            [right[s].reshape(NZ * jr * ch, sd) for s in range(ny)], axis=1
        )

        def one(g, carry):
            rows = jnp.concatenate([lbuf[s, g] for s in range(ny)], axis=1)
            prod = nt(rows, right)
            for q in range(ch):
                part = prod[q * ROWS : (q + 1) * ROWS]
                abuf[side * nx + g, :, q * slab * ch : (q + 1) * slab * ch] = jnp.concatenate(
                    [part[:, t * slab * ch : (t + 1) * slab * ch] for t in range(njo)], axis=0
                ).astype(BF16)
            return carry

        lax.fori_loop(0, nx, one, 0)

    outer(c)
    cross.wait_recv()
    outer(1 - c)
    step = njo * ROWS
    mixer = abuf[...].reshape(NC * nx * step, slab * ch * ch)
    total = jnp.dot(mixer, bd[...], preferred_element_type=F32)

    arrived(pbuf.at[pl.ds(0, nx - 1)], psem.at[1])
    for g in range(nx):
        tiles = []
        for kk in range(thirds):
            h, flat = divmod(kk, NZ * jr)
            o, t = divmod(flat, slab)
            start = (h * nx + g) * step + o * ROWS
            tiles.append(total[start : start + ROWS, t * cz : (t + 1) * cz])
        u = pbuf[g].astype(F32) + jnp.concatenate(tiles, axis=0) * (1.0 / seqs)
        u = u.astype(BF16)
        usend[g] = u
        vbuf[g * thirds * ROWS : (g + 1) * thirds * ROWS] = u.astype(F32)

    for i in range(ROWS):
        norm[i * width : (i + 1) * width] = zscore(
            vbuf[pl.ds(i, width, stride=ROWS), :], 1
        ).astype(BF16)
    own = place(x, y, z)
    turns = outward(nx)
    some = ny * NZ
    for turn in turns:
        weights = jnp.concatenate(
            [wt4[pl.ds(pl.multiple_of(t * cz + xpart[turn], some), some)] for t in range(4)], axis=0
        )
        four = nt(weights, norm[...])
        lhs = jax.nn.sigmoid(four[:some]) * four[some : 2 * some]
        rhs = jax.nn.sigmoid(four[2 * some : 3 * some]) * four[3 * some :]
        for i in range(ROWS):
            span = slice(i * width, (i + 1) * width)
            lrscr[pl.ds(i, some, stride=2 * ROWS), :] = lhs[:, span]
            lrscr[pl.ds(ROWS + i, some, stride=2 * ROWS), :] = rhs[:, span]
        tiles = lrscr[: some * 2 * ROWS].reshape(some, 2 * ROWS, width)
        lrsend[pl.ds(xpart[turn], some)] = tiles.astype(BF16)
        for ky in outward(ny):
            for kz in outward(NZ):
                if turn or kz or ky:
                    remote(
                        lrsend.at[xpart[turn] + ypart[ky] + zpart[kz]], lrbuf.at[own],
                        asem.at[0, turn], asem.at[1, turn], (xat[turn] + zat[kz], ys[ky]),
                    ).start()
    lrbuf[own] = lrsend[own]

    for g in range(nx):
        here = jnp.logical_and(x == g, y == x)

        @pl.when(here)
        def _():
            ubuf[y] = usend[g]

        @pl.when(jnp.logical_not(here))
        def _():
            remote(
                usend.at[g], ubuf.at[y], usend_sem.at[g], urecv_sem.at[y], device(g, x, z, c)
            ).start()

    group = lax.broadcasted_iota(jnp.int32, (zh * NC * ROWS, width), 1) // thirds
    swaps = []
    for turn in turns:
        base = lax.rem(x + nx - turn, nx) * ny * NZ
        arrived(lrbuf.at[pl.ds(0, ny * NZ - (turn == 0))], asem.at[1, turn])
        part = pl.ds(base, ny * NZ)
        swap = remote(
            lrbuf.at[part], lrsib.at[part], ssem.at[0, turn], ssem.at[1, turn], sibling
        )
        swap.start()
        swap.wait_recv()
        swaps.append(swap)
        for s in range(ny):
            mine = lrbuf[pl.ds(base + s * NZ, NZ)].astype(F32)
            other = lrsib[pl.ds(base + s * NZ, NZ)].astype(F32)
            m0, m1 = jnp.where(first, mine, other), jnp.where(first, other, mine)
            span = slice(s * width, (s + 1) * width)
            rows = []
            for z2 in range(NZ):
                at = z2 % 2 * zh + z2 // 2
                rows += [m0[at, ROWS:], m1[at, ROWS:]]
            right = jnp.concatenate(rows, axis=0)
            for m in range(nx):
                rolled = pltpu.roll(right, m * thirds, 1) if m else right
                rwide[m * width : (m + 1) * width, span] = rolled.astype(BF16)
            rows = []
            for m in (m0, m1):
                rows.append(jnp.where(first, m[:zh, :ROWS], m[zh:, :ROWS]))
            left = jnp.concatenate(rows, axis=1).reshape(zh * NC * ROWS, width)
            for g in range(nx):
                lwide[g * zh * NC * ROWS : (g + 1) * zh * NC * ROWS, span] = jnp.where(
                    group == g, left, 0.0
                ).astype(BF16)
        if turn == turns[0]:
            mixed[...] = nt(lwide[...], rwide[...])
        else:
            mixed[...] += nt(lwide[...], rwide[...])
    for g in range(nx):
        for m in range(nx):
            g2 = (g - m) % nx
            part = mixed[g * zh * NC * ROWS : (g + 1) * zh * NC * ROWS, m * width : (m + 1) * width]
            msend[(g2 * nx + g) * zh : (g2 * nx + g + 1) * zh] = part.reshape(
                zh, NC * ROWS, width
            ).astype(BF16)

    side = lax.rem(z, 2)
    home = (x * ny + y) * zh + lax.div(z, 2)
    stays = side == c

    zhs = [lax.rem(lax.div(z, 2) + k, zh) for k in range(zh)]
    xback = [v * (NZ * NC) + side for v in xs]
    zback = [v * (2 * NC) + c * NC for v in zhs]
    ypart = [v * (nx * zh) for v in ys]
    xpart = [v * zh for v in xs]

    def send_back(turn, kz, ky):
        remote(
            msend.at[ypart[ky] + xpart[turn] + zhs[kz]], mbuf.at[side, home],
            msem.at[0, turn], msem.at[1, turn], (xback[turn] + zback[kz], ys[ky]),
        ).start()

    for turn in turns:
        for kz in outward(zh):
            for ky in outward(ny):
                if turn or kz or ky:
                    send_back(turn, kz, ky)

    @pl.when(stays)
    def _():
        mbuf[side, home] = msend[(y * nx + x) * zh + lax.div(z, 2)]

    @pl.when(jnp.logical_not(stays))
    def _():
        send_back(0, 0, 0)

    for s in range(ny):

        @pl.when(jnp.logical_not(jnp.logical_and(x == y, y == s)))
        def _():
            arrived(ubuf.at[s], urecv_sem.at[s])

        part = ubuf[s].astype(F32)
        for kk in range(thirds):
            h, flat = divmod(kk, NZ * jr)
            j = ((flat // jr) * NC + h) * ROWS + s * jr + flat % jr
            vbuf[j * ROWS : (j + 1) * ROWS, :] = part[kk * ROWS : (kk + 1) * ROWS]
    for i in range(ROWS):
        u = vbuf[pl.ds(i, width, stride=ROWS), :]
        upd[i] = u
        unit = zscore(u, 1).astype(BF16)
        gates[i] = jax.nn.sigmoid(jnp.dot(unit, fg_v[...], preferred_element_type=F32))

    arrived(lbuf.at[0, pl.ds(0, nx - 1), low], lsem.at[0])
    arrived(lbuf.at[pl.ds(0, ny - 1), 0, high], lsem.at[2])
    arrived(lbuf.at[pl.ds(0, ny - 1), :, low], lsem.at[4])
    arrived(lbuf.at[:, pl.ds(0, nx - 1), high], lsem.at[6])
    arrived(rbuf.at[0, :, pl.ds(0, 2)], rsem.at[0])
    arrived(rbuf.at[0, :, pl.ds(0, 2)], rsem.at[2])
    arrived(rbuf.at[0, pl.ds(0, ny - 1), 0], rsem.at[6])
    arrived(rbuf.at[0, :, pl.ds(0, NZ - 5)], rsem.at[4])
    arrived(psend.at[pl.ds(0, nx - 1)], psem.at[0])
    cross.wait_send()
    for g in range(nx):

        @pl.when(jnp.logical_not(jnp.logical_and(x == g, y == x)))
        def _():
            arrived(usend.at[g], usend_sem.at[g])

    for turn in turns:
        arrived(lrbuf.at[pl.ds(0, ny * NZ - (turn == 0))], asem.at[0, turn])
    for copy in swaps:
        copy.wait_send()

    finals = []
    for turn in turns:
        base = lax.rem(x + nx - turn, nx) * ny * zh
        if turn:
            arrived(mbuf.at[c, pl.ds(0, ny * zh)], msem.at[1, turn])
        else:

            @pl.when(stays)
            def _():
                arrived(mbuf.at[c, pl.ds(0, ny * zh - 1)], msem.at[1, 0])

            @pl.when(jnp.logical_not(stays))
            def _():
                arrived(mbuf.at[c, pl.ds(0, ny * zh)], msem.at[1, 0])

        part = mbuf.at[c, pl.ds(base, ny * zh)]
        final = remote(part, part, fsem.at[0, turn], fsem.at[1, turn], sibling)
        final.start()
        finals.append(final)
    for final in finals:
        final.wait_recv()

    full = mbuf[...].astype(F32)
    full = jnp.where(first, full[:, :, :ROWS], full[:, :, ROWS:])
    unit = zscore(full.reshape(cz, ROWS, width), 0)
    for p in range(2):
        for s in range(nyx):
            start = s * NZ + p * zh
            part = unit[(p * nyx + s) * zh : (p * nyx + s + 1) * zh]
            nscr[start * ROWS : (start + zh) * ROWS] = part.reshape(zh * ROWS, width)
    for i in range(ROWS):
        unit = nscr[pl.ds(i, cz, stride=ROWS), :].T.astype(BF16)
        proj = jnp.dot(unit, fp_v[...], preferred_element_type=F32)
        out_ref[i] = (upd[i] + gates[i] * proj).astype(BF16)

    for turn in turns:
        if turn:
            arrived(msend.at[pl.ds(0, ny * zh)], msem.at[0, turn])

    @pl.when(stays)
    def _():
        arrived(msend.at[pl.ds(0, ny * zh - 1)], msem.at[0, 0])

    @pl.when(jnp.logical_not(stays))
    def _():
        arrived(msend.at[pl.ds(0, ny * zh)], msem.at[0, 0])

    for copy in finals:
        copy.wait_send()


def shards(msa, pair, wl, wr, wo, *weights):
    ny = lax.axis_size("blk")
    nx = lax.axis_size("dap") // (NZ * NC)
    sd, _, cm = msa.shape
    ch, cz = wl.shape[1], wo.shape[1]
    columns = pair.shape[1]
    jr = ROWS // ny
    width = NZ * NC * ROWS
    thirds = NC * NZ * jr
    step = NZ * jr // 4 * ROWS
    peers = nx * ny * NZ
    vmem = pltpu.VMEM
    dma = pltpu.SemaphoreType.DMA
    scratch = [
        vmem((cm // 128 * sd * ROWS + ROWS, 128), F32),
        vmem((ch * ROWS + ROWS, sd), F32),
        vmem((ny, nx, ch * ROWS, sd), BF16),
        vmem((ny, jr * ch, sd), BF16),
        vmem((NC, ny, NZ, jr * ch, sd), BF16),
        vmem((NC * nx, step, 4 * ch * ch), BF16),
        vmem((4 * ch * ch, 4 * cz), BF16),
        vmem((ROWS, columns, cz), BF16),
        vmem((ROWS * columns + 2 * ROWS, cz), F32),
        vmem((nx * thirds * ROWS + 2 * ROWS, cz), F32),
        vmem((nx, thirds * ROWS, cz), BF16),
        vmem((nx, thirds * ROWS, cz), BF16),
        vmem((nx, thirds * ROWS, cz), BF16),
        vmem((ny, thirds * ROWS, cz), BF16),
        vmem((width * ROWS + ROWS, cz), F32),
        vmem((ROWS, width, cz), F32),
        vmem((4 * cz, cz), BF16),
        vmem((ROWS * width, cz), BF16),
        vmem((ny * NZ * 2 * ROWS + 2 * ROWS, width), F32),
        vmem((cz, 2 * ROWS, width), BF16),
        vmem((peers, 2 * ROWS, width), BF16),
        vmem((peers, 2 * ROWS, width), BF16),
        vmem((nx * NZ * ROWS, ny * width), BF16),
        vmem((nx * width, ny * width), BF16),
        vmem((nx * NZ * ROWS, nx * width), F32),
        vmem((peers // 2, 2 * ROWS, width), BF16),
        vmem((2, peers // 2, 2 * ROWS, width), BF16),
        vmem((cz * ROWS + ROWS, width), F32),
        vmem((ROWS, width, cz), F32),
        vmem((sd * ROWS, cm), BF16),
        vmem((ch, cm), BF16),
        vmem((ch, cm), BF16),
        vmem((ch * ch, cz), BF16),
    ] + [vmem((cz, cz), BF16)] * 6 + [
        dma((10,)),
        dma,
        dma((10,)),
        dma((8,)),
        dma((2,)),
        dma((2,)),
        dma((nx,)),
        dma((ny,)),
        dma((2, nx)),
        dma((2, nx)),
        dma((2, nx)),
        dma((2, nx)),
    ]
    return pl.pallas_call(
        functools.partial(kernel, nx, ny, ny * sd),
        out_shape=pltpu.VMEM((ROWS, width, cz), BF16),
        in_specs=[pl.BlockSpec(memory_space=pltpu.HBM)] * 11,
        out_specs=pl.BlockSpec(memory_space=pltpu.VMEM),
        scratch_shapes=scratch,
        compiler_params=pltpu.CompilerParams(
            collective_id=0, has_side_effects=True, vmem_limit_bytes=48 * 2**20
        ),
    )(*[pltpu.with_memory_space_constraint(v, pltpu.HBM) for v in (msa.reshape(sd * ROWS, cm), pair, wl.T, wr.T, wo, *weights)])


def solution(mesh):
    placed = (P("blk", "dap", None), P("dap", None, None)) + (P(),) * 9
    return jax.shard_map(
        shards, mesh=mesh, in_specs=placed, out_specs=P("dap", "blk", None), check_vma=False
    )
```
